128 devices in a mesh: slab: 16 (over y_hi, z, core), split: 8 (over y_lo, x).
Axes of the slice: x: 4, y: 4 (y_hi: 2, y_lo: 2; y = y_hi * 2 + y_lo), z: 4, core: 2. Of those that a mesh axis runs over, the one named last changes fastest.
Arguments:
- displacement: float32 [3, 128, 256, 256], P(None, 'slab', 'split'), may hold values from -0.3 to 0.3
- velocity: float32 [3, 128, 256, 256], P(None, 'slab', 'split'), may hold values from -0.6 to 0.6
- acceleration: float32 [3, 128, 256, 256], P(None, 'slab', 'split'), may hold values from -1.8 to 1.8
- bond_masks: int32 [4, 128, 256, 256], P(None, 'slab', 'split'), may hold values from 0 to 255, as said below
- proj_pos: float32 [128, 3, 128], replicated, may hold values from -0.5 to 257, as said below
- proj_vel: float32 [128, 3, 128], replicated, may hold values from -1.8 to 1.8
- proj_acc: float32 [128, 3, 128], replicated, may hold values from -1.8 to 1.8
- contact_pairs: int32 [3, 2, 2048], P(None, None, ('slab', 'split')), may hold values from -1 to 127, as said below
Outputs:
- final_displacement: float32 [3, 128, 256, 256], P(None, 'slab', 'split')
- final_velocity: float32 [3, 128, 256, 256], P(None, 'slab', 'split')
- final_proj_pos: float32 [128, 3, 128], replicated
- final_proj_vel: float32 [128, 3, 128], replicated
The draws below stay inside these ranges and needn't reach their ends.
Inputs may be any that keep to these rules, and one draw needn't show every extreme that they name: `bond_masks`: bit b of word w (the value divided by 2 to the b, modulo 2) is 1 where the bond from the cell to the offset numbered 8 w + b is intact. `contact_pairs`: slots d * 16 to (d + 1) * 16 - 1 belong to device d. Row 0 names one of that device's 8 surface blocks; row 1 names a projectile block, or -1 for an empty slot. Live slots come first on every device and no pair repeats on a device within a substep. In every substep each projectile block is paired on exactly one device, one of the four devices of the 2 x 2 group of device blocks under it, and on another device than in the substep before; in every substep some device has all 16 slots live. `proj_pos`: the device blocks fall into 2 x 2 groups (slab indices 2a and 2a + 1, split indices 2b and 2b + 1). Every projectile block lies above one such group, between 0.5 and 2 cells over the top layer, and every group lies under exactly 4 projectile blocks.
All inputs are finite; a program needn't handle non-finite values.
Results may differ from the reference program's by a relative error of at most 0.0003.
Values sent between devices are 32-bit elements; how exact they have to be, the bound alone decides.
No kernel may reach another device: no remote copies, remote signals or barrier semaphores. Data moves between devices by JAX's collectives and lax.ppermute only.
A program may use at most 128 MiB of HBM per device.

```python
import math
import jax
import jax.numpy as jnp
from jax import lax

CX = 8
CY = 32
NZ = 256
SUB = 3
SL = 4
PTS = 128
MAXH = 4
NX = 128
NY = 256
SB_DEV = 8
TPB = 4
MAXP = 16
PB = 128
N_SPLIT = 8


def quad_owners(key):
    base_key = jax.random.fold_in(key, 7)
    keys = jax.random.split(base_key, 6)
    slab_count = NX // CX
    split_count = NY // CY
    devices = slab_count * split_count
    quad_count = devices // 4
    half_split = split_count // 2
    per_quad = PB // quad_count
    quad_of = jax.random.permutation(keys[0], (jnp.arange(PB) // per_quad).astype(jnp.int32)).astype(jnp.int32)
    center = jax.random.randint(keys[1], (), 0, quad_count)
    in_center = quad_of == center
    own_start = jax.random.randint(keys[2], (PB,), 0, 4)
    own_steps = jax.random.randint(keys[3], (SUB, PB), 1, 4)
    common_start = jax.random.randint(keys[4], (), 0, 4)
    common_steps = jax.random.randint(keys[5], (SUB, 1), 1, 4)
    corner = jnp.where(in_center, common_start, own_start).astype(jnp.int32)
    step_sizes = jnp.where(in_center[None, :], common_steps, own_steps).astype(jnp.int32)
    owner_rows = []
    for substep in range(SUB):
        if substep > 0:
            corner = (corner + step_sizes[substep]) % 4
        row_index = 2 * (quad_of // half_split) + corner // 2
        column_index = 2 * (quad_of % half_split) + corner % 2
        owner_rows.append((row_index * split_count + column_index).astype(jnp.int32))
    return (quad_of, jnp.stack(owner_rows))


def draw_bond_masks(key, part):
    mask_key = jax.random.fold_in(key, 41)
    packed = jnp.zeros((4, NX, NY, NZ), jnp.int32)
    for bit_index in range(8):
        digits = jax.random.randint(jax.random.fold_in(mask_key, bit_index), (4, NX, NY, NZ), 0, 5)
        packed = packed + (digits < 4).astype(jnp.int32) * 2 ** bit_index
    return packed


def draw_contact_pairs(key, part):
    quad_of, owners = quad_owners(key)
    devices = NX // CX * (NY // CY)
    indices = jnp.arange(PB).astype(jnp.int32)
    earlier = (owners[:, None, :] == owners[:, :, None]) & (indices[None, None, :] < indices[None, :, None])
    owner_rank = jnp.sum(earlier.astype(jnp.int32), axis=2)
    step_index = jnp.broadcast_to(jnp.arange(SUB).astype(jnp.int32)[:, None], (SUB, PB))
    block_index = jnp.broadcast_to(indices[None, :], (SUB, PB))
    home_table = jnp.full((SUB, devices, MAXH), -1, jnp.int32).at[step_index, owners, owner_rank].set(block_index)
    slot_keys = jax.random.split(jax.random.fold_in(key, 13), SUB * devices * MAXH)
    target_picks = jax.vmap(lambda slot_key: jax.random.permutation(slot_key, SB_DEV)[:TPB])(slot_keys)
    targets = target_picks.reshape(SUB, devices * MAXH * TPB).astype(jnp.int32)
    chosen = jnp.broadcast_to(home_table[:, :, :, None], (SUB, devices, MAXH, TPB)).reshape(SUB, devices * MAXH * TPB)
    return jnp.stack([targets, chosen.astype(jnp.int32)], axis=1)


def draw_proj_pos(key, part):
    quad_of, owners = quad_owners(key)
    half_split = NY // CY // 2
    base_x = (quad_of // half_split * 2 * CX).astype(jnp.float32)
    base_y = (quad_of % half_split * 2 * CY).astype(jnp.float32)
    float_keys = jax.random.split(jax.random.fold_in(key, 29), 3)
    along_x = base_x[:, None] + jax.random.uniform(float_keys[0], (PB, PTS), jnp.float32, -0.5, 2 * CX - 0.5)
    along_y = base_y[:, None] + jax.random.uniform(float_keys[1], (PB, PTS), jnp.float32, -0.5, 2 * CY - 0.5)
    height = NZ - 1 + jax.random.uniform(float_keys[2], (PB, PTS), jnp.float32, 0.5, 2.0)
    return jnp.stack([along_x, along_y, height], axis=1)


def level_of(stream_key, shape, cuts, smallest, high):
    def one(dim, blocks):
        draws = jax.random.uniform(jax.random.fold_in(jax.random.fold_in(stream_key, 6), dim), (blocks,), jnp.float32, smallest / len(cuts), high / len(cuts))
        return jnp.repeat(jnp.exp(draws), shape[dim] // blocks).reshape((-1,) + (1,) * (len(shape) - dim - 1))

    factor_of = one(*cuts[0])
    for cut in cuts[1:]:
        factor_of = factor_of * one(*cut)
    return factor_of


def normal_values(stream_key, dims, width, bound, cuts=(), kind=jnp.bfloat16):
    level = level_of(stream_key, dims, cuts, -0.22, 0.18) if cuts else 1.0
    entries = jax.random.normal(stream_key, dims, jnp.float32) * width * level
    return jnp.minimum(jnp.maximum(entries, -bound), bound).astype(kind)


def setup_inputs(seed: int = 0) -> dict:
    arg_keys = jax.random.split(jax.random.key(seed), 9)
    return {
        "displacement": normal_values(arg_keys[0], (3, NX, NY, NZ), 0.05, 0.3, ((1, 16), (2, 8)), jnp.float32),
        "velocity": normal_values(arg_keys[1], (3, NX, NY, NZ), 0.1, 0.6, ((1, 16), (2, 8)), jnp.float32),
        "acceleration": normal_values(arg_keys[2], (3, NX, NY, NZ), 0.3, 1.8, ((1, 16), (2, 8)), jnp.float32),
        "bond_masks": draw_bond_masks(jax.random.fold_in(arg_keys[8], 71), 0),
        "proj_pos": draw_proj_pos(jax.random.fold_in(arg_keys[8], 71), 0),
        "proj_vel": normal_values(arg_keys[5], (PB, 3, PTS), 0.3, 1.8, (), jnp.float32),
        "proj_acc": normal_values(arg_keys[6], (PB, 3, PTS), 0.3, 1.8, (), jnp.float32),
        "contact_pairs": draw_contact_pairs(jax.random.fold_in(arg_keys[8], 71), 0),
    }


time_step = 0.25
bond_stiffness = 0.5
contact_stiffness = 0.05
contact_width = 8.0
inverse_mass = 0.5

def bond_offsets():
    listed = []
    for shift_x in (-2, -1, 0, 1, 2):
        for shift_y in (-2, -1, 0, 1, 2):
            for shift_z in (-2, -1, 0, 1, 2):
                squared = shift_x * shift_x + shift_y * shift_y + shift_z * shift_z
                if 0 < squared <= 4:
                    listed.append((shift_x, shift_y, shift_z))
    return listed

def bond_term(neighbour, displace, intact, valid_bond, offset):
    shift_x, shift_y, shift_z = offset
    length = math.sqrt(shift_x * shift_x + shift_y * shift_y + shift_z * shift_z)
    along_x = shift_x + (neighbour[0] - displace[0])
    along_y = shift_y + (neighbour[1] - displace[1])
    along_z = shift_z + (neighbour[2] - displace[2])
    squared = along_x * along_x + along_y * along_y + along_z * along_z
    stretch = (squared - length * length) / (length * (jnp.sqrt(squared) + length))
    return bond_stiffness / length * stretch * intact * valid_bond

def add_bond(bond_total, coefficient, offset):
    direction = jnp.array(offset, bond_total.dtype)
    return bond_total + direction[:, None, None, None] * coefficient[None]

def bond_forces(displace, mask_words):
    padded = jnp.pad(displace, ((0, 0), (2, 2), (2, 2), (2, 2)))
    inside_x = jnp.pad(jnp.ones((NX,), displace.dtype), 2)
    inside_y = jnp.pad(jnp.ones((NY,), displace.dtype), 2)
    inside_z = jnp.pad(jnp.ones((NZ,), displace.dtype), 2)
    bond_total = jnp.zeros_like(displace)
    for number, offset in enumerate(bond_offsets()):
        shift_x, shift_y, shift_z = offset
        neighbour = padded[:, 2 + shift_x:2 + shift_x + NX, 2 + shift_y:2 + shift_y + NY, 2 + shift_z:2 + shift_z + NZ]
        valid_bond = inside_x[2 + shift_x:2 + shift_x + NX][:, None, None] * inside_y[2 + shift_y:2 + shift_y + NY][None, :, None] * inside_z[2 + shift_z:2 + shift_z + NZ][None, None, :]
        intact = (mask_words[number // 8] // 2 ** (number % 8) % 2).astype(displace.dtype)
        bond_total = add_bond(bond_total, bond_term(neighbour, displace, intact, valid_bond, offset), offset)
    return bond_total

def contact_tile(points, particles):
    separation = points[:, :, None] - particles[:, None, :]
    squared = lax.optimization_barrier(jnp.sum(separation * separation, axis=0))
    weight = contact_stiffness * jnp.exp(-squared / contact_width)
    pulled = weight[None] * separation
    return (lax.optimization_barrier(jnp.sum(pulled, axis=2)), -lax.optimization_barrier(jnp.sum(pulled, axis=1)))

def contact_forces(displace, positions, slot_pairs):
    anchor = jnp.zeros((), jnp.int32)
    lattice = jnp.stack([jnp.broadcast_to(jnp.arange(NX).astype(displace.dtype)[:, None, None], (NX, NY, SL)), jnp.broadcast_to(jnp.arange(NY).astype(displace.dtype)[None, :, None], (NX, NY, SL)), jnp.broadcast_to((NZ - SL + jnp.arange(SL)).astype(displace.dtype)[None, None, :], (NX, NY, SL))])
    places = displace[:, :, :, NZ - SL:] + lattice

    def visit(running, slot_index):
        surface_force, particle_force = running
        device = slot_index // MAXP
        corner_x = (device // N_SPLIT * CX).astype(jnp.int32)
        corner_y = (device % N_SPLIT * CY).astype(jnp.int32)
        starts = (anchor, corner_x, corner_y, anchor)
        region = lax.dynamic_slice(places, starts, (3, CX, CY, SL)).reshape(3, SB_DEV, PTS)
        surface_block = slot_pairs[0, slot_index]
        chosen = slot_pairs[1, slot_index]
        is_live = (chosen >= 0).astype(places.dtype)
        picked = jnp.maximum(chosen, 0)
        on_points, on_particles = contact_tile(region[:, surface_block], positions[picked])
        patch_force = jnp.zeros((3, SB_DEV, PTS), places.dtype).at[:, surface_block].set(on_points * is_live)
        current = lax.dynamic_slice(surface_force, starts, (3, CX, CY, SL))
        surface_force = lax.dynamic_update_slice(surface_force, current + patch_force.reshape(3, CX, CY, SL), starts)
        particle_force = particle_force.at[picked].add(on_particles * is_live)
        return ((surface_force, particle_force), None)
    initial = (jnp.zeros_like(places), jnp.zeros_like(positions))
    finals, ignored = lax.scan(visit, initial, jnp.arange(slot_pairs.shape[1]).astype(jnp.int32))
    return finals

def reference(displacement, velocity, acceleration, bond_masks, proj_pos, proj_vel, proj_acc, contact_pairs):
    for substep in range(SUB):
        half_velocity = velocity + 0.5 * time_step * acceleration
        displacement = displacement + time_step * half_velocity
        proj_half = proj_vel + 0.5 * time_step * proj_acc
        proj_pos = proj_pos + time_step * proj_half
        forces = bond_forces(displacement, bond_masks)
        surface_force, particle_force = contact_forces(displacement, proj_pos, contact_pairs[substep])
        forces = forces + jnp.pad(surface_force, ((0, 0), (0, 0), (0, 0), (NZ - SL, 0)))
        acceleration = forces
        velocity = half_velocity + 0.5 * time_step * acceleration
        proj_acc = inverse_mass * particle_force
        proj_vel = proj_half + 0.5 * time_step * proj_acc
    return (displacement, velocity, proj_pos, proj_vel)
```

```python
import functools
import math

import jax
import jax.numpy as jnp
from jax import lax
from jax.experimental import pallas as pl
from jax.experimental.pallas import tpu as pltpu
from jax.sharding import PartitionSpec as P

SUB = 3
SL = 4
SLOTS = 16
GROUP = 4

DT = 0.25
STIFF = 0.5
CONTACT = 0.05
WIDTH = 8.0
INV_MASS = 0.5

CX, CY, CZ = 8, 32, 256
LO = 8
F32 = jnp.float32
PARAMS = pltpu.CompilerParams(vmem_limit_bytes=48 * 1024 * 1024)


def bond_offsets():
    listed = []
    for sx in (-2, -1, 0, 1, 2):
        for sy in (-2, -1, 0, 1, 2):
            for sz in (-2, -1, 0, 1, 2):
                if 0 < sx * sx + sy * sy + sz * sz <= 4:
                    listed.append((sx, sy, sz))
    return listed


OFFSETS = bond_offsets()


def as_int32(bits):
    return bits - (1 << 32) if bits >= 1 << 31 else bits


def keep_bits(dim, allowed):
    return as_int32(sum(1 << n for n, e in enumerate(OFFSETS) if allowed(e[dim])))


def keep_word(index, last, dim):
    word = jnp.where(index == 0, keep_bits(dim, lambda e: e >= 0), -1)
    word = jnp.where(index == 1, keep_bits(dim, lambda e: e >= -1), word)
    word = jnp.where(index == last - 1, keep_bits(dim, lambda e: e <= 1), word)
    return jnp.where(index == last, keep_bits(dim, lambda e: e <= 0), word)


def position():
    return lax.axis_index("slab"), lax.axis_index("split")


def contact(substep, pairs, u_ref, half_ref, share, pos, ids, corner):
    row = lax.broadcasted_iota(jnp.int32, (CY, 128), 0)
    lane = lax.broadcasted_iota(jnp.int32, (CY, 128), 1)
    place_y = (row + corner[1]).astype(F32)
    live = jnp.int32(0)
    for k in range(SLOTS):
        live += (pairs[substep, 1, k] >= 0).astype(jnp.int32)

    def slot(k, totals):
        target = pairs[substep, 0, k]
        hit = ids == pairs[substep, 1, k]
        q = [jnp.sum(jnp.where(hit, pos[c], 0.0), axis=0, keepdims=True) for c in range(3)]
        tops = [u_ref[c, target, :, CZ - 128 :] for c in range(3)]
        place_x = (corner[0] + target).astype(F32)
        on_particles = [jnp.zeros((CY, 128), F32) for _ in range(3)]
        surface = [jnp.zeros((CY, 128), F32) for _ in range(3)]
        for z in range(SL):
            at = 128 - SL + z
            lattice = (place_x, place_y, float(CZ - SL + z))
            r = [(tops[c][:, at : at + 1] + lattice[c]) - q[c] for c in range(3)]
            squared = r[0] * r[0] + r[1] * r[1] + r[2] * r[2]
            weight = CONTACT * jnp.exp(squared * (-1.0 / WIDTH))
            for c in range(3):
                pulled = weight * r[c]
                on_particles[c] = on_particles[c] + pulled
                on_points = jnp.sum(pulled, axis=1, keepdims=True)
                surface[c] = jnp.where(lane == at, on_points, surface[c])
        for c in range(3):
            half_ref[c, target, :, CZ - 128 :] += share * surface[c]
        return tuple(
            totals[c] - jnp.where(hit, jnp.sum(on_particles[c], axis=0, keepdims=True), 0.0)
            for c in range(3)
        )

    return lax.fori_loop(0, live, slot, tuple(jnp.zeros((8, 128), F32) for _ in range(3)))


def send_edges(u_ref, force, xa, xb, ya, yb, even_x, even_y):
    at_a = jnp.where(even_x, CX - 2, 0)
    at_b = jnp.where(even_x, 0, CX - 2)
    for c in range(3):
        for layer in range(2):
            rows = slice((2 * c + layer) * CY, (2 * c + layer + 1) * CY)
            xa[rows, :] = u_ref[c, at_a + layer]
            xb[rows, :] = u_ref[c, at_b + layer]
        xa[6 * CY + 8 * c : 6 * CY + 8 * c + 8, 0:128] = force[c]
        xa[6 * CY + 8 * c : 6 * CY + 8 * c + 8, 128:256] = force[c]
    for want_even, low, high in ((True, yb, ya), (False, ya, yb)):

        @pl.when(even_y == want_even)
        def _(low=low, high=high):
            for c in range(3):
                for x in range(CX):
                    low[c, x] = u_ref[c, x, 0:2, :]
                    high[c, x] = u_ref[c, x, CY - 2 : CY, :]


def begin_kernel(pairs, u, v, a, masks, pp, pv, pa, u_out, half_out, w_out, pst, perm, xa, xb, ya, yb):
    slab, split = position()
    slabs, splits = lax.axis_size("slab"), lax.axis_size("split")
    even_x, even_y = lax.rem(slab, 2) == 0, lax.rem(split, 2) == 0

    def layer(x, carry):
        kx = keep_word(slab * CX + x, slabs * CX - 1, 0)
        ky = keep_word(split * CY + lax.broadcasted_iota(jnp.int32, (CY, CZ), 0), splits * CY - 1, 1)
        kz = keep_word(lax.broadcasted_iota(jnp.int32, (CY, CZ), 1), CZ - 1, 2)
        word = masks[0, x] | (masks[1, x] << 8) | (masks[2, x] << 16) | (masks[3, x] << 24)
        w_out[x] = word & ky & kz & kx
        for c in range(3):
            half = v[c, x] + 0.5 * DT * a[c, x]
            half_out[c, x] = half
            u_out[c, x] = u[c, x] + DT * half
        return carry

    lax.fori_loop(0, CX, layer, 0)

    blocks = pp.shape[1]
    mean_x = jnp.sum(pp[0], axis=1, keepdims=True) * (1.0 / pp.shape[2])
    mean_y = jnp.sum(pp[1], axis=1, keepdims=True) * (1.0 / pp.shape[2])
    group_x = jnp.floor((mean_x + 0.5) * (1.0 / (2 * CX)))
    group_y = jnp.floor((mean_y + 0.5) * (1.0 / (2 * CY)))
    group = jnp.broadcast_to(group_x * (splits // 2) + group_y, (blocks, blocks))
    row = lax.broadcasted_iota(jnp.int32, (blocks, blocks), 0)
    lane = lax.broadcasted_iota(jnp.int32, (blocks, blocks), 1)
    earlier = jnp.where((group == group.T) & (lane < row), 1.0, 0.0)
    rank = jnp.sum(earlier, axis=1, keepdims=True).astype(jnp.int32)
    group = group.astype(jnp.int32)
    mine = (slab // 2) * (splits // 2) + split // 2
    slot = (group ^ mine) * GROUP + rank
    perm[...] = jnp.where(slot == lane, 1.0, 0.0)

    pst[...] = jnp.zeros_like(pst)
    pst[6] = jnp.full((8, 128), -5.0, F32)
    for k in range(GROUP):
        chosen = slot == k
        pst[6, k : k + 1, :] = jnp.sum(jnp.where(chosen, row.astype(F32), 0.0), axis=0, keepdims=True)
        for c in range(3):
            pos, vel, acc = [
                jnp.sum(jnp.where(chosen, p[c], 0.0), axis=0, keepdims=True) for p in (pp, pv, pa)
            ]
            half = vel + 0.5 * DT * acc
            pst[3 + c, k : k + 1, :] = half
            pst[c, k : k + 1, :] = pos + DT * half
    ids = pst[6].astype(jnp.int32)
    force = contact(
        0, pairs, u_out, half_out, DT, [pst[c] for c in range(3)], ids, (slab * CX, split * CY)
    )
    for c in range(3):
        pst[7 + c] = force[c]
    send_edges(u_out, force, xa, xb, ya, yb, even_x, even_y)


def corner_kernel(ya_own, yb_own, xa, xb, pst, ya, yb):
    slab, split = position()
    even_x, even_y = lax.rem(slab, 2) == 0, lax.rem(split, 2) == 0
    for c in range(3):
        ya[c, 1 : CX + 1] = ya_own[c]
        yb[c, 1 : CX + 1] = yb_own[c]
        force = pst[7 + c] + xa[6 * CY + 8 * c : 6 * CY + 8 * c + 8, 0:128]
        for k in range(2):
            ya[c, CX + 2 + k, :, 0:128] = force[2 * k : 2 * k + 2]
            ya[c, CX + 2 + k, :, 128:256] = force[2 * k : 2 * k + 2]
    for is_x in (True, False):
        for is_y in (True, False):

            @pl.when((even_x == is_x) & (even_y == is_y))
            def _(is_x=is_x, is_y=is_y):
                for c in range(3):
                    for message, high in ((ya, is_y), (yb, not is_y)):
                        y = CY - 2 if high else 0
                        for got, top in ((xa, is_x), (xb, not is_x)):
                            entry, layer = (CX + 1, 0) if top else (0, 1)
                            at = (2 * c + layer) * CY + y
                            message[c, entry] = got[at : at + 2, :]


def bonds_kernel(substep, *refs):
    last = substep == SUB - 1
    pairs, u, half, w, xa, xb, ya, yb, pst = refs[:9]
    if last:
        u_out, half_out, pst_out = u, refs[9], refs[10]
        pad, left, right = refs[11:]
    else:
        u_out, half_out, pst_out, xa_out, xb_out, ya_out, yb_out = refs[9:16]
        pad, left, right = refs[16:]
    slab, split = position()
    even_x, even_y = lax.rem(slab, 2) == 0, lax.rem(split, 2) == 0
    rows = slice(LO, LO + CY)

    def fill(c, _):
        def own(x, carry):
            pad[c, x + 2, rows, :] = u[c, x]
            return carry

        lax.fori_loop(0, CX, own, 0)
        return _

    for c in range(3):
        fill(c, 0)
        to_a = jnp.where(even_x, CX + 2, 0)
        to_b = jnp.where(even_x, 0, CX + 2)
        for layer in range(2):
            part = slice((2 * c + layer) * CY, (2 * c + layer + 1) * CY)
            pad[c, to_a + layer, rows, :] = xa[part, :]
            pad[c, to_b + layer, rows, :] = xb[part, :]
    for is_y in (True, False):

        @pl.when(even_y == is_y)
        def _(is_y=is_y):
            for got, high in ((ya, is_y), (yb, not is_y)):
                at = LO + CY if high else LO - 2
                for c in range(3):
                    for entry in range(CX + 2):
                        pad[c, entry + 1, at : at + 2, :] = got[c, entry]

    def shifted(x, carry):
        for c in range(3):
            for y in range(0, CY + 16, 8):
                value = pad[c, x + 1, y : y + 8, :]
                left[c, x, y : y + 8, :] = pltpu.roll(value, CZ - 1, 1)
                right[c, x, y : y + 8, :] = pltpu.roll(value, 1, 1)
        return carry

    lax.fori_loop(0, CX + 2, shifted, 0)

    def forces(x, y, z):
        lanes = slice(z, z + 128)
        own = [pad[c, x + 2, LO + y : LO + y + 8, lanes] for c in range(3)]
        less = {(c, e): own[c] - float(e) if e else own[c] for c in range(3) for e in (-2, -1, 0, 1, 2)}
        word = w[x, y : y + 8, lanes]
        wide = [pad[c, x + 2, LO + y : LO + y + 8, :] for c in range(3)]
        total = [None] * 3
        for squared_length in (1, 2, 3, 4):
            sums = [None] * 3
            for number, e in enumerate(OFFSETS):
                if sum(k * k for k in e) != squared_length:
                    continue
                at = slice(LO + y + e[1], LO + y + e[1] + 8)
                if e[2] == 0:
                    near = [pad[c, x + 2 + e[0], at, lanes] for c in range(3)]
                elif abs(e[2]) == 2:
                    near = [pltpu.roll(wide[c], (CZ - e[2]) % CZ, 1)[:, lanes] for c in range(3)]
                else:
                    source = left if e[2] > 0 else right
                    near = [source[c, x + 1 + e[0], at, lanes] for c in range(3)]
                d = [near[c] - less[c, e[c]] for c in range(3)]
                q = jnp.maximum(d[0] * d[0] + d[1] * d[1] + d[2] * d[2], 1e-30)
                pull = q * lax.rsqrt(q) - math.sqrt(squared_length)
                pull = jnp.where((word & as_int32(1 << number)) != 0, pull, 0.0)
                for c in range(3):
                    if e[c] > 0:
                        sums[c] = pull if sums[c] is None else sums[c] + pull
                    elif e[c] < 0:
                        sums[c] = -pull if sums[c] is None else sums[c] - pull
            factor = STIFF / squared_length * (2.0 if squared_length == 4 else 1.0)
            for c in range(3):
                term = factor * sums[c]
                total[c] = term if total[c] is None else total[c] + term
        return total

    def layer(x, carry):
        for y in range(0, CY, 8):
            for z in range(0, CZ, 128):
                lanes = slice(z, z + 128)
                total = forces(x, y, z)
                for c in range(3):
                    moved = half[c, x, y : y + 8, lanes] + (0.5 * DT if last else DT) * total[c]
                    half_out[c, x, y : y + 8, lanes] = moved
                    if not last:
                        u_out[c, x, y : y + 8, lanes] = u[c, x, y : y + 8, lanes] + DT * moved
        return carry

    lax.fori_loop(0, CX, layer, 0)

    pst_out[6:] = pst[6:]
    pos = []
    for c in range(3):
        theirs = jnp.concatenate(
            [ya[c, CX + 2, :, 0:128], ya[c, CX + 3, :, 0:128], jnp.zeros((4, 128), F32)], axis=0
        )
        acc = INV_MASS * (pst[7 + c] + xa[6 * CY + 8 * c : 6 * CY + 8 * c + 8, 0:128] + theirs)
        if last:
            pst_out[c] = pst[c]
            pst_out[3 + c] = pst[3 + c] + 0.5 * DT * acc
        else:
            moved = pst[3 + c] + DT * acc
            pst_out[3 + c] = moved
            pos.append(pst[c] + DT * moved)
            pst_out[c] = pos[c]
    if last:
        return
    share = 0.5 * DT if substep == SUB - 2 else DT
    ids = pst[6].astype(jnp.int32)
    force = contact(
        substep + 1, pairs, u_out, half_out, share, pos, ids, (slab * CX, split * CY)
    )
    for c in range(3):
        pst_out[7 + c] = force[c]
    send_edges(u_out, force, xa_out, xb_out, ya_out, yb_out, even_x, even_y)


def final_kernel(perm, gathered, pos_out, vel_out):
    for c in range(3):
        for at, out in ((c, pos_out), (3 + c, vel_out)):
            out[c] = jnp.dot(
                perm[...],
                gathered[at],
                precision=lax.Precision.HIGHEST,
                preferred_element_type=F32,
            )


VMEM = pl.BlockSpec(memory_space=pltpu.VMEM)
SMEM = pl.BlockSpec(memory_space=pltpu.SMEM)
STATE = jax.ShapeDtypeStruct((3, CX, CY, CZ), F32)
WORDS = jax.ShapeDtypeStruct((CX, CY, CZ), jnp.int32)
PST = jax.ShapeDtypeStruct((10, 8, 128), F32)
XA = jax.ShapeDtypeStruct((6 * CY + 24, CZ), F32)
XB = jax.ShapeDtypeStruct((6 * CY, CZ), F32)
YE = jax.ShapeDtypeStruct((3, CX, 2, CZ), F32)
YA = jax.ShapeDtypeStruct((3, CX + 4, 2, CZ), F32)
YB = jax.ShapeDtypeStruct((3, CX + 2, 2, CZ), F32)


def call(kernel, inputs, outputs, scalars=0, scratch=()):
    return pl.pallas_call(
        kernel,
        out_shape=outputs,
        in_specs=[SMEM] * scalars + [VMEM] * (len(inputs) - scalars),
        out_specs=[VMEM] * len(outputs),
        scratch_shapes=list(scratch),
        compiler_params=PARAMS,
    )(*inputs)


def swap(value, axis, offset):
    pairs = []
    for i in range(offset, lax.axis_size(axis) - 1, 2):
        pairs += [(i, i + 1), (i + 1, i)]
    return lax.ppermute(value, axis, pairs)


def exchange(xa, xb, ya, yb, pst):
    xa, xb = swap(xa, "slab", 0), swap(xb, "slab", 1)
    ya, yb = call(corner_kernel, (ya, yb, xa, xb, pst), [YA, YB])
    return xa, xb, swap(ya, "split", 0), swap(yb, "split", 1)


def per_device(u, v, a, masks, proj_pos, proj_vel, proj_acc, pairs):
    pp, pv, pa = [jnp.transpose(p, (1, 0, 2)) for p in (proj_pos, proj_vel, proj_acc)]
    blocks = pp.shape[1]
    u, half, words, pst, perm, *edges = call(
        begin_kernel,
        (pairs, u, v, a, masks, pp, pv, pa),
        [STATE, STATE, WORDS, PST, jax.ShapeDtypeStruct((blocks, blocks), F32), XA, XB, YE, YE],
        scalars=1,
    )
    pad = pltpu.VMEM((3, CX + 4, CY + 16, CZ), F32)
    side = pltpu.VMEM((3, CX + 2, CY + 16, CZ), F32)
    for substep in range(SUB):
        halos = exchange(*edges, pst)
        last = substep == SUB - 1
        outputs = [STATE, PST] if last else [STATE, STATE, PST, XA, XB, YE, YE]
        got = call(
            functools.partial(bonds_kernel, substep),
            (pairs, u, half, words, *halos, pst),
            outputs,
            scalars=1,
            scratch=(pad, side, side),
        )
        if last:
            velocity, pst = got
        else:
            u, half, pst, *edges = got

    gathered = pst[:6, :GROUP]
    for axis, least in (("split", 2), ("slab", 2)):
        bit = least
        while bit < lax.axis_size(axis):
            theirs = lax.ppermute(
                gathered, axis, [(i, i ^ bit) for i in range(lax.axis_size(axis))]
            )
            gathered = jnp.concatenate([gathered, theirs], axis=1)
            bit *= 2
    final_pos, final_vel = call(final_kernel, (perm, gathered), [jax.ShapeDtypeStruct(pp.shape, F32)] * 2)
    return (
        u,
        velocity,
        jnp.transpose(final_pos, (1, 0, 2)),
        jnp.transpose(final_vel, (1, 0, 2)),
    )


def solution(mesh):
    cells = P(None, "slab", "split", None)
    return jax.shard_map(
        per_device,
        mesh=mesh,
        in_specs=(cells, cells, cells, cells, P(), P(), P(), P(None, None, ("slab", "split"))),
        out_specs=(cells, cells, P(), P()),
        check_vma=False,
    )
```

```python
import functools
import math

import jax
import jax.numpy as jnp
from jax import lax
from jax.experimental import pallas as pl
from jax.experimental.pallas import tpu as pltpu
from jax.sharding import PartitionSpec as P

SUB = 3
SL = 4
SLOTS = 16
CHUNK = 4
STEP = 2
GROUP = 4
ROUNDS = (("slab", 8), ("slab", 4), ("split", 2), ("split", 4), ("slab", 2))

DT = 0.25
STIFF = 0.5
CONTACT = 0.05
WIDTH = 8.0
INV_MASS = 0.5

CX, CY, CZ = 8, 32, 256
LO = 8
F32 = jnp.float32


def bond_offsets():
    listed = []
    for sx in (-2, -1, 0, 1, 2):
        for sy in (-2, -1, 0, 1, 2):
            for sz in (-2, -1, 0, 1, 2):
                if 0 < sx * sx + sy * sy + sz * sz <= 4:
                    listed.append((sx, sy, sz))
    return listed


OFFSETS = bond_offsets()


def as_int32(bits):
    return bits - (1 << 32) if bits >= 1 << 31 else bits


def keep_bits(dim, allowed):
    return as_int32(sum(1 << n for n, e in enumerate(OFFSETS) if allowed(e[dim])))


def keep_word(index, last, dim):
    word = jnp.where(index == 0, keep_bits(dim, lambda e: e >= 0), -1)
    word = jnp.where(index == 1, keep_bits(dim, lambda e: e >= -1), word)
    word = jnp.where(index == last - 1, keep_bits(dim, lambda e: e <= 1), word)
    return jnp.where(index == last, keep_bits(dim, lambda e: e <= 0), word)


def position():
    return lax.axis_index("slab"), lax.axis_index("split")


def lane_sums(parts):
    whole = jnp.concatenate(parts, axis=0)
    high = whole.astype(jnp.bfloat16)
    low = (whole - high.astype(F32)).astype(jnp.bfloat16)
    ones = jnp.ones((256, 128), jnp.bfloat16)
    return jnp.dot(jnp.concatenate([high, low], axis=1), ones, preferred_element_type=F32)


def contact(substep, pairs, u_ref, half_ref, places, share, pos, ids, corner):
    row = lax.broadcasted_iota(jnp.int32, (CY, 128), 0)
    lane = lax.broadcasted_iota(jnp.int32, (CY, 128), 1)
    place_y = (row + corner[1]).astype(F32)
    live = jnp.int32(0)
    for k in range(SLOTS):
        live += (pairs[substep, 1, k] >= 0).astype(jnp.int32)

    @pl.when(live > 0)
    def _():
        def place(x, carry):
            for c in range(3):
                top = u_ref[c, 1, x + 2, LO : LO + CY, :]
                for z in range(SL):
                    lattice = ((corner[0] + x).astype(F32), place_y, float(CZ - SL + z))[c]
                    at = 128 - SL + z
                    column = jnp.broadcast_to(top[:, at : at + 1], (CY, 128))
                    places[c, x, z * CY : (z + 1) * CY, :] = column + lattice
            return carry

        lax.fori_loop(0, CX, place, 0)

    def slot(k, totals):
        target = jnp.clip(pairs[substep, 0, k], 0, CX - 1)
        chosen = pairs[substep, 1, k]
        hit = ids == chosen
        stiff = jnp.where(chosen >= 0, CONTACT, 0.0)
        q = [jnp.sum(jnp.where(hit, pos[c], 0.0), axis=0, keepdims=True) for c in range(3)]
        r = [places[c, target] - q[c] for c in range(3)]
        squared = r[0] * r[0] + r[1] * r[1] + r[2] * r[2]
        weight = stiff * jnp.exp(squared * (-1.0 / WIDTH))
        pulled = [weight * r[c] for c in range(3)]
        sums = lane_sums(pulled)
        for c in range(3):
            surface = jnp.zeros((CY, 128), F32)
            for z in range(SL):
                at = c * SL * CY + z * CY
                surface = jnp.where(lane == 128 - SL + z, sums[at : at + CY], surface)
            half_ref[c, target, :, CZ - 128 :] += share * surface
        return tuple(
            totals[c] - jnp.where(hit, jnp.sum(pulled[c], axis=0, keepdims=True), 0.0)
            for c in range(3)
        )

    def some(k, totals):
        for j in range(CHUNK):
            totals = slot(CHUNK * k + j, totals)
        return totals

    none = tuple(jnp.zeros((8, 128), F32) for _ in range(3))
    return lax.fori_loop(0, (live + CHUNK - 1) // CHUNK, some, none)


def send_edges(u_ref, force, xa, xb, ya, yb, even_x, even_y):
    at_a = jnp.where(even_x, CX, 2)
    at_b = jnp.where(even_x, 2, CX)
    for c in range(3):
        for h in range(2):
            lanes = slice(128 * h, 128 * h + 128)
            for layer in range(2):
                rows = slice((2 * c + layer) * CY, (2 * c + layer + 1) * CY)
                xa[rows, lanes] = u_ref[c, h, at_a + layer, LO : LO + CY, :]
                xb[rows, lanes] = u_ref[c, h, at_b + layer, LO : LO + CY, :]
            xa[6 * CY + 8 * c : 6 * CY + 8 * c + 8, lanes] = force[c]
    for want_even, low, high in ((True, yb, ya), (False, ya, yb)):

        @pl.when(even_y == want_even)
        def _(low=low, high=high):
            for c in range(3):
                for h in range(2):
                    lanes = slice(128 * h, 128 * h + 128)
                    for x in range(CX):
                        for r in range(2):
                            low[c, r, x : x + 1, lanes] = u_ref[c, h, x + 2, LO + r : LO + r + 1, :]
                            high[c, r, x : x + 1, lanes] = u_ref[
                                c, h, x + 2, LO + CY - 2 + r : LO + CY - 1 + r, :
                            ]


def begin_kernel(
    pairs, u, v, a, pp, pv, pa,
    u_out, half_out, pst, perm, xa, xb, ya, yb, places, cells, blocks_in, sems, block_sems,
):
    slab, split = position()
    splits = lax.axis_size("split")
    even_x, even_y = lax.rem(slab, 2) == 0, lax.rem(split, 2) == 0

    copies = []
    for x in range(0, CX, STEP):
        copies.append(
            [
                pltpu.make_async_copy(
                    source.at[:, x : x + STEP], cells.at[k, :, x : x + STEP], sems.at[k, x // STEP]
                )
                for k, source in enumerate((u, v, a))
            ]
        )
    block_copies = [
        pltpu.make_async_copy(source, blocks_in.at[k], block_sems.at[k])
        for k, source in enumerate((pp, pv, pa))
    ]
    for copy in block_copies:
        copy.start()
    for group in copies:
        for copy in group:
            copy.start()

    for copy in block_copies:
        copy.wait()
    pp, pv, pa = blocks_in.at[0], blocks_in.at[1], blocks_in.at[2]
    blocks = pp.shape[1]
    mean_x = jnp.sum(pp[0], axis=1, keepdims=True) * (1.0 / pp.shape[2])
    mean_y = jnp.sum(pp[1], axis=1, keepdims=True) * (1.0 / pp.shape[2])
    group_x = jnp.floor((mean_x + 0.5) * (1.0 / (2 * CX)))
    group_y = jnp.floor((mean_y + 0.5) * (1.0 / (2 * CY)))
    group = jnp.broadcast_to(group_x * (splits // 2) + group_y, (blocks, blocks))
    row = lax.broadcasted_iota(jnp.int32, (blocks, blocks), 0)
    lane = lax.broadcasted_iota(jnp.int32, (blocks, blocks), 1)
    earlier = jnp.where((group == group.T) & (lane < row), 1.0, 0.0)
    rank = jnp.sum(earlier, axis=1, keepdims=True).astype(jnp.int32)
    group = group.astype(jnp.int32)
    mine = (slab // 2) * (splits // 2) + split // 2
    other = group ^ mine
    slot = rank
    for order, (axis, bit) in enumerate(ROUNDS):
        place = bit // 2 * (splits // 2 if axis == "slab" else 1)
        slot = slot + jnp.where((other & place) != 0, GROUP << order, 0)
    perm[...] = jnp.where(slot == lane, 1.0, 0.0)

    pst[...] = jnp.zeros_like(pst)
    pst[6] = jnp.full((8, 128), -5.0, F32)
    for k in range(GROUP):
        chosen = slot == k
        pst[6, k : k + 1, :] = jnp.sum(jnp.where(chosen, row.astype(F32), 0.0), axis=0, keepdims=True)
        for c in range(3):
            pos, vel, acc = [
                jnp.sum(jnp.where(chosen, p[c], 0.0), axis=0, keepdims=True) for p in (pp, pv, pa)
            ]
            half = vel + 0.5 * DT * acc
            pst[3 + c, k : k + 1, :] = half
            pst[c, k : k + 1, :] = pos + DT * half

    for at, waits in zip(range(0, CX, STEP), copies):
        for copy in waits:
            copy.wait()
        for x in range(at, at + STEP):
            for c in range(3):
                half = cells[1, c, x] + 0.5 * DT * cells[2, c, x]
                half_out[c, x] = half
                moved = cells[0, c, x] + DT * half
                for h in range(2):
                    u_out[c, h, x + 2, LO : LO + CY, :] = moved[:, 128 * h : 128 * h + 128]

    ids = pst[6].astype(jnp.int32)
    pos = [pst[c] for c in range(3)]
    force = contact(0, pairs, u_out, half_out, places, DT, pos, ids, (slab * CX, split * CY))
    for c in range(3):
        pst[7 + c] = force[c]
    send_edges(u_out, force, xa, xb, ya, yb, even_x, even_y)


def words_kernel(masks, w_out, rim_out):
    slab, split = position()
    slabs, splits = lax.axis_size("slab"), lax.axis_size("split")

    for x in range(CX):
        kx = keep_word(slab * CX + x, slabs * CX - 1, 0)
        y = lax.broadcasted_iota(jnp.int32, (CY, CZ), 0)
        ky = keep_word(split * CY + y, splits * CY - 1, 1)
        kz = keep_word(lax.broadcasted_iota(jnp.int32, (CY, CZ), 1), CZ - 1, 2)
        word = masks[0, x] | (masks[1, x] << 8) | (masks[2, x] << 16) | (masks[3, x] << 24)
        word = word & ky & kz & kx
        w_out[x] = word & keep_word(y, CY - 1, 1)
        for r in range(4):
            y = r if r < 2 else CY - 4 + r
            rim_out[r, x : x + 1, :] = word[y : y + 1, :]


def corner_kernel(ya_own, yb_own, xa, xb, pst, token, ya, yb):
    slab, split = position()
    even_x, even_y = lax.rem(slab, 2) == 0, lax.rem(split, 2) == 0
    for c in range(3):
        for r in range(2):
            ya[c, r, 0:CX, :] = ya_own[c, r]
            yb[c, r, 0:CX, :] = yb_own[c, r]
        force = pst[7 + c] + xa[6 * CY + 8 * c : 6 * CY + 8 * c + 8, 0:128]
        for h in range(2):
            ya[c, 0, CX + 2 : CX + 2 + GROUP, 128 * h : 128 * h + 128] = force[0:GROUP]
    for is_x in (True, False):
        for is_y in (True, False):

            @pl.when((even_x == is_x) & (even_y == is_y))
            def _(is_x=is_x, is_y=is_y):
                for c in range(3):
                    for message, high in ((ya, is_y), (yb, not is_y)):
                        for got, top in ((xa, is_x), (xb, not is_x)):
                            entry, layer = (CX + 1, 0) if top else (CX, 1)
                            for r in range(2):
                                at = (2 * c + layer) * CY + (CY - 2 if high else 0) + r
                                message[c, r, entry : entry + 1, :] = got[at : at + 1, :]


def rolled(u, c, x, at, by):
    lane = lax.broadcasted_iota(jnp.int32, (8, 128), 1)
    turned = [pltpu.roll(u[c, h, x, at, :], by % 128, 1) for h in range(2)]
    wraps = lane < by if by > 0 else lane >= 128 + by
    return [jnp.where(wraps, turned[1 - h], turned[h]) for h in range(2)]


def turn(u, left, right, x, y):
    at = slice(y, y + 8)
    for c in range(3):
        for side, by in ((left, -1), (right, 1)):
            for h, value in enumerate(rolled(u, c, x, at, by)):
                side[c, h, x - 1, at, :] = value


def forces(u, left, right, w, x, y, h):
    own = [u[c, h, x + 2, LO + y : LO + y + 8, :] for c in range(3)]
    less = {(c, e): own[c] - float(e) if e else own[c] for c in range(3) for e in (-2, -1, 0, 1, 2)}
    word = w[x, y : y + 8, 128 * h : 128 * h + 128]
    total = [None] * 3
    for squared_length in (1, 2, 3, 4):
        sums = [None] * 3
        for number, e in enumerate(OFFSETS):
            if sum(k * k for k in e) != squared_length:
                continue
            at = slice(LO + y + e[1], LO + y + e[1] + 8)
            if e[2] == 0:
                near = [u[c, h, x + 2 + e[0], at, :] for c in range(3)]
            elif abs(e[2]) == 2:
                near = [rolled(u, c, x + 2, at, -e[2])[h] for c in range(3)]
            else:
                source = left if e[2] > 0 else right
                near = [source[c, h, x + 1 + e[0], at, :] for c in range(3)]
            d = [near[c] - less[c, e[c]] for c in range(3)]
            q = jnp.maximum(d[0] * d[0] + d[1] * d[1] + d[2] * d[2], 1e-30)
            pull = q * lax.rsqrt(q) - math.sqrt(squared_length)
            pull = jnp.where((word & as_int32(1 << number)) != 0, pull, 0.0)
            for c in range(3):
                if e[c] > 0:
                    sums[c] = pull if sums[c] is None else sums[c] + pull
                elif e[c] < 0:
                    sums[c] = -pull if sums[c] is None else sums[c] - pull
        factor = STIFF / squared_length * (2.0 if squared_length == 4 else 1.0)
        for c in range(3):
            term = factor * sums[c]
            total[c] = term if total[c] is None else total[c] + term
    return total


def advance(scale, u, left, right, w, half, half_out, first, out_first, count):
    def layer(k, carry):
        x = first + k
        for y in range(0, CY, 8):
            for h in range(2):
                at, lanes = slice(y, y + 8), slice(128 * h, 128 * h + 128)
                total = forces(u, left, right, w, x, y, h)
                for c in range(3):
                    half_out[c, out_first + k, at, lanes] = half[c, x, at, lanes] + scale * total[c]
        return carry

    lax.fori_loop(0, count, layer, 0)


def turned_layers(u, left, right):
    def shifted(x, carry):
        for y in range(LO, LO + CY, 8):
            turn(u, left, right, x, y)
        return carry

    lax.fori_loop(2, CX + 2, shifted, 0)


def inner_kernel(scale, u, half, w, half_out, left, right, token):
    turned_layers(u, left, right)
    advance(scale, u, left, right, w, half, half_out, 2, 0, CX - 4)
    token[...] = half_out[0, 0, 0:8, 0:128]


def edge_kernel(scale, xa, xb, u_own, left_own, right_own, half, w, after, half_out, token, u, left, right):
    slab, split = position()
    even_x = lax.rem(slab, 2) == 0
    to_a = jnp.where(even_x, CX + 2, 0)
    to_b = jnp.where(even_x, 0, CX + 2)
    rows = slice(LO, LO + CY)
    for c in range(3):
        for layer in range(2):
            part = slice((2 * c + layer) * CY, (2 * c + layer + 1) * CY)
            for h in range(2):
                lanes = slice(128 * h, 128 * h + 128)
                u[c, h, to_a + layer, rows, :] = xa[part, lanes]
                u[c, h, to_b + layer, rows, :] = xb[part, lanes]

    def own(x, carry):
        for c in range(3):
            for h in range(2):
                u[c, h, x + 2, rows, :] = u_own[c, h, x + 2, rows, :]
                left[c, h, x + 1, rows, :] = left_own[c, h, x + 1, rows, :]
                right[c, h, x + 1, rows, :] = right_own[c, h, x + 1, rows, :]
        return carry

    lax.fori_loop(0, CX, own, 0)
    for x in (1, CX + 2):
        for y in range(LO, LO + CY, 8):
            turn(u, left, right, x, y)
    advance(scale, u, left, right, w, half, half_out, 0, 0, 2)
    advance(scale, u, left, right, w, half, half_out, CX - 2, 2, 2)
    token[...] = half_out[0, 0, 0:8, 0:128]


def rim_forces(own, halo, rim, side, even_y, crossing):
    sub = lax.broadcasted_iota(jnp.int32, (8, 128), 0)
    lane = lax.broadcasted_iota(jnp.int32, (8, 128), 1)
    sign = -1 if side == 0 else 1
    for h in range(2):
        lanes = slice(128 * h, 128 * h + 128)
        total = [[None] * 3, [None] * 3]
        variants = {}

        def near(c, r, ex, ez):
            key = (c, r, ex, ez)
            if key not in variants:
                if ez:
                    both = [near_at(c, r, ex, k) for k in range(2)]
                    turned = [pltpu.roll(value, -ez % 128, 1) for value in both]
                    wraps = lane < -ez if ez < 0 else lane >= 128 - ez
                    variants[key] = jnp.where(wraps, turned[1 - h], turned[h])
                else:
                    variants[key] = near_at(c, r, ex, h)
            return variants[key]

        def near_at(c, r, ex, k):
            here = halo(c, r, slice(0, 8), k)
            if ex == 0:
                return here
            ends = halo(c, r, slice(8, 16), k)
            if ex > 0:
                return jnp.where(sub == 7, ends[1:2], pltpu.roll(here, 7, 0))
            return jnp.where(sub == 0, ends[0:1], pltpu.roll(here, 1, 0))

        for number, e in enumerate(OFFSETS):
            if e[1] * sign <= 0:
                continue
            squared_length = sum(k * k for k in e)
            for r in range(2):
                if abs(e[1]) <= r:
                    continue
                beyond = abs(e[1]) - r - 1
                mine = 1 - r if side else r
                theirs = beyond if side else 1 - beyond
                d = [near(c, theirs, e[0], e[2]) - (own(c, mine, h) - float(e[c])) for c in range(3)]
                q = jnp.maximum(d[0] * d[0] + d[1] * d[1] + d[2] * d[2], 1e-30)
                pull = (q * lax.rsqrt(q) - math.sqrt(squared_length)) * (STIFF / squared_length)
                word = rim[2 * side + mine, :, lanes]
                pull = jnp.where((word & as_int32(1 << number)) != 0, pull, 0.0)
                for c in range(3):
                    if e[c]:
                        term = float(e[c]) * pull
                        total[mine][c] = term if total[mine][c] is None else total[mine][c] + term
        for mine in range(2):
            for c in range(3):
                value = total[mine][c]
                crossing[2 * side + mine, c, h] = jnp.zeros((8, 128), F32) if value is None else value


def close(scale, inner, edge, ya_own, yb_own, ya, yb, rim, even_y, crossing, store):
    for side in range(2):
        first = even_y == (side == 1)

        def own(c, r, h):
            lanes = slice(128 * h, 128 * h + 128)
            return jnp.where(first, ya_own[c, r, :, lanes], yb_own[c, r, :, lanes])

        def halo(c, r, rows, h):
            lanes = slice(128 * h, 128 * h + 128)
            return jnp.where(first, ya[c, r, rows, lanes], yb[c, r, rows, lanes])

        rim_forces(own, halo, rim, side, even_y, crossing)
    sub = lax.broadcasted_iota(jnp.int32, (8, 128), 0)
    for x in range(CX):
        source, at = (inner, x - 2) if 2 <= x < CX - 2 else (edge, x if x < 2 else x - CX + 4)
        for c in range(3):
            for h in range(2):
                for y in range(0, CY, 8):
                    value = source[c, at, y : y + 8, 128 * h : 128 * h + 128]
                    for r in (0, 1) if y == 0 else (2, 3) if y == CY - 8 else ():
                        more = crossing[r, c, h, x : x + 1, :]
                        value = value + scale * jnp.where(sub == (r if r < 2 else r + 4), more, 0.0)
                    store(c, x, y, h, value)


def particle_force(xa, ya, pst, c):
    theirs = jnp.concatenate([ya[c, 0, CX + 2 : CX + 2 + GROUP, 0:128], jnp.zeros((4, 128), F32)], axis=0)
    return pst[7 + c] + xa[6 * CY + 8 * c : 6 * CY + 8 * c + 8, 0:128] + theirs


def close_kernel(
    substep, pairs, u, inner, edge, ya_own, yb_own, xa, ya, yb, rim, pst,
    u_out, half_out, pst_out, xa_out, xb_out, ya_out, yb_out, places, crossing,
):
    slab, split = position()
    even_x, even_y = lax.rem(slab, 2) == 0, lax.rem(split, 2) == 0

    def store(c, x, y, h, value):
        half_out[c, x, y : y + 8, 128 * h : 128 * h + 128] = value
        pad = slice(LO + y, LO + y + 8)
        u_out[c, h, x + 2, pad, :] = u[c, h, x + 2, pad, :] + DT * value

    close(DT, inner, edge, ya_own, yb_own, ya, yb, rim, even_y, crossing, store)

    pst_out[6:] = pst[6:]
    pos = []
    for c in range(3):
        moved = pst[3 + c] + DT * INV_MASS * particle_force(xa, ya, pst, c)
        pst_out[3 + c] = moved
        pos.append(pst[c] + DT * moved)
        pst_out[c] = pos[c]
    share = 0.5 * DT if substep == SUB - 2 else DT
    ids = pst[6].astype(jnp.int32)
    corner = (slab * CX, split * CY)
    force = contact(substep + 1, pairs, u_out, half_out, places, share, pos, ids, corner)
    for c in range(3):
        pst_out[7 + c] = force[c]
    send_edges(u_out, force, xa_out, xb_out, ya_out, yb_out, even_x, even_y)


def pair_kernel(xa, pst, out):
    for c in range(3):
        out[c] = pst[7 + c] + xa[6 * CY + 8 * c : 6 * CY + 8 * c + 8, 0:128]


def state_kernel(ours, theirs, pst, token, out):
    for c in range(3):
        out[c] = pst[c, 0:GROUP]
        acc = INV_MASS * (ours[c] + theirs[c])
        out[3 + c] = (pst[3 + c] + 0.5 * DT * acc)[0:GROUP]


def merge_kernel(ours, theirs, token, out):
    count = ours.shape[1]
    out[:, 0:count] = ours[...]
    out[:, count : 2 * count] = theirs[...]


def last_kernel(u, inner, edge, ya_own, yb_own, ya, yb, rim, after, u_out, v_out, token, crossing):
    slab, split = position()

    def store(c, x, y, h, value):
        lanes = slice(128 * h, 128 * h + 128)
        v_out[c, x, y : y + 8, lanes] = value
        u_out[c, x, y : y + 8, lanes] = u[c, h, x + 2, LO + y : LO + y + 8, :]

    even_y = lax.rem(split, 2) == 0
    close(0.5 * DT, inner, edge, ya_own, yb_own, ya, yb, rim, even_y, crossing, store)
    token[...] = crossing[0, 0, 0]


def final_kernel(perm, gathered, pos_out, vel_out):
    for c in range(3):
        for at, out in ((c, pos_out), (3 + c, vel_out)):
            out[c] = jnp.dot(
                perm[...],
                gathered[at],
                precision=lax.Precision.HIGHEST,
                preferred_element_type=F32,
            )


VMEM = pl.BlockSpec(memory_space=pltpu.VMEM)
SMEM = pl.BlockSpec(memory_space=pltpu.SMEM)
HBM = pl.BlockSpec(memory_space=pltpu.HBM)
STATE = jax.ShapeDtypeStruct((3, CX, CY, CZ), F32)
PADDED = jax.ShapeDtypeStruct((3, 2, CX + 4, CY + 16, 128), F32)
SIDE = jax.ShapeDtypeStruct((3, 2, CX + 2, CY + 16, 128), F32)
WORDS = jax.ShapeDtypeStruct((CX, CY, CZ), jnp.int32)
PST = jax.ShapeDtypeStruct((10, 8, 128), F32)
XA = jax.ShapeDtypeStruct((6 * CY + 24, CZ), F32)
XB = jax.ShapeDtypeStruct((6 * CY, CZ), F32)
YE = jax.ShapeDtypeStruct((3, 2, CX, CZ), F32)
YA = jax.ShapeDtypeStruct((3, 2, 16, CZ), F32)
PAIR = jax.ShapeDtypeStruct((3, 8, 128), F32)
TOKEN = jax.ShapeDtypeStruct((8, 128), F32)
HALVES = jax.ShapeDtypeStruct((3, 4, CY, CZ), F32)
RIM = jax.ShapeDtypeStruct((4, CX, CZ), jnp.int32)
CROSSING = pltpu.VMEM((4, 3, 2, CX, 128), F32)
PLACES = pltpu.VMEM((3, CX, SL * CY, 128), F32)


def call(kernel, inputs, outputs, scalars=0, scratch=(), ins=None, limit=40, us=1.0):
    return pl.pallas_call(
        kernel,
        out_shape=outputs,
        in_specs=ins or [SMEM] * scalars + [VMEM] * (len(inputs) - scalars),
        out_specs=[VMEM] * len(outputs),
        scratch_shapes=list(scratch),
        compiler_params=pltpu.CompilerParams(vmem_limit_bytes=limit << 20),
        cost_estimate=pl.CostEstimate(flops=0, transcendentals=0, bytes_accessed=int(us * 3.0e6)),
    )(*inputs)


def swap(value, axis, offset):
    pairs = []
    for i in range(offset, lax.axis_size(axis) - 1, 2):
        pairs += [(i, i + 1), (i + 1, i)]
    return lax.ppermute(value, axis, pairs)


def rows_of(count):
    return jax.ShapeDtypeStruct((6, count, 128), F32)


def share_round(gathered, number, token):
    axis, bit = ROUNDS[number]
    theirs = lax.ppermute(gathered, axis, [(i, i ^ bit) for i in range(lax.axis_size(axis))])
    (merged,) = call(merge_kernel, (gathered, theirs, token), [rows_of(2 * gathered.shape[1])], us=0.1)
    return merged


def per_device(u, v, a, masks, proj_pos, proj_vel, proj_acc, pairs):
    pp, pv, pa = [jnp.transpose(p, (1, 0, 2)) for p in (proj_pos, proj_vel, proj_acc)]
    blocks = pp.shape[1]
    u, half, pst, perm, *edges = call(
        begin_kernel,
        (pairs, u, v, a, pp, pv, pa),
        [PADDED, STATE, PST, jax.ShapeDtypeStruct((blocks, blocks), F32), XA, XB, YE, YE],
        ins=[SMEM] + [HBM] * 6,
        limit=60,
        scratch=(
            PLACES,
            pltpu.VMEM((3, *STATE.shape), F32),
            pltpu.VMEM((3, *pp.shape), F32),
            pltpu.SemaphoreType.DMA((3, CX // STEP)),
            pltpu.SemaphoreType.DMA((3,)),
        ),
    )
    words, rim = call(words_kernel, (masks,), [WORDS, RIM])
    for substep in range(SUB):
        last = substep == SUB - 1
        scale = 0.5 * DT if last else DT
        xa, xb, ya_own, yb_own = edges
        xa, xb = swap(xa, "slab", 0), swap(xb, "slab", 1)
        if last:
            (ours,) = call(pair_kernel, (xa, pst), [PAIR], us=0.1)
            theirs = swap(ours, "split", 0)
        inner, left, right, token = call(
            functools.partial(inner_kernel, scale), (u, half, words), [HALVES, SIDE, SIDE, TOKEN], us=3.6
        )
        ya, yb = call(corner_kernel, (ya_own, yb_own, xa, xb, pst, token), [YA, YA], us=0.1)
        ya, yb = swap(ya, "split", 0), swap(yb, "split", 1)
        after = token
        if last:
            (gathered,) = call(state_kernel, (ours, theirs, pst, token), [rows_of(GROUP)], us=0.1)
            gathered = after = share_round(gathered, 0, token)
        edge, token = call(
            functools.partial(edge_kernel, scale),
            (xa, xb, u, left, right, half, words, after),
            [HALVES, TOKEN],
            scratch=[pltpu.VMEM(shape.shape, F32) for shape in (PADDED, SIDE, SIDE)],
            us=3.6,
        )
        if last:
            break
        u, half, pst, *edges = call(
            functools.partial(close_kernel, substep),
            (pairs, u, inner, edge, ya_own, yb_own, xa, ya, yb, rim, pst),
            [PADDED, STATE, PST, XA, XB, YE, YE],
            scalars=1,
            scratch=(PLACES, CROSSING),
            us=3.0,
        )

    gathered = share_round(gathered, 1, token)
    final_u, final_v, token = call(
        last_kernel,
        (u, inner, edge, ya_own, yb_own, ya, yb, rim, gathered),
        [STATE, STATE, TOKEN],
        scratch=(CROSSING,),
        us=1.4,
    )
    for number in range(2, len(ROUNDS)):
        gathered = share_round(gathered, number, token)
    final_pos, final_vel = call(final_kernel, (perm, gathered), [jax.ShapeDtypeStruct(pp.shape, F32)] * 2)
    return (
        final_u,
        final_v,
        jnp.transpose(final_pos, (1, 0, 2)),
        jnp.transpose(final_vel, (1, 0, 2)),
    )


def solution(mesh):
    cells = P(None, "slab", "split", None)
    return jax.shard_map(
        per_device,
        mesh=mesh,
        in_specs=(cells, cells, cells, cells, P(), P(), P(), P(None, None, ("slab", "split"))),
        out_specs=(cells, cells, P(), P()),
        check_vma=False,
    )
```

```python
import functools
import math

import jax
import jax.numpy as jnp
from jax import lax
from jax.experimental import pallas as pl
from jax.experimental.pallas import tpu as pltpu
from jax.sharding import PartitionSpec as P

SUB = 3
SL = 4
SLOTS = 16
CHUNK = 4
STEP = 2
GROUP = 4
ROUNDS = (("slab", 8), ("slab", 4), ("split", 2), ("split", 4), ("slab", 2))

DT = 0.25
STIFF = 0.5
CONTACT = 0.05
WIDTH = 8.0
INV_MASS = 0.5

CX, CY, CZ = 8, 32, 256
LO = 8
F32 = jnp.float32


def bond_offsets():
    listed = []
    for sx in (-2, -1, 0, 1, 2):
        for sy in (-2, -1, 0, 1, 2):
            for sz in (-2, -1, 0, 1, 2):
                if 0 < sx * sx + sy * sy + sz * sz <= 4:
                    listed.append((sx, sy, sz))
    return listed


OFFSETS = bond_offsets()


def as_int32(bits):
    return bits - (1 << 32) if bits >= 1 << 31 else bits


def keep_bits(dim, allowed):
    return as_int32(sum(1 << n for n, e in enumerate(OFFSETS) if allowed(e[dim])))


def keep_word(index, last, dim):
    word = jnp.where(index == 0, keep_bits(dim, lambda e: e >= 0), -1)
    word = jnp.where(index == 1, keep_bits(dim, lambda e: e >= -1), word)
    word = jnp.where(index == last - 1, keep_bits(dim, lambda e: e <= 1), word)
    return jnp.where(index == last, keep_bits(dim, lambda e: e <= 0), word)


def position():
    return lax.axis_index("slab"), lax.axis_index("split")


def lane_sums(parts):
    whole = jnp.concatenate(parts, axis=0)
    high = whole.astype(jnp.bfloat16)
    low = (whole - high.astype(F32)).astype(jnp.bfloat16)
    ones = jnp.ones((256, 128), jnp.bfloat16)
    return jnp.dot(jnp.concatenate([high, low], axis=1), ones, preferred_element_type=F32)


def contact(substep, pairs, u_ref, half_ref, places, share, pos, ids, corner):
    row = lax.broadcasted_iota(jnp.int32, (CY, 128), 0)
    lane = lax.broadcasted_iota(jnp.int32, (CY, 128), 1)
    place_y = (row + corner[1]).astype(F32)
    live = jnp.int32(0)
    for k in range(SLOTS):
        live += (pairs[substep, 1, k] >= 0).astype(jnp.int32)

    @pl.when(live > 0)
    def _():
        def place(x, carry):
            for c in range(3):
                top = u_ref[c, 1, x + 2, LO : LO + CY, :]
                for z in range(SL):
                    lattice = ((corner[0] + x).astype(F32), place_y, float(CZ - SL + z))[c]
                    at = 128 - SL + z
                    column = jnp.broadcast_to(top[:, at : at + 1], (CY, 128))
                    places[c, x, z * CY : (z + 1) * CY, :] = column + lattice
            return carry

        lax.fori_loop(0, CX, place, 0)

    def slot(k, totals):
        target = jnp.clip(pairs[substep, 0, k], 0, CX - 1)
        chosen = pairs[substep, 1, k]
        hit = ids == chosen
        stiff = jnp.where(chosen >= 0, CONTACT, 0.0)
        q = [jnp.sum(jnp.where(hit, pos[c], 0.0), axis=0, keepdims=True) for c in range(3)]
        r = [places[c, target] - q[c] for c in range(3)]
        squared = r[0] * r[0] + r[1] * r[1] + r[2] * r[2]
        weight = stiff * jnp.exp(squared * (-1.0 / WIDTH))
        pulled = [weight * r[c] for c in range(3)]
        sums = lane_sums(pulled)
        for c in range(3):
            surface = jnp.zeros((CY, 128), F32)
            for z in range(SL):
                at = c * SL * CY + z * CY
                surface = jnp.where(lane == 128 - SL + z, sums[at : at + CY], surface)
            half_ref[c, target, :, CZ - 128 :] += share * surface
        return tuple(
            totals[c] - jnp.where(hit, jnp.sum(pulled[c], axis=0, keepdims=True), 0.0)
            for c in range(3)
        )

    def some(k, totals):
        for j in range(CHUNK):
            totals = slot(CHUNK * k + j, totals)
        return totals

    none = tuple(jnp.zeros((8, 128), F32) for _ in range(3))
    return lax.fori_loop(0, (live + CHUNK - 1) // CHUNK, some, none)


def send_edges(u_ref, force, xa, xb, ya, yb, even_x, even_y):
    at_a = jnp.where(even_x, CX, 2)
    at_b = jnp.where(even_x, 2, CX)
    for c in range(3):
        for h in range(2):
            lanes = slice(128 * h, 128 * h + 128)
            for layer in range(2):
                rows = slice((2 * c + layer) * CY, (2 * c + layer + 1) * CY)
                xa[rows, lanes] = u_ref[c, h, at_a + layer, LO : LO + CY, :]
                xb[rows, lanes] = u_ref[c, h, at_b + layer, LO : LO + CY, :]
            xa[6 * CY + 8 * c : 6 * CY + 8 * c + 8, lanes] = force[c]
    for want_even, low, high in ((True, yb, ya), (False, ya, yb)):

        @pl.when(even_y == want_even)
        def _(low=low, high=high):
            for c in range(3):
                for h in range(2):
                    lanes = slice(128 * h, 128 * h + 128)
                    for x in range(CX):
                        for r in range(2):
                            low[c, r, x : x + 1, lanes] = u_ref[c, h, x + 2, LO + r : LO + r + 1, :]
                            high[c, r, x : x + 1, lanes] = u_ref[
                                c, h, x + 2, LO + CY - 2 + r : LO + CY - 1 + r, :
                            ]


def begin_kernel(
    pairs, u, v, a, pp, pv, pa,
    u_out, half_out, pst, perm, xa, xb, ya, yb, places, cells, blocks_in, sems, block_sems,
):
    slab, split = position()
    splits = lax.axis_size("split")
    even_x, even_y = lax.rem(slab, 2) == 0, lax.rem(split, 2) == 0

    copies = []
    for x in range(0, CX, STEP):
        copies.append(
            [
                pltpu.make_async_copy(
                    source.at[:, x : x + STEP], cells.at[k, :, x : x + STEP], sems.at[k, x // STEP]
                )
                for k, source in enumerate((u, v, a))
            ]
        )
    block_copies = [
        pltpu.make_async_copy(source, blocks_in.at[k], block_sems.at[k])
        for k, source in enumerate((pp, pv, pa))
    ]
    for copy in block_copies:
        copy.start()
    for group in copies:
        for copy in group:
            copy.start()

    for copy in block_copies:
        copy.wait()
    pp, pv, pa = blocks_in.at[0], blocks_in.at[1], blocks_in.at[2]
    blocks = pp.shape[1]
    mean_x = jnp.sum(pp[0], axis=1, keepdims=True) * (1.0 / pp.shape[2])
    mean_y = jnp.sum(pp[1], axis=1, keepdims=True) * (1.0 / pp.shape[2])
    group_x = jnp.floor((mean_x + 0.5) * (1.0 / (2 * CX)))
    group_y = jnp.floor((mean_y + 0.5) * (1.0 / (2 * CY)))
    group = jnp.broadcast_to(group_x * (splits // 2) + group_y, (blocks, blocks))
    row = lax.broadcasted_iota(jnp.int32, (blocks, blocks), 0)
    lane = lax.broadcasted_iota(jnp.int32, (blocks, blocks), 1)
    earlier = jnp.where((group == group.T) & (lane < row), 1.0, 0.0)
    rank = jnp.sum(earlier, axis=1, keepdims=True).astype(jnp.int32)
    group = group.astype(jnp.int32)
    mine = (slab // 2) * (splits // 2) + split // 2
    other = group ^ mine
    slot = rank
    for order, (axis, bit) in enumerate(ROUNDS):
        place = bit // 2 * (splits // 2 if axis == "slab" else 1)
        slot = slot + jnp.where((other & place) != 0, GROUP << order, 0)
    perm[...] = jnp.where(slot == lane, 1.0, 0.0)

    pst[...] = jnp.zeros_like(pst)
    pst[6] = jnp.full((8, 128), -5.0, F32)
    for k in range(GROUP):
        chosen = slot == k
        pst[6, k : k + 1, :] = jnp.sum(jnp.where(chosen, row.astype(F32), 0.0), axis=0, keepdims=True)
        for c in range(3):
            pos, vel, acc = [
                jnp.sum(jnp.where(chosen, p[c], 0.0), axis=0, keepdims=True) for p in (pp, pv, pa)
            ]
            half = vel + 0.5 * DT * acc
            pst[3 + c, k : k + 1, :] = half
            pst[c, k : k + 1, :] = pos + DT * half

    for at, waits in zip(range(0, CX, STEP), copies):
        for copy in waits:
            copy.wait()
        for x in range(at, at + STEP):
            for c in range(3):
                half = cells[1, c, x] + 0.5 * DT * cells[2, c, x]
                half_out[c, x] = half
                moved = cells[0, c, x] + DT * half
                for h in range(2):
                    u_out[c, h, x + 2, LO : LO + CY, :] = moved[:, 128 * h : 128 * h + 128]

    ids = pst[6].astype(jnp.int32)
    pos = [pst[c] for c in range(3)]
    force = contact(0, pairs, u_out, half_out, places, DT, pos, ids, (slab * CX, split * CY))
    for c in range(3):
        pst[7 + c] = force[c]
    send_edges(u_out, force, xa, xb, ya, yb, even_x, even_y)


def words_kernel(masks, w_out, rim_out):
    slab, split = position()
    slabs, splits = lax.axis_size("slab"), lax.axis_size("split")

    for x in range(CX):
        kx = keep_word(slab * CX + x, slabs * CX - 1, 0)
        y = lax.broadcasted_iota(jnp.int32, (CY, CZ), 0)
        ky = keep_word(split * CY + y, splits * CY - 1, 1)
        kz = keep_word(lax.broadcasted_iota(jnp.int32, (CY, CZ), 1), CZ - 1, 2)
        word = masks[0, x] | (masks[1, x] << 8) | (masks[2, x] << 16) | (masks[3, x] << 24)
        word = word & ky & kz & kx
        w_out[x] = word & keep_word(y, CY - 1, 1)
        for r in range(4):
            y = r if r < 2 else CY - 4 + r
            rim_out[r, x : x + 1, :] = word[y : y + 1, :]


def corner_kernel(ya_own, yb_own, xa, xb, pst, token, ya, yb):
    slab, split = position()
    even_x, even_y = lax.rem(slab, 2) == 0, lax.rem(split, 2) == 0
    for c in range(3):
        for r in range(2):
            ya[c, r, 0:CX, :] = ya_own[c, r]
            yb[c, r, 0:CX, :] = yb_own[c, r]
        force = pst[7 + c] + xa[6 * CY + 8 * c : 6 * CY + 8 * c + 8, 0:128]
        for h in range(2):
            ya[c, 0, CX + 2 : CX + 2 + GROUP, 128 * h : 128 * h + 128] = force[0:GROUP]
    for is_x in (True, False):
        for is_y in (True, False):

            @pl.when((even_x == is_x) & (even_y == is_y))
            def _(is_x=is_x, is_y=is_y):
                for c in range(3):
                    for message, high in ((ya, is_y), (yb, not is_y)):
                        for got, top in ((xa, is_x), (xb, not is_x)):
                            entry, layer = (CX + 1, 0) if top else (CX, 1)
                            for r in range(2):
                                at = (2 * c + layer) * CY + (CY - 2 if high else 0) + r
                                message[c, r, entry : entry + 1, :] = got[at : at + 1, :]


def rolled(u, c, x, at, by):
    lane = lax.broadcasted_iota(jnp.int32, (8, 128), 1)
    turned = [pltpu.roll(u[c, h, x, at, :], by % 128, 1) for h in range(2)]
    wraps = lane < by if by > 0 else lane >= 128 + by
    return [jnp.where(wraps, turned[1 - h], turned[h]) for h in range(2)]


def turn(u, left, right, x, y):
    at = slice(y, y + 8)
    for c in range(3):
        for side, by in ((left, -1), (right, 1)):
            for h, value in enumerate(rolled(u, c, x, at, by)):
                side[c, h, x - 1, at, :] = value


def forces(u, left, right, w, x, y, h):
    own = [u[c, h, x + 2, LO + y : LO + y + 8, :] for c in range(3)]
    less = {(c, e): own[c] - float(e) if e else own[c] for c in range(3) for e in (-2, -1, 0, 1, 2)}
    word = w[x, y : y + 8, 128 * h : 128 * h + 128]
    total = [None] * 3
    for squared_length in (1, 2, 3, 4):
        sums = [None] * 3
        for number, e in enumerate(OFFSETS):
            if sum(k * k for k in e) != squared_length:
                continue
            at = slice(LO + y + e[1], LO + y + e[1] + 8)
            if e[2] == 0:
                near = [u[c, h, x + 2 + e[0], at, :] for c in range(3)]
            elif abs(e[2]) == 2:
                near = [rolled(u, c, x + 2, at, -e[2])[h] for c in range(3)]
            else:
                source = left if e[2] > 0 else right
                near = [source[c, h, x + 1 + e[0], at, :] for c in range(3)]
            d = [near[c] - less[c, e[c]] for c in range(3)]
            q = jnp.maximum(d[0] * d[0] + d[1] * d[1] + d[2] * d[2], 1e-30)
            pull = q * lax.rsqrt(q) - math.sqrt(squared_length)
            pull = jnp.where((word & as_int32(1 << number)) != 0, pull, 0.0)
            for c in range(3):
                if e[c] > 0:
                    sums[c] = pull if sums[c] is None else sums[c] + pull
                elif e[c] < 0:
                    sums[c] = -pull if sums[c] is None else sums[c] - pull
        factor = STIFF / squared_length * (2.0 if squared_length == 4 else 1.0)
        for c in range(3):
            term = factor * sums[c]
            total[c] = term if total[c] is None else total[c] + term
    return total


def advance(scale, u, left, right, w, half, half_out, first, out_first, count):
    def layer(k, carry):
        x = first + k
        for y in range(0, CY, 8):
            for h in range(2):
                at, lanes = slice(y, y + 8), slice(128 * h, 128 * h + 128)
                total = forces(u, left, right, w, x, y, h)
                for c in range(3):
                    half_out[c, out_first + k, at, lanes] = half[c, x, at, lanes] + scale * total[c]
        return carry

    lax.fori_loop(0, count, layer, 0)


def turned_layers(u, left, right):
    def shifted(x, carry):
        for y in range(LO, LO + CY, 8):
            turn(u, left, right, x, y)
        return carry

    lax.fori_loop(2, CX + 2, shifted, 0)


def turn_kernel(u, left, right, token):
    turned_layers(u, left, right)
    token[...] = left[0, 0, 1, LO : LO + 8, :]


def late_inner_kernel(scale, u, left, right, half, w, after, half_out, token):
    advance(scale, u, left, right, w, half, half_out, 2, 0, CX - 4)
    token[...] = half_out[0, 0, 0:8, 0:128]


def inner_kernel(scale, u, half, w, half_out, left, right, token):
    turned_layers(u, left, right)
    advance(scale, u, left, right, w, half, half_out, 2, 0, CX - 4)
    token[...] = half_out[0, 0, 0:8, 0:128]


def edge_kernel(scale, xa, xb, u_own, left_own, right_own, half, w, after, half_out, token, u, left, right):
    slab, split = position()
    even_x = lax.rem(slab, 2) == 0
    to_a = jnp.where(even_x, CX + 2, 0)
    to_b = jnp.where(even_x, 0, CX + 2)
    rows = slice(LO, LO + CY)
    for c in range(3):
        for layer in range(2):
            part = slice((2 * c + layer) * CY, (2 * c + layer + 1) * CY)
            for h in range(2):
                lanes = slice(128 * h, 128 * h + 128)
                u[c, h, to_a + layer, rows, :] = xa[part, lanes]
                u[c, h, to_b + layer, rows, :] = xb[part, lanes]

    def own(x, carry):
        for c in range(3):
            for h in range(2):
                u[c, h, x + 2, rows, :] = u_own[c, h, x + 2, rows, :]
                left[c, h, x + 1, rows, :] = left_own[c, h, x + 1, rows, :]
                right[c, h, x + 1, rows, :] = right_own[c, h, x + 1, rows, :]
        return carry

    lax.fori_loop(0, CX, own, 0)
    for x in (1, CX + 2):
        for y in range(LO, LO + CY, 8):
            turn(u, left, right, x, y)
    advance(scale, u, left, right, w, half, half_out, 0, 0, 2)
    advance(scale, u, left, right, w, half, half_out, CX - 2, 2, 2)
    token[...] = half_out[0, 0, 0:8, 0:128]


def rim_forces(own, halo, rim, side, even_y, crossing):
    sub = lax.broadcasted_iota(jnp.int32, (8, 128), 0)
    lane = lax.broadcasted_iota(jnp.int32, (8, 128), 1)
    sign = -1 if side == 0 else 1
    for h in range(2):
        lanes = slice(128 * h, 128 * h + 128)
        total = [[None] * 3, [None] * 3]
        variants = {}

        def near(c, r, ex, ez):
            key = (c, r, ex, ez)
            if key not in variants:
                if ez:
                    both = [near_at(c, r, ex, k) for k in range(2)]
                    turned = [pltpu.roll(value, -ez % 128, 1) for value in both]
                    wraps = lane < -ez if ez < 0 else lane >= 128 - ez
                    variants[key] = jnp.where(wraps, turned[1 - h], turned[h])
                else:
                    variants[key] = near_at(c, r, ex, h)
            return variants[key]

        def near_at(c, r, ex, k):
            here = halo(c, r, slice(0, 8), k)
            if ex == 0:
                return here
            ends = halo(c, r, slice(8, 16), k)
            if ex > 0:
                return jnp.where(sub == 7, ends[1:2], pltpu.roll(here, 7, 0))
            return jnp.where(sub == 0, ends[0:1], pltpu.roll(here, 1, 0))

        for number, e in enumerate(OFFSETS):
            if e[1] * sign <= 0:
                continue
            squared_length = sum(k * k for k in e)
            for r in range(2):
                if abs(e[1]) <= r:
                    continue
                beyond = abs(e[1]) - r - 1
                mine = 1 - r if side else r
                theirs = beyond if side else 1 - beyond
                d = [near(c, theirs, e[0], e[2]) - (own(c, mine, h) - float(e[c])) for c in range(3)]
                q = jnp.maximum(d[0] * d[0] + d[1] * d[1] + d[2] * d[2], 1e-30)
                pull = (q * lax.rsqrt(q) - math.sqrt(squared_length)) * (STIFF / squared_length)
                word = rim[2 * side + mine, :, lanes]
                pull = jnp.where((word & as_int32(1 << number)) != 0, pull, 0.0)
                for c in range(3):
                    if e[c]:
                        term = float(e[c]) * pull
                        total[mine][c] = term if total[mine][c] is None else total[mine][c] + term
        for mine in range(2):
            for c in range(3):
                value = total[mine][c]
                crossing[2 * side + mine, c, h] = jnp.zeros((8, 128), F32) if value is None else value


def close(scale, inner, edge, ya_own, yb_own, ya, yb, rim, even_y, crossing, store):
    for side in range(2):
        first = even_y == (side == 1)

        def own(c, r, h):
            lanes = slice(128 * h, 128 * h + 128)
            return jnp.where(first, ya_own[c, r, :, lanes], yb_own[c, r, :, lanes])

        def halo(c, r, rows, h):
            lanes = slice(128 * h, 128 * h + 128)
            return jnp.where(first, ya[c, r, rows, lanes], yb[c, r, rows, lanes])

        rim_forces(own, halo, rim, side, even_y, crossing)
    sub = lax.broadcasted_iota(jnp.int32, (8, 128), 0)
    for x in range(CX):
        source, at = (inner, x - 2) if 2 <= x < CX - 2 else (edge, x if x < 2 else x - CX + 4)
        for c in range(3):
            for h in range(2):
                for y in range(0, CY, 8):
                    value = source[c, at, y : y + 8, 128 * h : 128 * h + 128]
                    for r in (0, 1) if y == 0 else (2, 3) if y == CY - 8 else ():
                        more = crossing[r, c, h, x : x + 1, :]
                        value = value + scale * jnp.where(sub == (r if r < 2 else r + 4), more, 0.0)
                    store(c, x, y, h, value)


def particle_force(xa, ya, pst, c):
    theirs = jnp.concatenate([ya[c, 0, CX + 2 : CX + 2 + GROUP, 0:128], jnp.zeros((4, 128), F32)], axis=0)
    return pst[7 + c] + xa[6 * CY + 8 * c : 6 * CY + 8 * c + 8, 0:128] + theirs


def close_kernel(
    substep, pairs, u, inner, edge, ya_own, yb_own, xa, ya, yb, rim, pst,
    u_out, half_out, pst_out, xa_out, xb_out, ya_out, yb_out, places, crossing,
):
    slab, split = position()
    even_x, even_y = lax.rem(slab, 2) == 0, lax.rem(split, 2) == 0

    def store(c, x, y, h, value):
        half_out[c, x, y : y + 8, 128 * h : 128 * h + 128] = value
        pad = slice(LO + y, LO + y + 8)
        u_out[c, h, x + 2, pad, :] = u[c, h, x + 2, pad, :] + DT * value

    close(DT, inner, edge, ya_own, yb_own, ya, yb, rim, even_y, crossing, store)

    pst_out[6:] = pst[6:]
    pos = []
    for c in range(3):
        moved = pst[3 + c] + DT * INV_MASS * particle_force(xa, ya, pst, c)
        pst_out[3 + c] = moved
        pos.append(pst[c] + DT * moved)
        pst_out[c] = pos[c]
    share = 0.5 * DT if substep == SUB - 2 else DT
    ids = pst[6].astype(jnp.int32)
    corner = (slab * CX, split * CY)
    force = contact(substep + 1, pairs, u_out, half_out, places, share, pos, ids, corner)
    for c in range(3):
        pst_out[7 + c] = force[c]
    send_edges(u_out, force, xa_out, xb_out, ya_out, yb_out, even_x, even_y)


def pair_kernel(xa, pst, out):
    for c in range(3):
        out[c] = pst[7 + c] + xa[6 * CY + 8 * c : 6 * CY + 8 * c + 8, 0:128]


def state_kernel(ours, theirs, pst, token, out):
    for c in range(3):
        out[c] = pst[c, 0:GROUP]
        acc = INV_MASS * (ours[c] + theirs[c])
        out[3 + c] = (pst[3 + c] + 0.5 * DT * acc)[0:GROUP]


def merge_kernel(ours, theirs, token, out):
    count = ours.shape[1]
    out[:, 0:count] = ours[...]
    out[:, count : 2 * count] = theirs[...]


def last_kernel(u, inner, edge, ya_own, yb_own, ya, yb, rim, after, u_out, v_out, token, crossing):
    slab, split = position()

    def store(c, x, y, h, value):
        lanes = slice(128 * h, 128 * h + 128)
        v_out[c, x, y : y + 8, lanes] = value
        u_out[c, x, y : y + 8, lanes] = u[c, h, x + 2, LO + y : LO + y + 8, :]

    even_y = lax.rem(split, 2) == 0
    close(0.5 * DT, inner, edge, ya_own, yb_own, ya, yb, rim, even_y, crossing, store)
    token[...] = crossing[0, 0, 0]


def final_kernel(perm, gathered, pos_out, vel_out):
    for c in range(3):
        for at, out in ((c, pos_out), (3 + c, vel_out)):
            out[c] = jnp.dot(
                perm[...],
                gathered[at],
                precision=lax.Precision.HIGHEST,
                preferred_element_type=F32,
            )


VMEM = pl.BlockSpec(memory_space=pltpu.VMEM)
SMEM = pl.BlockSpec(memory_space=pltpu.SMEM)
HBM = pl.BlockSpec(memory_space=pltpu.HBM)
STATE = jax.ShapeDtypeStruct((3, CX, CY, CZ), F32)
PADDED = jax.ShapeDtypeStruct((3, 2, CX + 4, CY + 16, 128), F32)
SIDE = jax.ShapeDtypeStruct((3, 2, CX + 2, CY + 16, 128), F32)
WORDS = jax.ShapeDtypeStruct((CX, CY, CZ), jnp.int32)
PST = jax.ShapeDtypeStruct((10, 8, 128), F32)
XA = jax.ShapeDtypeStruct((6 * CY + 24, CZ), F32)
XB = jax.ShapeDtypeStruct((6 * CY, CZ), F32)
YE = jax.ShapeDtypeStruct((3, 2, CX, CZ), F32)
YA = jax.ShapeDtypeStruct((3, 2, 16, CZ), F32)
PAIR = jax.ShapeDtypeStruct((3, 8, 128), F32)
TOKEN = jax.ShapeDtypeStruct((8, 128), F32)
HALVES = jax.ShapeDtypeStruct((3, 4, CY, CZ), F32)
RIM = jax.ShapeDtypeStruct((4, CX, CZ), jnp.int32)
CROSSING = pltpu.VMEM((4, 3, 2, CX, 128), F32)
PLACES = pltpu.VMEM((3, CX, SL * CY, 128), F32)


def call(kernel, inputs, outputs, scalars=0, scratch=(), ins=None, limit=40, us=1.0):
    return pl.pallas_call(
        kernel,
        out_shape=outputs,
        in_specs=ins or [SMEM] * scalars + [VMEM] * (len(inputs) - scalars),
        out_specs=[VMEM] * len(outputs),
        scratch_shapes=list(scratch),
        compiler_params=pltpu.CompilerParams(vmem_limit_bytes=limit << 20),
        cost_estimate=pl.CostEstimate(flops=0, transcendentals=0, bytes_accessed=int(us * 3.0e6)),
    )(*inputs)


def swap(value, axis, offset):
    count = lax.axis_size(axis)
    pairs = []
    for i in range(offset, count, 2):
        pairs += [(i, (i + 1) % count), ((i + 1) % count, i)]
    return lax.ppermute(value, axis, pairs)


def rows_of(count):
    return jax.ShapeDtypeStruct((6, count, 128), F32)


def share_round(gathered, number, token):
    axis, bit = ROUNDS[number]
    theirs = lax.ppermute(gathered, axis, [(i, i ^ bit) for i in range(lax.axis_size(axis))])
    (merged,) = call(merge_kernel, (gathered, theirs, token), [rows_of(2 * gathered.shape[1])], us=0.1)
    return merged


def per_device(u, v, a, masks, proj_pos, proj_vel, proj_acc, pairs):
    pp, pv, pa = [jnp.transpose(p, (1, 0, 2)) for p in (proj_pos, proj_vel, proj_acc)]
    blocks = pp.shape[1]
    u, v, a, pp, pv, pa = [pltpu.with_memory_space_constraint(x, pltpu.HBM) for x in (u, v, a, pp, pv, pa)]
    u, half, pst, perm, *edges = call(
        begin_kernel,
        (pairs, u, v, a, pp, pv, pa),
        [PADDED, STATE, PST, jax.ShapeDtypeStruct((blocks, blocks), F32), XA, XB, YE, YE],
        ins=[SMEM] + [HBM] * 6,
        limit=40,
        scratch=(
            PLACES,
            pltpu.VMEM((3, *STATE.shape), F32),
            pltpu.VMEM((3, *pp.shape), F32),
            pltpu.SemaphoreType.DMA((3, CX // STEP)),
            pltpu.SemaphoreType.DMA((3,)),
        ),
    )
    words, rim = call(words_kernel, (masks,), [WORDS, RIM])
    for substep in range(SUB):
        last = substep == SUB - 1
        scale = 0.5 * DT if last else DT
        xa, xb, ya_own, yb_own = edges
        xa, xb = swap(xa, "slab", 0), swap(xb, "slab", 1)
        if last:
            (ours,) = call(pair_kernel, (xa, pst), [PAIR], us=0.1)
            theirs = swap(ours, "split", 0)
            left, right, token = call(turn_kernel, (u,), [SIDE, SIDE, TOKEN])
            (gathered,) = call(state_kernel, (ours, theirs, pst, token), [rows_of(GROUP)], us=0.1)
            inner, token = call(
                functools.partial(late_inner_kernel, scale),
                (u, left, right, half, words, gathered),
                [HALVES, TOKEN],
                us=2.6,
            )
        else:
            inner, left, right, token = call(
                functools.partial(inner_kernel, scale), (u, half, words), [HALVES, SIDE, SIDE, TOKEN], us=3.6
            )
        after = gathered if last else token
        ya, yb = call(corner_kernel, (ya_own, yb_own, xa, xb, pst, after), [YA, YA], us=0.1)
        ya, yb = swap(ya, "split", 0), swap(yb, "split", 1)
        if last:
            gathered = after = share_round(gathered, 0, token)
        edge, token = call(
            functools.partial(edge_kernel, scale),
            (xa, xb, u, left, right, half, words, after),
            [HALVES, TOKEN],
            scratch=[pltpu.VMEM(shape.shape, F32) for shape in (PADDED, SIDE, SIDE)],
            us=3.6,
        )
        if last:
            break
        u, half, pst, *edges = call(
            functools.partial(close_kernel, substep),
            (pairs, u, inner, edge, ya_own, yb_own, xa, ya, yb, rim, pst),
            [PADDED, STATE, PST, XA, XB, YE, YE],
            scalars=1,
            scratch=(PLACES, CROSSING),
            us=3.0,
        )

    gathered = share_round(gathered, 1, token)
    final_u, final_v, token = call(
        last_kernel,
        (u, inner, edge, ya_own, yb_own, ya, yb, rim, gathered),
        [STATE, STATE, TOKEN],
        scratch=(CROSSING,),
        us=1.4,
    )
    for number in range(2, len(ROUNDS)):
        gathered = share_round(gathered, number, token)
    final_pos, final_vel = call(final_kernel, (perm, gathered), [jax.ShapeDtypeStruct(pp.shape, F32)] * 2)
    return (
        final_u,
        final_v,
        jnp.transpose(final_pos, (1, 0, 2)),
        jnp.transpose(final_vel, (1, 0, 2)),
    )


def solution(mesh):
    cells = P(None, "slab", "split", None)
    return jax.shard_map(
        per_device,
        mesh=mesh,
        in_specs=(cells, cells, cells, cells, P(), P(), P(), P(None, None, ("slab", "split"))),
        out_specs=(cells, cells, P(), P()),
        check_vma=False,
    )
```

```python
import functools
import math

import jax
import jax.numpy as jnp
from jax import lax
from jax.experimental import pallas as pl
from jax.experimental.pallas import tpu as pltpu
from jax.sharding import PartitionSpec as P

SUB = 3
SL = 4
SLOTS = 16
CHUNK = 4
STEP = 2
GROUP = 4
ROUNDS = (("slab", 8), ("slab", 4), ("split", 2), ("split", 4), ("slab", 2))

DT = 0.25
STIFF = 0.5
CONTACT = 0.05
WIDTH = 8.0
INV_MASS = 0.5

CX, CY, CZ = 8, 32, 256
LO = 8
F32 = jnp.float32


def bond_offsets():
    listed = []
    for sx in (-2, -1, 0, 1, 2):
        for sy in (-2, -1, 0, 1, 2):
            for sz in (-2, -1, 0, 1, 2):
                if 0 < sx * sx + sy * sy + sz * sz <= 4:
                    listed.append((sx, sy, sz))
    return listed


OFFSETS = bond_offsets()


def as_int32(bits):
    return bits - (1 << 32) if bits >= 1 << 31 else bits


def keep_bits(dim, allowed):
    return as_int32(sum(1 << n for n, e in enumerate(OFFSETS) if allowed(e[dim])))


def keep_word(index, last, dim):
    word = jnp.where(index == 0, keep_bits(dim, lambda e: e >= 0), -1)
    word = jnp.where(index == 1, keep_bits(dim, lambda e: e >= -1), word)
    word = jnp.where(index == last - 1, keep_bits(dim, lambda e: e <= 1), word)
    return jnp.where(index == last, keep_bits(dim, lambda e: e <= 0), word)


def position():
    return lax.axis_index("slab"), lax.axis_index("split")


def lane_sums(parts):
    whole = jnp.concatenate(parts, axis=0)
    high = whole.astype(jnp.bfloat16)
    low = (whole - high.astype(F32)).astype(jnp.bfloat16)
    ones = jnp.ones((256, 128), jnp.bfloat16)
    return jnp.dot(jnp.concatenate([high, low], axis=1), ones, preferred_element_type=F32)


def contact_kernel(substep, pairs, u_ref, pst, surface_out, force_out, xa, places):
    slab, split = position()
    corner = (slab * CX, split * CY)
    share = 0.5 * DT if substep == SUB - 1 else DT
    at_a = jnp.where(lax.rem(slab, 2) == 0, CX, 2)
    pos, ids = [pst[c] for c in range(3)], pst[6].astype(jnp.int32)
    surface_out[...] = jnp.zeros_like(surface_out)
    row = lax.broadcasted_iota(jnp.int32, (CY, 128), 0)
    lane = lax.broadcasted_iota(jnp.int32, (CY, 128), 1)
    place_y = (row + corner[1]).astype(F32)
    live = jnp.int32(0)
    for k in range(SLOTS):
        live += (pairs[substep, 1, k] >= 0).astype(jnp.int32)

    @pl.when(live > 0)
    def _():
        def place(x, carry):
            for c in range(3):
                top = u_ref[c, 1, x + 2, LO : LO + CY, :]
                for z in range(SL):
                    lattice = ((corner[0] + x).astype(F32), place_y, float(CZ - SL + z))[c]
                    at = 128 - SL + z
                    column = jnp.broadcast_to(top[:, at : at + 1], (CY, 128))
                    places[c, x, z * CY : (z + 1) * CY, :] = column + lattice
            return carry

        lax.fori_loop(0, CX, place, 0)

    def slot(k, totals):
        target = jnp.clip(pairs[substep, 0, k], 0, CX - 1)
        chosen = pairs[substep, 1, k]
        hit = ids == chosen
        stiff = jnp.where(chosen >= 0, CONTACT, 0.0)
        q = [jnp.sum(jnp.where(hit, pos[c], 0.0), axis=0, keepdims=True) for c in range(3)]
        r = [places[c, target] - q[c] for c in range(3)]
        squared = r[0] * r[0] + r[1] * r[1] + r[2] * r[2]
        weight = stiff * jnp.exp(squared * (-1.0 / WIDTH))
        pulled = [weight * r[c] for c in range(3)]
        sums = lane_sums(pulled)
        for c in range(3):
            surface = jnp.zeros((CY, 128), F32)
            for z in range(SL):
                at = c * SL * CY + z * CY
                surface = jnp.where(lane == 128 - SL + z, sums[at : at + CY], surface)
            surface_out[c, target] += share * surface
        return tuple(
            totals[c] - jnp.where(hit, jnp.sum(pulled[c], axis=0, keepdims=True), 0.0)
            for c in range(3)
        )

    def some(k, totals):
        for j in range(CHUNK):
            totals = slot(CHUNK * k + j, totals)
        return totals

    none = tuple(jnp.zeros((8, 128), F32) for _ in range(3))
    force = lax.fori_loop(0, (live + CHUNK - 1) // CHUNK, some, none)
    for c in range(3):
        force_out[c] = force[c]
        for h in range(2):
            lanes = slice(128 * h, 128 * h + 128)
            for layer in range(2):
                rows = slice((2 * c + layer) * CY, (2 * c + layer + 1) * CY)
                xa[rows, lanes] = u_ref[c, h, at_a + layer, LO : LO + CY, :]


    xa[6 * CY :, 0:128] = jnp.concatenate([force[0][0:GROUP], force[2][0:GROUP]], axis=0)
    xa[6 * CY :, 128:256] = force[1]


def chip_force(xa, c):
    at, lane = 6 * CY + GROUP * (c // 2), 128 * (c % 2)
    return jnp.concatenate(
        [xa[at : at + GROUP, lane : lane + 128], jnp.zeros((8 - GROUP, 128), F32)], axis=0
    )


def send_edges(u_ref, xb, ya, yb, even_x, even_y):
    at_b = jnp.where(even_x, 2, CX)
    xb[6 * CY :, :] = jnp.zeros((XB.shape[0] - 6 * CY, CZ), F32)
    for c in range(3):
        for h in range(2):
            lanes = slice(128 * h, 128 * h + 128)
            for layer in range(2):
                rows = slice((2 * c + layer) * CY, (2 * c + layer + 1) * CY)
                xb[rows, lanes] = u_ref[c, h, at_b + layer, LO : LO + CY, :]
    for want_even, low, high in ((True, yb, ya), (False, ya, yb)):

        @pl.when(even_y == want_even)
        def _(low=low, high=high):
            for c in range(3):
                for h in range(2):
                    lanes = slice(128 * h, 128 * h + 128)
                    for x in range(CX):
                        for r in range(2):
                            low[c, r, x : x + 1, lanes] = u_ref[c, h, x + 2, LO + r : LO + r + 1, :]
                            high[c, r, x : x + 1, lanes] = u_ref[
                                c, h, x + 2, LO + CY - 2 + r : LO + CY - 1 + r, :
                            ]


def begin_kernel(
    u, v, a, pp, pv, pa, u_out, half_out, pst, perm, xb, ya, yb, cells, blocks_in, sems, block_sems
):
    slab, split = position()
    splits = lax.axis_size("split")
    even_x, even_y = lax.rem(slab, 2) == 0, lax.rem(split, 2) == 0

    copies = []
    for x in range(0, CX, STEP):
        copies.append(
            [
                pltpu.make_async_copy(
                    source.at[:, x : x + STEP], cells.at[k, :, x : x + STEP], sems.at[k, x // STEP]
                )
                for k, source in enumerate((u, v, a))
            ]
        )
    block_copies = [
        pltpu.make_async_copy(source, blocks_in.at[k], block_sems.at[k])
        for k, source in enumerate((pp, pv, pa))
    ]
    for copy in block_copies:
        copy.start()
    for group in copies:
        for copy in group:
            copy.start()

    for copy in block_copies:
        copy.wait()
    pp, pv, pa = blocks_in.at[0], blocks_in.at[1], blocks_in.at[2]
    blocks = pp.shape[1]
    mean_x = jnp.sum(pp[0], axis=1, keepdims=True) * (1.0 / pp.shape[2])
    mean_y = jnp.sum(pp[1], axis=1, keepdims=True) * (1.0 / pp.shape[2])
    group_x = jnp.floor((mean_x + 0.5) * (1.0 / (2 * CX)))
    group_y = jnp.floor((mean_y + 0.5) * (1.0 / (2 * CY)))
    group = jnp.broadcast_to(group_x * (splits // 2) + group_y, (blocks, blocks))
    row = lax.broadcasted_iota(jnp.int32, (blocks, blocks), 0)
    lane = lax.broadcasted_iota(jnp.int32, (blocks, blocks), 1)
    earlier = jnp.where((group == group.T) & (lane < row), 1.0, 0.0)
    rank = jnp.sum(earlier, axis=1, keepdims=True).astype(jnp.int32)
    group = group.astype(jnp.int32)
    mine = (slab // 2) * (splits // 2) + split // 2
    other = group ^ mine
    slot = rank
    for order, (axis, bit) in enumerate(ROUNDS):
        place = bit // 2 * (splits // 2 if axis == "slab" else 1)
        slot = slot + jnp.where((other & place) != 0, GROUP << order, 0)
    perm[...] = jnp.where(slot == lane, 1.0, 0.0)

    pst[...] = jnp.zeros_like(pst)
    pst[6] = jnp.full((8, 128), -5.0, F32)
    for k in range(GROUP):
        chosen = slot == k
        pst[6, k : k + 1, :] = jnp.sum(jnp.where(chosen, row.astype(F32), 0.0), axis=0, keepdims=True)
        for c in range(3):
            pos, vel, acc = [
                jnp.sum(jnp.where(chosen, p[c], 0.0), axis=0, keepdims=True) for p in (pp, pv, pa)
            ]
            half = vel + 0.5 * DT * acc
            pst[3 + c, k : k + 1, :] = half
            pst[c, k : k + 1, :] = pos + DT * half

    for at, waits in zip(range(0, CX, STEP), copies):
        for copy in waits:
            copy.wait()
        for x in range(at, at + STEP):
            for c in range(3):
                half = cells[1, c, x] + 0.5 * DT * cells[2, c, x]
                half_out[c, x] = half
                moved = cells[0, c, x] + DT * half
                for h in range(2):
                    u_out[c, h, x + 2, LO : LO + CY, :] = moved[:, 128 * h : 128 * h + 128]
    send_edges(u_out, xb, ya, yb, even_x, even_y)


def words_kernel(masks, w_out, rim_out):
    slab, split = position()
    slabs, splits = lax.axis_size("slab"), lax.axis_size("split")

    for x in range(CX):
        kx = keep_word(slab * CX + x, slabs * CX - 1, 0)
        y = lax.broadcasted_iota(jnp.int32, (CY, CZ), 0)
        ky = keep_word(split * CY + y, splits * CY - 1, 1)
        kz = keep_word(lax.broadcasted_iota(jnp.int32, (CY, CZ), 1), CZ - 1, 2)
        word = masks[0, x] | (masks[1, x] << 8) | (masks[2, x] << 16) | (masks[3, x] << 24)
        word = word & ky & kz & kx
        w_out[x] = word & keep_word(y, CY - 1, 1)
        for r in range(4):
            y = r if r < 2 else CY - 4 + r
            rim_out[r, x : x + 1, :] = word[y : y + 1, :]


def corner_kernel(ya_own, yb_own, xa, xb, own_force, token, ya, yb):
    slab, split = position()
    even_x, even_y = lax.rem(slab, 2) == 0, lax.rem(split, 2) == 0
    for c in range(3):
        for r in range(2):
            ya[c, r, 0:CX, :] = ya_own[c, r]
            yb[c, r, 0:CX, :] = yb_own[c, r]
        force = own_force[c] + chip_force(xa, c)
        for h in range(2):
            ya[c, 0, CX + 2 : CX + 2 + GROUP, 128 * h : 128 * h + 128] = force[0:GROUP]
    for is_x in (True, False):
        for is_y in (True, False):

            @pl.when((even_x == is_x) & (even_y == is_y))
            def _(is_x=is_x, is_y=is_y):
                for c in range(3):
                    for message, high in ((ya, is_y), (yb, not is_y)):
                        for got, top in ((xa, is_x), (xb, not is_x)):
                            entry, layer = (CX + 1, 0) if top else (CX, 1)
                            for r in range(2):
                                at = (2 * c + layer) * CY + (CY - 2 if high else 0) + r
                                message[c, r, entry : entry + 1, :] = got[at : at + 1, :]


def rolled(u, c, x, at, by):
    lane = lax.broadcasted_iota(jnp.int32, (8, 128), 1)
    turned = [pltpu.roll(u[c, h, x, at, :], by % 128, 1) for h in range(2)]
    wraps = lane < by if by > 0 else lane >= 128 + by
    return [jnp.where(wraps, turned[1 - h], turned[h]) for h in range(2)]


def turn(u, left, right, x, y):
    at = slice(y, y + 8)
    for c in range(3):
        for side, by in ((left, -1), (right, 1)):
            for h, value in enumerate(rolled(u, c, x, at, by)):
                side[c, h, x - 1, at, :] = value


def forces(u, left, right, w, x, y, h):
    own = [u[c, h, x + 2, LO + y : LO + y + 8, :] for c in range(3)]
    less = {(c, e): own[c] - float(e) if e else own[c] for c in range(3) for e in (-2, -1, 0, 1, 2)}
    word = w[x, y : y + 8, 128 * h : 128 * h + 128]
    total = [None] * 3
    for squared_length in (1, 2, 3, 4):
        sums = [None] * 3
        for number, e in enumerate(OFFSETS):
            if sum(k * k for k in e) != squared_length:
                continue
            at = slice(LO + y + e[1], LO + y + e[1] + 8)
            if e[2] == 0:
                near = [u[c, h, x + 2 + e[0], at, :] for c in range(3)]
            elif abs(e[2]) == 2:
                near = [rolled(u, c, x + 2, at, -e[2])[h] for c in range(3)]
            else:
                source = left if e[2] > 0 else right
                near = [source[c, h, x + 1 + e[0], at, :] for c in range(3)]
            d = [near[c] - less[c, e[c]] for c in range(3)]
            q = jnp.maximum(d[0] * d[0] + d[1] * d[1] + d[2] * d[2], 1e-30)
            pull = q * lax.rsqrt(q) - math.sqrt(squared_length)
            pull = jnp.where((word & as_int32(1 << number)) != 0, pull, 0.0)
            for c in range(3):
                if e[c] > 0:
                    sums[c] = pull if sums[c] is None else sums[c] + pull
                elif e[c] < 0:
                    sums[c] = -pull if sums[c] is None else sums[c] - pull
        factor = STIFF / squared_length * (2.0 if squared_length == 4 else 1.0)
        for c in range(3):
            term = factor * sums[c]
            total[c] = term if total[c] is None else total[c] + term
    return total


def advance(scale, u, left, right, w, half, half_out, first, out_first, count):
    def layer(k, carry):
        x = first + k
        for y in range(0, CY, 8):
            for h in range(2):
                at, lanes = slice(y, y + 8), slice(128 * h, 128 * h + 128)
                total = forces(u, left, right, w, x, y, h)
                for c in range(3):
                    half_out[c, out_first + k, at, lanes] = half[c, x, at, lanes] + scale * total[c]
        return carry

    lax.fori_loop(0, count, layer, 0)


def turned_layers(u, left, right):
    def shifted(x, carry):
        for y in range(LO, LO + CY, 8):
            turn(u, left, right, x, y)
        return carry

    lax.fori_loop(2, CX + 2, shifted, 0)


def turn_kernel(u, left, right, token):
    turned_layers(u, left, right)
    token[...] = left[0, 0, 1, LO : LO + 8, :]


def late_inner_kernel(scale, u, left, right, half, w, after, half_out, token):
    advance(scale, u, left, right, w, half, half_out, 2, 0, CX - 4)
    token[...] = half_out[0, 0, 0:8, 0:128]


def inner_kernel(scale, u, half, w, half_out, left, right, token):
    turned_layers(u, left, right)
    advance(scale, u, left, right, w, half, half_out, 2, 0, CX - 4)
    token[...] = half_out[0, 0, 0:8, 0:128]


def edge_kernel(scale, xa, xb, u_own, left_own, right_own, half, w, after, half_out, token, u, left, right):
    slab, split = position()
    even_x = lax.rem(slab, 2) == 0
    to_a = jnp.where(even_x, CX + 2, 0)
    to_b = jnp.where(even_x, 0, CX + 2)
    rows = slice(LO, LO + CY)
    for c in range(3):
        for layer in range(2):
            part = slice((2 * c + layer) * CY, (2 * c + layer + 1) * CY)
            for h in range(2):
                lanes = slice(128 * h, 128 * h + 128)
                u[c, h, to_a + layer, rows, :] = xa[part, lanes]
                u[c, h, to_b + layer, rows, :] = xb[part, lanes]

    def own(x, carry):
        for c in range(3):
            for h in range(2):
                u[c, h, x + 2, rows, :] = u_own[c, h, x + 2, rows, :]
                left[c, h, x + 1, rows, :] = left_own[c, h, x + 1, rows, :]
                right[c, h, x + 1, rows, :] = right_own[c, h, x + 1, rows, :]
        return carry

    lax.fori_loop(0, CX, own, 0)
    for x in (1, CX + 2):
        for y in range(LO, LO + CY, 8):
            turn(u, left, right, x, y)
    advance(scale, u, left, right, w, half, half_out, 0, 0, 2)
    advance(scale, u, left, right, w, half, half_out, CX - 2, 2, 2)
    token[...] = half_out[0, 0, 0:8, 0:128]


def rim_forces(own, halo, rim, side, even_y, crossing):
    sub = lax.broadcasted_iota(jnp.int32, (8, 128), 0)
    lane = lax.broadcasted_iota(jnp.int32, (8, 128), 1)
    sign = -1 if side == 0 else 1
    for h in range(2):
        lanes = slice(128 * h, 128 * h + 128)
        total = [[None] * 3, [None] * 3]
        variants = {}

        def near(c, r, ex, ez):
            key = (c, r, ex, ez)
            if key not in variants:
                if ez:
                    both = [near_at(c, r, ex, k) for k in range(2)]
                    turned = [pltpu.roll(value, -ez % 128, 1) for value in both]
                    wraps = lane < -ez if ez < 0 else lane >= 128 - ez
                    variants[key] = jnp.where(wraps, turned[1 - h], turned[h])
                else:
                    variants[key] = near_at(c, r, ex, h)
            return variants[key]

        def near_at(c, r, ex, k):
            here = halo(c, r, slice(0, 8), k)
            if ex == 0:
                return here
            ends = halo(c, r, slice(8, 16), k)
            if ex > 0:
                return jnp.where(sub == 7, ends[1:2], pltpu.roll(here, 7, 0))
            return jnp.where(sub == 0, ends[0:1], pltpu.roll(here, 1, 0))

        for number, e in enumerate(OFFSETS):
            if e[1] * sign <= 0:
                continue
            squared_length = sum(k * k for k in e)
            for r in range(2):
                if abs(e[1]) <= r:
                    continue
                beyond = abs(e[1]) - r - 1
                mine = 1 - r if side else r
                theirs = beyond if side else 1 - beyond
                d = [near(c, theirs, e[0], e[2]) - (own(c, mine, h) - float(e[c])) for c in range(3)]
                q = jnp.maximum(d[0] * d[0] + d[1] * d[1] + d[2] * d[2], 1e-30)
                pull = (q * lax.rsqrt(q) - math.sqrt(squared_length)) * (STIFF / squared_length)
                word = rim[2 * side + mine, :, lanes]
                pull = jnp.where((word & as_int32(1 << number)) != 0, pull, 0.0)
                for c in range(3):
                    if e[c]:
                        term = float(e[c]) * pull
                        total[mine][c] = term if total[mine][c] is None else total[mine][c] + term
        for mine in range(2):
            for c in range(3):
                value = total[mine][c]
                crossing[2 * side + mine, c, h] = jnp.zeros((8, 128), F32) if value is None else value


def close(scale, inner, edge, surface, ya_own, yb_own, ya, yb, rim, even_y, crossing, store):
    for side in range(2):
        first = even_y == (side == 1)

        def own(c, r, h):
            lanes = slice(128 * h, 128 * h + 128)
            return jnp.where(first, ya_own[c, r, :, lanes], yb_own[c, r, :, lanes])

        def halo(c, r, rows, h):
            lanes = slice(128 * h, 128 * h + 128)
            return jnp.where(first, ya[c, r, rows, lanes], yb[c, r, rows, lanes])

        rim_forces(own, halo, rim, side, even_y, crossing)
    sub = lax.broadcasted_iota(jnp.int32, (8, 128), 0)
    for x in range(CX):
        source, at = (inner, x - 2) if 2 <= x < CX - 2 else (edge, x if x < 2 else x - CX + 4)
        for c in range(3):
            for h in range(2):
                for y in range(0, CY, 8):
                    value = source[c, at, y : y + 8, 128 * h : 128 * h + 128]
                    if h == 1:
                        value = value + surface[c, x, y : y + 8, :]
                    for r in (0, 1) if y == 0 else (2, 3) if y == CY - 8 else ():
                        more = crossing[r, c, h, x : x + 1, :]
                        value = value + scale * jnp.where(sub == (r if r < 2 else r + 4), more, 0.0)
                    store(c, x, y, h, value)


def particle_force(xa, ya, own_force, c):
    theirs = jnp.concatenate([ya[c, 0, CX + 2 : CX + 2 + GROUP, 0:128], jnp.zeros((4, 128), F32)], axis=0)
    return own_force[c] + chip_force(xa, c) + theirs


def close_kernel(
    u, inner, edge, surface, ya_own, yb_own, xa, ya, yb, rim, pst, own_force,
    u_out, half_out, pst_out, xb_out, ya_out, yb_out, crossing,
):
    slab, split = position()
    even_x, even_y = lax.rem(slab, 2) == 0, lax.rem(split, 2) == 0

    def store(c, x, y, h, value):
        half_out[c, x, y : y + 8, 128 * h : 128 * h + 128] = value
        pad = slice(LO + y, LO + y + 8)
        u_out[c, h, x + 2, pad, :] = u[c, h, x + 2, pad, :] + DT * value

    close(DT, inner, edge, surface, ya_own, yb_own, ya, yb, rim, even_y, crossing, store)

    pst_out[6] = pst[6]
    for c in range(3):
        moved = pst[3 + c] + DT * INV_MASS * particle_force(xa, ya, own_force, c)
        pst_out[3 + c] = moved
        pst_out[c] = pst[c] + DT * moved
    send_edges(u_out, xb_out, ya_out, yb_out, even_x, even_y)


def pair_kernel(xa, own_force, out):
    for c in range(3):
        out[c] = own_force[c] + chip_force(xa, c)


def state_kernel(ours, theirs, pst, token, out):
    for c in range(3):
        out[c] = pst[c, 0:GROUP]
        acc = INV_MASS * (ours[c] + theirs[c])
        out[3 + c] = (pst[3 + c] + 0.5 * DT * acc)[0:GROUP]


def merge_kernel(ours, theirs, token, out):
    count = ours.shape[1]
    out[:, 0:count] = ours[...]
    out[:, count : 2 * count] = theirs[...]


def last_kernel(u, inner, edge, surface, ya_own, yb_own, ya, yb, rim, after, u_out, v_out, token, crossing):
    slab, split = position()

    def store(c, x, y, h, value):
        lanes = slice(128 * h, 128 * h + 128)
        v_out[c, x, y : y + 8, lanes] = value
        u_out[c, x, y : y + 8, lanes] = u[c, h, x + 2, LO + y : LO + y + 8, :]

    even_y = lax.rem(split, 2) == 0
    close(0.5 * DT, inner, edge, surface, ya_own, yb_own, ya, yb, rim, even_y, crossing, store)
    token[...] = crossing[0, 0, 0]


def final_kernel(perm, gathered, pos_out, vel_out):
    for c in range(3):
        for at, out in ((c, pos_out), (3 + c, vel_out)):
            out[c] = jnp.dot(
                perm[...],
                gathered[at],
                precision=lax.Precision.HIGHEST,
                preferred_element_type=F32,
            )


VMEM = pl.BlockSpec(memory_space=pltpu.VMEM)
SMEM = pl.BlockSpec(memory_space=pltpu.SMEM)
HBM = pl.BlockSpec(memory_space=pltpu.HBM)
STATE = jax.ShapeDtypeStruct((3, CX, CY, CZ), F32)
PADDED = jax.ShapeDtypeStruct((3, 2, CX + 4, CY + 16, 128), F32)
SIDE = jax.ShapeDtypeStruct((3, 2, CX + 2, CY + 16, 128), F32)
WORDS = jax.ShapeDtypeStruct((CX, CY, CZ), jnp.int32)
PST = jax.ShapeDtypeStruct((7, 8, 128), F32)
SURFACE = jax.ShapeDtypeStruct((3, CX, CY, 128), F32)
XA = jax.ShapeDtypeStruct((6 * CY + 8, CZ), F32)
XB = jax.ShapeDtypeStruct((6 * CY + 16, CZ), F32)
YE = jax.ShapeDtypeStruct((3, 2, CX, CZ), F32)
YA = jax.ShapeDtypeStruct((3, 2, 16, CZ), F32)
PAIR = jax.ShapeDtypeStruct((3, 8, 128), F32)
TOKEN = jax.ShapeDtypeStruct((8, 128), F32)
HALVES = jax.ShapeDtypeStruct((3, 4, CY, CZ), F32)
RIM = jax.ShapeDtypeStruct((4, CX, CZ), jnp.int32)
CROSSING = pltpu.VMEM((4, 3, 2, CX, 128), F32)
PLACES = pltpu.VMEM((3, CX, SL * CY, 128), F32)


def call(kernel, inputs, outputs, scalars=0, scratch=(), ins=None, limit=40, us=1.0):
    return pl.pallas_call(
        kernel,
        out_shape=outputs,
        in_specs=ins or [SMEM] * scalars + [VMEM] * (len(inputs) - scalars),
        out_specs=[VMEM] * len(outputs),
        scratch_shapes=list(scratch),
        compiler_params=pltpu.CompilerParams(vmem_limit_bytes=limit << 20),
        cost_estimate=pl.CostEstimate(flops=0, transcendentals=0, bytes_accessed=int(us * 3.0e6)),
    )(*inputs)


def swap(value, axis, offset):
    count = lax.axis_size(axis)
    pairs = []
    for i in range(offset, count, 2):
        pairs += [(i, (i + 1) % count), ((i + 1) % count, i)]
    return lax.ppermute(value, axis, pairs)


def rows_of(count):
    return jax.ShapeDtypeStruct((6, count, 128), F32)


def share_round(gathered, number, token):
    axis, bit = ROUNDS[number]
    theirs = lax.ppermute(gathered, axis, [(i, i ^ bit) for i in range(lax.axis_size(axis))])
    (merged,) = call(merge_kernel, (gathered, theirs, token), [rows_of(2 * gathered.shape[1])], us=0.1)
    return merged


def per_device(u, v, a, masks, proj_pos, proj_vel, proj_acc, pairs):
    pp, pv, pa = [jnp.transpose(p, (1, 0, 2)) for p in (proj_pos, proj_vel, proj_acc)]
    blocks = pp.shape[1]
    u, v, a, pp, pv, pa = [pltpu.with_memory_space_constraint(x, pltpu.HBM) for x in (u, v, a, pp, pv, pa)]
    u, half, pst, perm, *edges = call(
        begin_kernel,
        (u, v, a, pp, pv, pa),
        [PADDED, STATE, PST, jax.ShapeDtypeStruct((blocks, blocks), F32), XB, YE, YE],
        ins=[HBM] * 6,
        scratch=(
            pltpu.VMEM((3, *STATE.shape), F32),
            pltpu.VMEM((3, *pp.shape), F32),
            pltpu.SemaphoreType.DMA((3, CX // STEP)),
            pltpu.SemaphoreType.DMA((3,)),
        ),
    )
    words, rim = call(words_kernel, (masks,), [WORDS, RIM])
    for substep in range(SUB):
        last = substep == SUB - 1
        scale = 0.5 * DT if last else DT
        xb, ya_own, yb_own = edges
        xb = swap(xb, "slab", 1)
        surface, own_force, xa = call(
            functools.partial(contact_kernel, substep),
            (pairs, u, pst),
            [SURFACE, PAIR, XA],
            scalars=1,
            scratch=(PLACES,),
            us=1.5,
        )
        xa = swap(xa, "slab", 0)
        if last:
            (ours,) = call(pair_kernel, (xa, own_force), [PAIR], us=0.1)
            theirs = swap(ours, "split", 0)
            left, right, token = call(turn_kernel, (u,), [SIDE, SIDE, TOKEN])
            (gathered,) = call(state_kernel, (ours, theirs, pst, token), [rows_of(GROUP)], us=0.1)
            inner, token = call(
                functools.partial(late_inner_kernel, scale),
                (u, left, right, half, words, gathered),
                [HALVES, TOKEN],
                us=2.6,
            )
        else:
            inner, left, right, token = call(
                functools.partial(inner_kernel, scale), (u, half, words), [HALVES, SIDE, SIDE, TOKEN], us=3.6
            )
        after = gathered if last else token
        ya, yb = call(corner_kernel, (ya_own, yb_own, xa, xb, own_force, after), [YA, YA], us=0.1)
        ya, yb = swap(ya, "split", 0), swap(yb, "split", 1)
        if last:
            gathered = after = share_round(gathered, 0, token)
        edge, token = call(
            functools.partial(edge_kernel, scale),
            (xa, xb, u, left, right, half, words, after),
            [HALVES, TOKEN],
            scratch=[pltpu.VMEM(shape.shape, F32) for shape in (PADDED, SIDE, SIDE)],
            us=3.6,
        )
        if last:
            break
        u, half, pst, *edges = call(
            close_kernel,
            (u, inner, edge, surface, ya_own, yb_own, xa, ya, yb, rim, pst, own_force),
            [PADDED, STATE, PST, XB, YE, YE],
            scratch=(CROSSING,),
            us=1.3,
        )

    gathered = share_round(gathered, 1, token)
    final_u, final_v, token = call(
        last_kernel,
        (u, inner, edge, surface, ya_own, yb_own, ya, yb, rim, gathered),
        [STATE, STATE, TOKEN],
        scratch=(CROSSING,),
        us=1.4,
    )
    for number in range(2, len(ROUNDS)):
        gathered = share_round(gathered, number, token)
    final_pos, final_vel = call(final_kernel, (perm, gathered), [jax.ShapeDtypeStruct(pp.shape, F32)] * 2)
    return (
        final_u,
        final_v,
        jnp.transpose(final_pos, (1, 0, 2)),
        jnp.transpose(final_vel, (1, 0, 2)),
    )


def solution(mesh):
    cells = P(None, "slab", "split", None)
    return jax.shard_map(
        per_device,
        mesh=mesh,
        in_specs=(cells, cells, cells, cells, P(), P(), P(), P(None, None, ("slab", "split"))),
        out_specs=(cells, cells, P(), P()),
        check_vma=False,
    )
```

```python
import functools
import math

import jax
import jax.numpy as jnp
from jax import lax
from jax.experimental import pallas as pl
from jax.experimental.pallas import tpu as pltpu
from jax.sharding import PartitionSpec as P

SUB = 3
SL = 4
SLOTS = 16
CHUNK = 4
STEP = 2
GROUP = 4
ROUNDS = (
    (("slab", 8), ("slab", 4), ("split", 2), ("split", 4), ("slab", 2)),
    (("slab", 8), ("split", 2), ("slab", 4), ("slab", 2), ("split", 4)),
)

DT = 0.25
STIFF = 0.5
CONTACT = 0.05
WIDTH = 8.0
INV_MASS = 0.5

CX, CY, CZ = 8, 32, 256
LO = 8
F32 = jnp.float32


def bond_offsets():
    listed = []
    for sx in (-2, -1, 0, 1, 2):
        for sy in (-2, -1, 0, 1, 2):
            for sz in (-2, -1, 0, 1, 2):
                if 0 < sx * sx + sy * sy + sz * sz <= 4:
                    listed.append((sx, sy, sz))
    return listed


OFFSETS = bond_offsets()


def as_int32(bits):
    return bits - (1 << 32) if bits >= 1 << 31 else bits


def keep_bits(dim, allowed):
    return as_int32(sum(1 << n for n, e in enumerate(OFFSETS) if allowed(e[dim])))


def keep_word(index, last, dim):
    word = jnp.where(index == 0, keep_bits(dim, lambda e: e >= 0), -1)
    word = jnp.where(index == 1, keep_bits(dim, lambda e: e >= -1), word)
    word = jnp.where(index == last - 1, keep_bits(dim, lambda e: e <= 1), word)
    return jnp.where(index == last, keep_bits(dim, lambda e: e <= 0), word)


def position():
    return lax.axis_index("slab"), lax.axis_index("split")


def lane_sums(parts):
    whole = jnp.concatenate(parts, axis=0)
    high = whole.astype(jnp.bfloat16)
    low = (whole - high.astype(F32)).astype(jnp.bfloat16)
    ones = jnp.ones((256, 128), jnp.bfloat16)
    return jnp.dot(jnp.concatenate([high, low], axis=1), ones, preferred_element_type=F32)


def contact_kernel(substep, pairs, u_ref, pst, surface_out, force_out, xa, places):
    slab, split = position()
    corner = (slab * CX, split * CY)
    share = 0.5 * DT if substep == SUB - 1 else DT
    at_a = jnp.where(lax.rem(slab, 2) == 0, CX, 2)
    pos, ids = [pst[c] for c in range(3)], pst[6].astype(jnp.int32)
    surface_out[...] = jnp.zeros_like(surface_out)
    row = lax.broadcasted_iota(jnp.int32, (CY, 128), 0)
    lane = lax.broadcasted_iota(jnp.int32, (CY, 128), 1)
    place_y = (row + corner[1]).astype(F32)
    live = jnp.int32(0)
    for k in range(SLOTS):
        live += (pairs[substep, 1, k] >= 0).astype(jnp.int32)

    @pl.when(live > 0)
    def _():
        def place(x, carry):
            for c in range(3):
                top = u_ref[c, 1, x + 2, LO : LO + CY, :]
                for z in range(SL):
                    lattice = ((corner[0] + x).astype(F32), place_y, float(CZ - SL + z))[c]
                    at = 128 - SL + z
                    column = jnp.broadcast_to(top[:, at : at + 1], (CY, 128))
                    places[c, x, z * CY : (z + 1) * CY, :] = column + lattice
            return carry

        lax.fori_loop(0, CX, place, 0)

    def slot(k, totals):
        target = jnp.clip(pairs[substep, 0, k], 0, CX - 1)
        chosen = pairs[substep, 1, k]
        hit = ids == chosen
        stiff = jnp.where(chosen >= 0, CONTACT, 0.0)
        q = [jnp.sum(jnp.where(hit, pos[c], 0.0), axis=0, keepdims=True) for c in range(3)]
        r = [places[c, target] - q[c] for c in range(3)]
        squared = r[0] * r[0] + r[1] * r[1] + r[2] * r[2]
        weight = stiff * jnp.exp(squared * (-1.0 / WIDTH))
        pulled = [weight * r[c] for c in range(3)]
        sums = lane_sums(pulled)
        for c in range(3):
            surface = jnp.zeros((CY, 128), F32)
            for z in range(SL):
                at = c * SL * CY + z * CY
                surface = jnp.where(lane == 128 - SL + z, sums[at : at + CY], surface)
            surface_out[c, target] += share * surface
        return tuple(
            totals[c] - jnp.where(hit, jnp.sum(pulled[c], axis=0, keepdims=True), 0.0)
            for c in range(3)
        )

    def some(k, totals):
        for j in range(CHUNK):
            totals = slot(CHUNK * k + j, totals)
        return totals

    none = tuple(jnp.zeros((8, 128), F32) for _ in range(3))
    force = lax.fori_loop(0, (live + CHUNK - 1) // CHUNK, some, none)
    for c in range(3):
        force_out[c] = force[c]
        for h in range(2):
            lanes = slice(128 * h, 128 * h + 128)
            for layer in range(2):
                rows = slice((2 * c + layer) * CY, (2 * c + layer + 1) * CY)
                xa[rows, lanes] = u_ref[c, h, at_a + layer, LO : LO + CY, :]


    xa[6 * CY :, 0:128] = jnp.concatenate([force[0][0:GROUP], force[2][0:GROUP]], axis=0)
    xa[6 * CY :, 128:256] = force[1]


def chip_force(xa, c):
    at, lane = 6 * CY + GROUP * (c // 2), 128 * (c % 2)
    return jnp.concatenate(
        [xa[at : at + GROUP, lane : lane + 128], jnp.zeros((8 - GROUP, 128), F32)], axis=0
    )


def send_edges(u_ref, xb, ya, yb, even_x, even_y):
    at_b = jnp.where(even_x, 2, CX)
    xb[6 * CY :, :] = jnp.zeros((XB.shape[0] - 6 * CY, CZ), F32)
    for c in range(3):
        for h in range(2):
            lanes = slice(128 * h, 128 * h + 128)
            for layer in range(2):
                rows = slice((2 * c + layer) * CY, (2 * c + layer + 1) * CY)
                xb[rows, lanes] = u_ref[c, h, at_b + layer, LO : LO + CY, :]
    for want_even, low, high in ((True, yb, ya), (False, ya, yb)):

        @pl.when(even_y == want_even)
        def _(low=low, high=high):
            for c in range(3):
                for h in range(2):
                    lanes = slice(128 * h, 128 * h + 128)
                    for x in range(CX):
                        for r in range(2):
                            low[c, r, x : x + 1, lanes] = u_ref[c, h, x + 2, LO + r : LO + r + 1, :]
                            high[c, r, x : x + 1, lanes] = u_ref[
                                c, h, x + 2, LO + CY - 2 + r : LO + CY - 1 + r, :
                            ]


def begin_kernel(
    u, v, a, pp, pv, pa, u_out, half_out, pst, perm, xb, ya, yb, cells, blocks_in, sems, block_sems
):
    slab, split = position()
    splits = lax.axis_size("split")
    even_x, even_y = lax.rem(slab, 2) == 0, lax.rem(split, 2) == 0

    copies = []
    for x in range(0, CX, STEP):
        copies.append(
            [
                pltpu.make_async_copy(
                    source.at[:, x : x + STEP], cells.at[k, :, x : x + STEP], sems.at[k, x // STEP]
                )
                for k, source in enumerate((u, v, a))
            ]
        )
    block_copies = [
        pltpu.make_async_copy(source, blocks_in.at[k], block_sems.at[k])
        for k, source in enumerate((pp, pv, pa))
    ]
    for copy in block_copies:
        copy.start()
    for group in copies:
        for copy in group:
            copy.start()

    for copy in block_copies:
        copy.wait()
    pp, pv, pa = blocks_in.at[0], blocks_in.at[1], blocks_in.at[2]
    blocks = pp.shape[1]
    mean_x = jnp.sum(pp[0], axis=1, keepdims=True) * (1.0 / pp.shape[2])
    mean_y = jnp.sum(pp[1], axis=1, keepdims=True) * (1.0 / pp.shape[2])
    group_x = jnp.floor((mean_x + 0.5) * (1.0 / (2 * CX)))
    group_y = jnp.floor((mean_y + 0.5) * (1.0 / (2 * CY)))
    group = jnp.broadcast_to(group_x * (splits // 2) + group_y, (blocks, blocks))
    row = lax.broadcasted_iota(jnp.int32, (blocks, blocks), 0)
    lane = lax.broadcasted_iota(jnp.int32, (blocks, blocks), 1)
    earlier = jnp.where((group == group.T) & (lane < row), 1.0, 0.0)
    rank = jnp.sum(earlier, axis=1, keepdims=True).astype(jnp.int32)
    group = group.astype(jnp.int32)
    mine = (slab // 2) * (splits // 2) + split // 2
    other = group ^ mine
    slot = rank
    for order, ways in enumerate(zip(*ROUNDS)):
        even, odd = [bit // 2 * (splits // 2 if axis == "slab" else 1) for axis, bit in ways]
        slot = slot + jnp.where((other & jnp.where(even_x, even, odd)) != 0, GROUP << order, 0)
    perm[...] = jnp.where(slot == lane, 1.0, 0.0)

    pst[...] = jnp.zeros_like(pst)
    pst[6] = jnp.full((8, 128), -5.0, F32)
    for k in range(GROUP):
        chosen = slot == k
        pst[6, k : k + 1, :] = jnp.sum(jnp.where(chosen, row.astype(F32), 0.0), axis=0, keepdims=True)
        for c in range(3):
            pos, vel, acc = [
                jnp.sum(jnp.where(chosen, p[c], 0.0), axis=0, keepdims=True) for p in (pp, pv, pa)
            ]
            half = vel + 0.5 * DT * acc
            pst[3 + c, k : k + 1, :] = half
            pst[c, k : k + 1, :] = pos + DT * half

    for at, waits in zip(range(0, CX, STEP), copies):
        for copy in waits:
            copy.wait()
        for x in range(at, at + STEP):
            for c in range(3):
                half = cells[1, c, x] + 0.5 * DT * cells[2, c, x]
                half_out[c, x] = half
                moved = cells[0, c, x] + DT * half
                for h in range(2):
                    u_out[c, h, x + 2, LO : LO + CY, :] = moved[:, 128 * h : 128 * h + 128]
    send_edges(u_out, xb, ya, yb, even_x, even_y)


def words_kernel(masks, w_out, rim_out):
    slab, split = position()
    slabs, splits = lax.axis_size("slab"), lax.axis_size("split")

    for x in range(CX):
        kx = keep_word(slab * CX + x, slabs * CX - 1, 0)
        y = lax.broadcasted_iota(jnp.int32, (CY, CZ), 0)
        ky = keep_word(split * CY + y, splits * CY - 1, 1)
        kz = keep_word(lax.broadcasted_iota(jnp.int32, (CY, CZ), 1), CZ - 1, 2)
        word = masks[0, x] | (masks[1, x] << 8) | (masks[2, x] << 16) | (masks[3, x] << 24)
        word = word & ky & kz & kx
        w_out[x] = word & keep_word(y, CY - 1, 1)
        for r in range(4):
            y = r if r < 2 else CY - 4 + r
            rim_out[r, x : x + 1, :] = word[y : y + 1, :]


def corner_kernel(ya_own, yb_own, xa, xb, own_force, token, ya, yb):
    slab, split = position()
    even_x, even_y = lax.rem(slab, 2) == 0, lax.rem(split, 2) == 0
    for c in range(3):
        for r in range(2):
            ya[c, r, 0:CX, :] = ya_own[c, r]
            yb[c, r, 0:CX, :] = yb_own[c, r]
        force = own_force[c] + chip_force(xa, c)
        for h in range(2):
            ya[c, 0, CX + 2 : CX + 2 + GROUP, 128 * h : 128 * h + 128] = force[0:GROUP]
    for is_x in (True, False):
        for is_y in (True, False):

            @pl.when((even_x == is_x) & (even_y == is_y))
            def _(is_x=is_x, is_y=is_y):
                for c in range(3):
                    for message, high in ((ya, is_y), (yb, not is_y)):
                        for got, top in ((xa, is_x), (xb, not is_x)):
                            entry, layer = (CX + 1, 0) if top else (CX, 1)
                            for r in range(2):
                                at = (2 * c + layer) * CY + (CY - 2 if high else 0) + r
                                message[c, r, entry : entry + 1, :] = got[at : at + 1, :]


def rolled(u, c, x, at, by):
    lane = lax.broadcasted_iota(jnp.int32, (8, 128), 1)
    turned = [pltpu.roll(u[c, h, x, at, :], by % 128, 1) for h in range(2)]
    wraps = lane < by if by > 0 else lane >= 128 + by
    return [jnp.where(wraps, turned[1 - h], turned[h]) for h in range(2)]


def turn(u, left, right, x, y):
    at = slice(y, y + 8)
    for c in range(3):
        for side, by in ((left, -1), (right, 1)):
            for h, value in enumerate(rolled(u, c, x, at, by)):
                side[c, h, x - 1, at, :] = value


def forces(u, left, right, w, x, y, h):
    own = [u[c, h, x + 2, LO + y : LO + y + 8, :] for c in range(3)]
    less = {(c, e): own[c] - float(e) if e else own[c] for c in range(3) for e in (-2, -1, 0, 1, 2)}
    word = w[x, y : y + 8, 128 * h : 128 * h + 128]
    total = [None] * 3
    for squared_length in (1, 2, 3, 4):
        sums = [None] * 3
        for number, e in enumerate(OFFSETS):
            if sum(k * k for k in e) != squared_length:
                continue
            at = slice(LO + y + e[1], LO + y + e[1] + 8)
            if e[2] == 0:
                near = [u[c, h, x + 2 + e[0], at, :] for c in range(3)]
            elif abs(e[2]) == 2:
                near = [rolled(u, c, x + 2, at, -e[2])[h] for c in range(3)]
            else:
                source = left if e[2] > 0 else right
                near = [source[c, h, x + 1 + e[0], at, :] for c in range(3)]
            d = [near[c] - less[c, e[c]] for c in range(3)]
            q = jnp.maximum(d[0] * d[0] + d[1] * d[1] + d[2] * d[2], 1e-30)
            pull = q * lax.rsqrt(q) - math.sqrt(squared_length)
            pull = jnp.where((word & as_int32(1 << number)) != 0, pull, 0.0)
            for c in range(3):
                if e[c] > 0:
                    sums[c] = pull if sums[c] is None else sums[c] + pull
                elif e[c] < 0:
                    sums[c] = -pull if sums[c] is None else sums[c] - pull
        factor = STIFF / squared_length * (2.0 if squared_length == 4 else 1.0)
        for c in range(3):
            term = factor * sums[c]
            total[c] = term if total[c] is None else total[c] + term
    return total


def advance(scale, u, left, right, w, half, half_out, first, out_first, count):
    def layer(k, carry):
        x = first + k
        for y in range(0, CY, 8):
            for h in range(2):
                at, lanes = slice(y, y + 8), slice(128 * h, 128 * h + 128)
                total = forces(u, left, right, w, x, y, h)
                for c in range(3):
                    half_out[c, out_first + k, at, lanes] = half[c, x, at, lanes] + scale * total[c]
        return carry

    lax.fori_loop(0, count, layer, 0)


def turned_layers(u, left, right):
    def shifted(x, carry):
        for y in range(LO, LO + CY, 8):
            turn(u, left, right, x, y)
        return carry

    lax.fori_loop(2, CX + 2, shifted, 0)


def turn_kernel(u, left, right, token):
    turned_layers(u, left, right)
    token[...] = left[0, 0, 1, LO : LO + 8, :]


def late_inner_kernel(scale, u, left, right, half, w, after, half_out, token):
    advance(scale, u, left, right, w, half, half_out, 2, 0, CX - 4)
    token[...] = half_out[0, 0, 0:8, 0:128]


def inner_kernel(scale, u, half, w, half_out, left, right, token):
    turned_layers(u, left, right)
    advance(scale, u, left, right, w, half, half_out, 2, 0, CX - 4)
    token[...] = half_out[0, 0, 0:8, 0:128]


def edge_kernel(scale, xa, xb, u_own, left_own, right_own, half, w, after, half_out, token, u, left, right):
    slab, split = position()
    even_x = lax.rem(slab, 2) == 0
    to_a = jnp.where(even_x, CX + 2, 0)
    to_b = jnp.where(even_x, 0, CX + 2)
    rows = slice(LO, LO + CY)
    for c in range(3):
        for layer in range(2):
            part = slice((2 * c + layer) * CY, (2 * c + layer + 1) * CY)
            for h in range(2):
                lanes = slice(128 * h, 128 * h + 128)
                u[c, h, to_a + layer, rows, :] = xa[part, lanes]
                u[c, h, to_b + layer, rows, :] = xb[part, lanes]

    def own(x, carry):
        for c in range(3):
            for h in range(2):
                u[c, h, x + 2, rows, :] = u_own[c, h, x + 2, rows, :]
        return carry

    def sides(k, carry):
        x = jnp.where(k < 3, k, k + CX - 6)
        for c in range(3):
            for h in range(2):
                left[c, h, x + 1, rows, :] = left_own[c, h, x + 1, rows, :]
                right[c, h, x + 1, rows, :] = right_own[c, h, x + 1, rows, :]
        return carry

    lax.fori_loop(0, CX, own, 0)
    lax.fori_loop(0, 6, sides, 0)
    for x in (1, CX + 2):
        for y in range(LO, LO + CY, 8):
            turn(u, left, right, x, y)
    advance(scale, u, left, right, w, half, half_out, 0, 0, 2)
    advance(scale, u, left, right, w, half, half_out, CX - 2, 2, 2)
    token[...] = half_out[0, 0, 0:8, 0:128]


def rim_forces(own, halo, rim, side, even_y, crossing):
    sub = lax.broadcasted_iota(jnp.int32, (8, 128), 0)
    lane = lax.broadcasted_iota(jnp.int32, (8, 128), 1)
    sign = -1 if side == 0 else 1
    for h in range(2):
        lanes = slice(128 * h, 128 * h + 128)
        total = [[None] * 3, [None] * 3]
        variants = {}

        def near(c, r, ex, ez):
            key = (c, r, ex, ez)
            if key not in variants:
                if ez:
                    both = [near_at(c, r, ex, k) for k in range(2)]
                    turned = [pltpu.roll(value, -ez % 128, 1) for value in both]
                    wraps = lane < -ez if ez < 0 else lane >= 128 - ez
                    variants[key] = jnp.where(wraps, turned[1 - h], turned[h])
                else:
                    variants[key] = near_at(c, r, ex, h)
            return variants[key]

        def near_at(c, r, ex, k):
            here = halo(c, r, slice(0, 8), k)
            if ex == 0:
                return here
            ends = halo(c, r, slice(8, 16), k)
            if ex > 0:
                return jnp.where(sub == 7, ends[1:2], pltpu.roll(here, 7, 0))
            return jnp.where(sub == 0, ends[0:1], pltpu.roll(here, 1, 0))

        for number, e in enumerate(OFFSETS):
            if e[1] * sign <= 0:
                continue
            squared_length = sum(k * k for k in e)
            for r in range(2):
                if abs(e[1]) <= r:
                    continue
                beyond = abs(e[1]) - r - 1
                mine = 1 - r if side else r
                theirs = beyond if side else 1 - beyond
                d = [near(c, theirs, e[0], e[2]) - (own(c, mine, h) - float(e[c])) for c in range(3)]
                q = jnp.maximum(d[0] * d[0] + d[1] * d[1] + d[2] * d[2], 1e-30)
                pull = (q * lax.rsqrt(q) - math.sqrt(squared_length)) * (STIFF / squared_length)
                word = rim[2 * side + mine, :, lanes]
                pull = jnp.where((word & as_int32(1 << number)) != 0, pull, 0.0)
                for c in range(3):
                    if e[c]:
                        term = float(e[c]) * pull
                        total[mine][c] = term if total[mine][c] is None else total[mine][c] + term
        for mine in range(2):
            for c in range(3):
                value = total[mine][c]
                crossing[2 * side + mine, c, h] = jnp.zeros((8, 128), F32) if value is None else value


def close(scale, inner, edge, surface, ya_own, yb_own, ya, yb, rim, even_y, crossing, store):
    for side in range(2):
        first = even_y == (side == 1)

        def own(c, r, h):
            lanes = slice(128 * h, 128 * h + 128)
            return jnp.where(first, ya_own[c, r, :, lanes], yb_own[c, r, :, lanes])

        def halo(c, r, rows, h):
            lanes = slice(128 * h, 128 * h + 128)
            return jnp.where(first, ya[c, r, rows, lanes], yb[c, r, rows, lanes])

        rim_forces(own, halo, rim, side, even_y, crossing)
    sub = lax.broadcasted_iota(jnp.int32, (8, 128), 0)
    for x in range(CX):
        source, at = (inner, x - 2) if 2 <= x < CX - 2 else (edge, x if x < 2 else x - CX + 4)
        for c in range(3):
            for h in range(2):
                for y in range(0, CY, 8):
                    value = source[c, at, y : y + 8, 128 * h : 128 * h + 128]
                    if h == 1:
                        value = value + surface[c, x, y : y + 8, :]
                    for r in (0, 1) if y == 0 else (2, 3) if y == CY - 8 else ():
                        more = crossing[r, c, h, x : x + 1, :]
                        value = value + scale * jnp.where(sub == (r if r < 2 else r + 4), more, 0.0)
                    store(c, x, y, h, value)


def particle_force(xa, ya, own_force, c):
    theirs = jnp.concatenate([ya[c, 0, CX + 2 : CX + 2 + GROUP, 0:128], jnp.zeros((4, 128), F32)], axis=0)
    return own_force[c] + chip_force(xa, c) + theirs


def close_kernel(
    u, inner, edge, surface, ya_own, yb_own, xa, ya, yb, rim, pst, own_force,
    u_out, half_out, pst_out, xb_out, ya_out, yb_out, crossing,
):
    slab, split = position()
    even_x, even_y = lax.rem(slab, 2) == 0, lax.rem(split, 2) == 0

    def store(c, x, y, h, value):
        half_out[c, x, y : y + 8, 128 * h : 128 * h + 128] = value
        pad = slice(LO + y, LO + y + 8)
        u_out[c, h, x + 2, pad, :] = u[c, h, x + 2, pad, :] + DT * value

    close(DT, inner, edge, surface, ya_own, yb_own, ya, yb, rim, even_y, crossing, store)

    pst_out[6] = pst[6]
    for c in range(3):
        moved = pst[3 + c] + DT * INV_MASS * particle_force(xa, ya, own_force, c)
        pst_out[3 + c] = moved
        pst_out[c] = pst[c] + DT * moved
    send_edges(u_out, xb_out, ya_out, yb_out, even_x, even_y)


def pair_kernel(xa, own_force, out):
    for c in range(3):
        out[c] = own_force[c] + chip_force(xa, c)


def state_kernel(ours, theirs, pst, token, out):
    for c in range(3):
        out[c] = pst[c, 0:GROUP]
        acc = INV_MASS * (ours[c] + theirs[c])
        out[3 + c] = (pst[3 + c] + 0.5 * DT * acc)[0:GROUP]


def merge_kernel(ours, theirs, token, out):
    count = ours.shape[1]
    out[:, 0:count] = ours[...]
    out[:, count : 2 * count] = theirs[...]


def last_kernel(u, inner, edge, surface, ya_own, yb_own, ya, yb, rim, after, u_out, v_out, token, crossing):
    slab, split = position()

    def store(c, x, y, h, value):
        lanes = slice(128 * h, 128 * h + 128)
        v_out[c, x, y : y + 8, lanes] = value
        u_out[c, x, y : y + 8, lanes] = u[c, h, x + 2, LO + y : LO + y + 8, :]

    even_y = lax.rem(split, 2) == 0
    close(0.5 * DT, inner, edge, surface, ya_own, yb_own, ya, yb, rim, even_y, crossing, store)
    token[...] = crossing[0, 0, 0]


def final_kernel(perm, gathered, pos_out, vel_out):
    for c in range(3):
        for at, out in ((c, pos_out), (3 + c, vel_out)):
            out[c] = jnp.dot(
                perm[...],
                gathered[at],
                precision=lax.Precision.HIGHEST,
                preferred_element_type=F32,
            )


VMEM = pl.BlockSpec(memory_space=pltpu.VMEM)
SMEM = pl.BlockSpec(memory_space=pltpu.SMEM)
HBM = pl.BlockSpec(memory_space=pltpu.HBM)
STATE = jax.ShapeDtypeStruct((3, CX, CY, CZ), F32)
PADDED = jax.ShapeDtypeStruct((3, 2, CX + 4, CY + 16, 128), F32)
SIDE = jax.ShapeDtypeStruct((3, 2, CX + 2, CY + 16, 128), F32)
WORDS = jax.ShapeDtypeStruct((CX, CY, CZ), jnp.int32)
PST = jax.ShapeDtypeStruct((7, 8, 128), F32)
SURFACE = jax.ShapeDtypeStruct((3, CX, CY, 128), F32)
XA = jax.ShapeDtypeStruct((6 * CY + 8, CZ), F32)
XB = jax.ShapeDtypeStruct((6 * CY + 16, CZ), F32)
YE = jax.ShapeDtypeStruct((3, 2, CX, CZ), F32)
YA = jax.ShapeDtypeStruct((3, 2, 16, CZ), F32)
PAIR = jax.ShapeDtypeStruct((3, 8, 128), F32)
TOKEN = jax.ShapeDtypeStruct((8, 128), F32)
HALVES = jax.ShapeDtypeStruct((3, 4, CY, CZ), F32)
RIM = jax.ShapeDtypeStruct((4, CX, CZ), jnp.int32)
CROSSING = pltpu.VMEM((4, 3, 2, CX, 128), F32)
PLACES = pltpu.VMEM((3, CX, SL * CY, 128), F32)


def call(kernel, inputs, outputs, scalars=0, scratch=(), ins=None, limit=40, us=1.0):
    return pl.pallas_call(
        kernel,
        out_shape=outputs,
        in_specs=ins or [SMEM] * scalars + [VMEM] * (len(inputs) - scalars),
        out_specs=[VMEM] * len(outputs),
        scratch_shapes=list(scratch),
        compiler_params=pltpu.CompilerParams(vmem_limit_bytes=limit << 20),
        cost_estimate=pl.CostEstimate(flops=0, transcendentals=0, bytes_accessed=int(us * 3.0e6)),
    )(*inputs)


def swap(value, axis, offset):
    count = lax.axis_size(axis)
    pairs = []
    for i in range(offset, count, 2):
        pairs += [(i, (i + 1) % count), ((i + 1) % count, i)]
    return lax.ppermute(value, axis, pairs)


def rows_of(count):
    return jax.ShapeDtypeStruct((6, count, 128), F32)


def share_round(gathered, number, token):
    slabs, splits = lax.axis_size("slab"), lax.axis_size("split")
    pairs = []
    for i in range(slabs):
        axis, bit = ROUNDS[i % 2][number]
        other, across = (i ^ bit, 0) if axis == "slab" else (i, bit)
        pairs += [(i * splits + j, other * splits + (j ^ across)) for j in range(splits)]
    theirs = lax.ppermute(gathered, ("slab", "split"), pairs)
    (merged,) = call(merge_kernel, (gathered, theirs, token), [rows_of(2 * gathered.shape[1])], us=0.1)
    return merged


def per_device(u, v, a, masks, proj_pos, proj_vel, proj_acc, pairs):
    pp, pv, pa = [jnp.transpose(p, (1, 0, 2)) for p in (proj_pos, proj_vel, proj_acc)]
    blocks = pp.shape[1]
    u, v, a, pp, pv, pa = [pltpu.with_memory_space_constraint(x, pltpu.HBM) for x in (u, v, a, pp, pv, pa)]
    u, half, pst, perm, *edges = call(
        begin_kernel,
        (u, v, a, pp, pv, pa),
        [PADDED, STATE, PST, jax.ShapeDtypeStruct((blocks, blocks), F32), XB, YE, YE],
        ins=[HBM] * 6,
        scratch=(
            pltpu.VMEM((3, *STATE.shape), F32),
            pltpu.VMEM((3, *pp.shape), F32),
            pltpu.SemaphoreType.DMA((3, CX // STEP)),
            pltpu.SemaphoreType.DMA((3,)),
        ),
    )
    words, rim = call(words_kernel, (masks,), [WORDS, RIM])
    for substep in range(SUB):
        last = substep == SUB - 1
        scale = 0.5 * DT if last else DT
        xb, ya_own, yb_own = edges
        xb = swap(xb, "slab", 1)
        surface, own_force, xa = call(
            functools.partial(contact_kernel, substep),
            (pairs, u, pst),
            [SURFACE, PAIR, XA],
            scalars=1,
            scratch=(PLACES,),
            us=1.5,
        )
        xa = swap(xa, "slab", 0)
        if last:
            (ours,) = call(pair_kernel, (xa, own_force), [PAIR], us=0.1)
            theirs = swap(ours, "split", 0)
            left, right, token = call(turn_kernel, (u,), [SIDE, SIDE, TOKEN])
            (gathered,) = call(state_kernel, (ours, theirs, pst, token), [rows_of(GROUP)], us=0.1)
            inner, token = call(
                functools.partial(late_inner_kernel, scale),
                (u, left, right, half, words, gathered),
                [HALVES, TOKEN],
                us=2.6,
            )
        else:
            inner, left, right, token = call(
                functools.partial(inner_kernel, scale), (u, half, words), [HALVES, SIDE, SIDE, TOKEN], us=3.6
            )
        after = gathered if last else token
        ya, yb = call(corner_kernel, (ya_own, yb_own, xa, xb, own_force, after), [YA, YA], us=0.1)
        ya, yb = swap(ya, "split", 0), swap(yb, "split", 1)
        if last:
            gathered = after = share_round(gathered, 0, token)
        edge, token = call(
            functools.partial(edge_kernel, scale),
            (xa, xb, u, left, right, half, words, after),
            [HALVES, TOKEN],
            scratch=[pltpu.VMEM(shape.shape, F32) for shape in (PADDED, SIDE, SIDE)],
            us=3.6,
        )
        if last:
            break
        u, half, pst, *edges = call(
            close_kernel,
            (u, inner, edge, surface, ya_own, yb_own, xa, ya, yb, rim, pst, own_force),
            [PADDED, STATE, PST, XB, YE, YE],
            scratch=(CROSSING,),
            us=1.3,
        )

    gathered = share_round(gathered, 1, token)
    final_u, final_v, token = call(
        last_kernel,
        (u, inner, edge, surface, ya_own, yb_own, ya, yb, rim, gathered),
        [STATE, STATE, TOKEN],
        scratch=(CROSSING,),
        us=1.4,
    )
    for number in range(2, len(ROUNDS[0])):
        gathered = share_round(gathered, number, token)
    final_pos, final_vel = call(final_kernel, (perm, gathered), [jax.ShapeDtypeStruct(pp.shape, F32)] * 2)
    return (
        final_u,
        final_v,
        jnp.transpose(final_pos, (1, 0, 2)),
        jnp.transpose(final_vel, (1, 0, 2)),
    )


def solution(mesh):
    cells = P(None, "slab", "split", None)
    return jax.shard_map(
        per_device,
        mesh=mesh,
        in_specs=(cells, cells, cells, cells, P(), P(), P(), P(None, None, ("slab", "split"))),
        out_specs=(cells, cells, P(), P()),
        check_vma=False,
    )
```

```python
import functools
import math

import jax
import jax.numpy as jnp
from jax import lax
from jax.experimental import pallas as pl
from jax.experimental.pallas import tpu as pltpu
from jax.sharding import PartitionSpec as P

SUB = 3
SL = 4
SLOTS = 16
CHUNK = 4
STEP = 2
GROUP = 4
ROUNDS = (
    (("slab", 8), ("slab", 4), ("split", 2), ("split", 4), ("slab", 2)),
    (("slab", 8), ("split", 2), ("slab", 4), ("slab", 2), ("split", 4)),
)

DT = 0.25
STIFF = 0.5
CONTACT = 0.05
WIDTH = 8.0
INV_MASS = 0.5

CX, CY, CZ = 8, 32, 256
LO = 8
F32 = jnp.float32


def bond_offsets():
    listed = []
    for sx in (-2, -1, 0, 1, 2):
        for sy in (-2, -1, 0, 1, 2):
            for sz in (-2, -1, 0, 1, 2):
                if 0 < sx * sx + sy * sy + sz * sz <= 4:
                    listed.append((sx, sy, sz))
    return listed


OFFSETS = bond_offsets()


def as_int32(bits):
    return bits - (1 << 32) if bits >= 1 << 31 else bits


def keep_bits(dim, allowed):
    return as_int32(sum(1 << n for n, e in enumerate(OFFSETS) if allowed(e[dim])))


def keep_word(index, last, dim):
    word = jnp.where(index == 0, keep_bits(dim, lambda e: e >= 0), -1)
    word = jnp.where(index == 1, keep_bits(dim, lambda e: e >= -1), word)
    word = jnp.where(index == last - 1, keep_bits(dim, lambda e: e <= 1), word)
    return jnp.where(index == last, keep_bits(dim, lambda e: e <= 0), word)


def position():
    return lax.axis_index("slab"), lax.axis_index("split")


def lane_sums(parts):
    whole = jnp.concatenate(parts, axis=0)
    high = whole.astype(jnp.bfloat16)
    low = (whole - high.astype(F32)).astype(jnp.bfloat16)
    ones = jnp.ones((256, 128), jnp.bfloat16)
    return jnp.dot(jnp.concatenate([high, low], axis=1), ones, preferred_element_type=F32)


def contact_kernel(substep, pairs, u_ref, pst, surface_out, force_out, xa, places):
    slab, split = position()
    corner = (slab * CX, split * CY)
    share = 0.5 * DT if substep == SUB - 1 else DT
    at_a = jnp.where(lax.rem(slab, 2) == 0, CX, 2)
    pos, ids = [pst[c] for c in range(3)], pst[6].astype(jnp.int32)
    surface_out[...] = jnp.zeros_like(surface_out)
    row = lax.broadcasted_iota(jnp.int32, (CY, 128), 0)
    lane = lax.broadcasted_iota(jnp.int32, (CY, 128), 1)
    place_y = (row + corner[1]).astype(F32)
    live = jnp.int32(0)
    for k in range(SLOTS):
        live += (pairs[substep, 1, k] >= 0).astype(jnp.int32)

    @pl.when(live > 0)
    def _():
        def place(x, carry):
            for c in range(3):
                top = u_ref[c, 1, x + 2, LO : LO + CY, :]
                for z in range(SL):
                    lattice = ((corner[0] + x).astype(F32), place_y, float(CZ - SL + z))[c]
                    at = 128 - SL + z
                    column = jnp.broadcast_to(top[:, at : at + 1], (CY, 128))
                    places[c, x, z * CY : (z + 1) * CY, :] = column + lattice
            return carry

        lax.fori_loop(0, CX, place, 0)

    def slot(k, totals):
        target = jnp.clip(pairs[substep, 0, k], 0, CX - 1)
        chosen = pairs[substep, 1, k]
        hit = ids == chosen
        stiff = jnp.where(chosen >= 0, CONTACT, 0.0)
        q = [jnp.sum(jnp.where(hit, pos[c], 0.0), axis=0, keepdims=True) for c in range(3)]
        r = [places[c, target] - q[c] for c in range(3)]
        squared = r[0] * r[0] + r[1] * r[1] + r[2] * r[2]
        weight = stiff * jnp.exp(squared * (-1.0 / WIDTH))
        pulled = [weight * r[c] for c in range(3)]
        sums = lane_sums(pulled)
        for c in range(3):
            surface = jnp.zeros((CY, 128), F32)
            for z in range(SL):
                at = c * SL * CY + z * CY
                surface = jnp.where(lane == 128 - SL + z, sums[at : at + CY], surface)
            surface_out[c, target] += share * surface
        return tuple(
            totals[c] - jnp.where(hit, jnp.sum(pulled[c], axis=0, keepdims=True), 0.0)
            for c in range(3)
        )

    def some(k, totals):
        for j in range(CHUNK):
            totals = slot(CHUNK * k + j, totals)
        return totals

    none = tuple(jnp.zeros((8, 128), F32) for _ in range(3))
    force = lax.fori_loop(0, (live + CHUNK - 1) // CHUNK, some, none)
    for c in range(3):
        force_out[c] = force[c]
        for h in range(2):
            lanes = slice(128 * h, 128 * h + 128)
            for layer in range(2):
                rows = slice((2 * c + layer) * CY, (2 * c + layer + 1) * CY)
                xa[rows, lanes] = u_ref[c, h, at_a + layer, LO : LO + CY, :]


    xa[6 * CY :, 0:128] = jnp.concatenate([force[0][0:GROUP], force[2][0:GROUP]], axis=0)
    xa[6 * CY :, 128:256] = force[1]


def chip_force(xa, c):
    at, lane = 6 * CY + GROUP * (c // 2), 128 * (c % 2)
    return jnp.concatenate(
        [xa[at : at + GROUP, lane : lane + 128], jnp.zeros((8 - GROUP, 128), F32)], axis=0
    )


def send_edges(u_ref, xb, ya, yb, even_x, even_y):
    at_b = jnp.where(even_x, 2, CX)
    xb[6 * CY :, :] = jnp.zeros((XB.shape[0] - 6 * CY, CZ), F32)
    for c in range(3):
        for h in range(2):
            lanes = slice(128 * h, 128 * h + 128)
            for layer in range(2):
                rows = slice((2 * c + layer) * CY, (2 * c + layer + 1) * CY)
                xb[rows, lanes] = u_ref[c, h, at_b + layer, LO : LO + CY, :]
    for want_even, low, high in ((True, yb, ya), (False, ya, yb)):

        @pl.when(even_y == want_even)
        def _(low=low, high=high):
            for c in range(3):
                for h in range(2):
                    lanes = slice(128 * h, 128 * h + 128)
                    for x in range(CX):
                        for r in range(2):
                            low[c, r, x : x + 1, lanes] = u_ref[c, h, x + 2, LO + r : LO + r + 1, :]
                            high[c, r, x : x + 1, lanes] = u_ref[
                                c, h, x + 2, LO + CY - 2 + r : LO + CY - 1 + r, :
                            ]


def begin_kernel(
    u, v, a, pp, pv, pa, u_out, half_out, pst, perm, xb, ya, yb, cells, blocks_in, sems, block_sems
):
    slab, split = position()
    splits = lax.axis_size("split")
    even_x, even_y = lax.rem(slab, 2) == 0, lax.rem(split, 2) == 0

    copies = []
    for x in range(0, CX, STEP):
        copies.append(
            [
                pltpu.make_async_copy(
                    source.at[:, x : x + STEP], cells.at[k, :, x : x + STEP], sems.at[k, x // STEP]
                )
                for k, source in enumerate((u, v, a))
            ]
        )
    block_copies = [
        pltpu.make_async_copy(source, blocks_in.at[k], block_sems.at[k])
        for k, source in enumerate((pp, pv, pa))
    ]
    for copy in block_copies:
        copy.start()
    for group in copies:
        for copy in group:
            copy.start()

    for copy in block_copies:
        copy.wait()
    pp, pv, pa = blocks_in.at[0], blocks_in.at[1], blocks_in.at[2]
    blocks = pp.shape[1]
    mean_x = jnp.sum(pp[0], axis=1, keepdims=True) * (1.0 / pp.shape[2])
    mean_y = jnp.sum(pp[1], axis=1, keepdims=True) * (1.0 / pp.shape[2])
    group_x = jnp.floor((mean_x + 0.5) * (1.0 / (2 * CX)))
    group_y = jnp.floor((mean_y + 0.5) * (1.0 / (2 * CY)))
    group = jnp.broadcast_to(group_x * (splits // 2) + group_y, (blocks, blocks))
    row = lax.broadcasted_iota(jnp.int32, (blocks, blocks), 0)
    lane = lax.broadcasted_iota(jnp.int32, (blocks, blocks), 1)
    earlier = jnp.where((group == group.T) & (lane < row), 1.0, 0.0)
    rank = jnp.sum(earlier, axis=1, keepdims=True).astype(jnp.int32)
    group = group.astype(jnp.int32)
    mine = (slab // 2) * (splits // 2) + split // 2
    other = group ^ mine
    slot = rank
    for order, ways in enumerate(zip(*ROUNDS)):
        even, odd = [bit // 2 * (splits // 2 if axis == "slab" else 1) for axis, bit in ways]
        slot = slot + jnp.where((other & jnp.where(even_x, even, odd)) != 0, GROUP << order, 0)
    perm[...] = jnp.where(slot == lane, 1.0, 0.0)

    pst[...] = jnp.zeros_like(pst)
    pst[6] = jnp.full((8, 128), -5.0, F32)
    for k in range(GROUP):
        chosen = slot == k
        pst[6, k : k + 1, :] = jnp.sum(jnp.where(chosen, row.astype(F32), 0.0), axis=0, keepdims=True)
        for c in range(3):
            pos, vel, acc = [
                jnp.sum(jnp.where(chosen, p[c], 0.0), axis=0, keepdims=True) for p in (pp, pv, pa)
            ]
            half = vel + 0.5 * DT * acc
            pst[3 + c, k : k + 1, :] = half
            pst[c, k : k + 1, :] = pos + DT * half

    for at, waits in zip(range(0, CX, STEP), copies):
        for copy in waits:
            copy.wait()
        for x in range(at, at + STEP):
            for c in range(3):
                half = cells[1, c, x] + 0.5 * DT * cells[2, c, x]
                half_out[c, x] = half
                moved = cells[0, c, x] + DT * half
                for h in range(2):
                    u_out[c, h, x + 2, LO : LO + CY, :] = moved[:, 128 * h : 128 * h + 128]
    send_edges(u_out, xb, ya, yb, even_x, even_y)


def words_kernel(masks, w_out, rim_out):
    slab, split = position()
    slabs, splits = lax.axis_size("slab"), lax.axis_size("split")

    for x in range(CX):
        kx = keep_word(slab * CX + x, slabs * CX - 1, 0)
        y = lax.broadcasted_iota(jnp.int32, (CY, CZ), 0)
        ky = keep_word(split * CY + y, splits * CY - 1, 1)
        kz = keep_word(lax.broadcasted_iota(jnp.int32, (CY, CZ), 1), CZ - 1, 2)
        word = masks[0, x] | (masks[1, x] << 8) | (masks[2, x] << 16) | (masks[3, x] << 24)
        word = word & ky & kz & kx
        w_out[x] = word & keep_word(y, CY - 1, 1)
        for r in range(4):
            y = r if r < 2 else CY - 4 + r
            rim_out[r, x : x + 1, :] = word[y : y + 1, :]


def corner_kernel(ya_own, yb_own, xa, xb, own_force, token, ya, yb):
    slab, split = position()
    even_x, even_y = lax.rem(slab, 2) == 0, lax.rem(split, 2) == 0
    for c in range(3):
        for r in range(2):
            ya[c, r, 0:CX, :] = ya_own[c, r]
            yb[c, r, 0:CX, :] = yb_own[c, r]
        force = own_force[c] + chip_force(xa, c)
        for h in range(2):
            ya[c, 0, CX + 2 : CX + 2 + GROUP, 128 * h : 128 * h + 128] = force[0:GROUP]
    for is_x in (True, False):
        for is_y in (True, False):

            @pl.when((even_x == is_x) & (even_y == is_y))
            def _(is_x=is_x, is_y=is_y):
                for c in range(3):
                    for message, high in ((ya, is_y), (yb, not is_y)):
                        for got, top in ((xa, is_x), (xb, not is_x)):
                            entry, layer = (CX + 1, 0) if top else (CX, 1)
                            for r in range(2):
                                at = (2 * c + layer) * CY + (CY - 2 if high else 0) + r
                                message[c, r, entry : entry + 1, :] = got[at : at + 1, :]


def rolled(u, c, x, at, by):
    lane = lax.broadcasted_iota(jnp.int32, (8, 128), 1)
    turned = [pltpu.roll(u[c, h, x, at, :], by % 128, 1) for h in range(2)]
    wraps = lane < by if by > 0 else lane >= 128 + by
    return [jnp.where(wraps, turned[1 - h], turned[h]) for h in range(2)]


def turn(u, left, right, x, y):
    at = slice(y, y + 8)
    for c in range(3):
        for side, by in ((left, -1), (right, 1)):
            for h, value in enumerate(rolled(u, c, x, at, by)):
                side[c, h, x - 1, at, :] = value


def forces(u, left, right, w, x, y, h):
    own = [u[c, h, x + 2, LO + y : LO + y + 8, :] for c in range(3)]
    less = {(c, e): own[c] - float(e) if e else own[c] for c in range(3) for e in (-2, -1, 0, 1, 2)}
    word = w[x, y : y + 8, 128 * h : 128 * h + 128]
    total = [None] * 3
    for squared_length in (1, 2, 3, 4):
        sums = [None] * 3
        for number, e in enumerate(OFFSETS):
            if sum(k * k for k in e) != squared_length:
                continue
            at = slice(LO + y + e[1], LO + y + e[1] + 8)
            if e[2] == 0:
                near = [u[c, h, x + 2 + e[0], at, :] for c in range(3)]
            elif abs(e[2]) == 2:
                near = [rolled(u, c, x + 2, at, -e[2])[h] for c in range(3)]
            else:
                source = left if e[2] > 0 else right
                near = [source[c, h, x + 1 + e[0], at, :] for c in range(3)]
            d = [near[c] - less[c, e[c]] for c in range(3)]
            q = jnp.maximum(d[0] * d[0] + d[1] * d[1] + d[2] * d[2], 1e-30)
            pull = q * lax.rsqrt(q) - math.sqrt(squared_length)
            pull = jnp.where((word & as_int32(1 << number)) != 0, pull, 0.0)
            for c in range(3):
                if e[c] > 0:
                    sums[c] = pull if sums[c] is None else sums[c] + pull
                elif e[c] < 0:
                    sums[c] = -pull if sums[c] is None else sums[c] - pull
        factor = STIFF / squared_length * (2.0 if squared_length == 4 else 1.0)
        for c in range(3):
            term = factor * sums[c]
            total[c] = term if total[c] is None else total[c] + term
    return total


def advance(scale, u, left, right, w, half, half_out, first, out_first, count):
    def layer(k, carry):
        x = first + k
        for y in range(0, CY, 8):
            for h in range(2):
                at, lanes = slice(y, y + 8), slice(128 * h, 128 * h + 128)
                total = forces(u, left, right, w, x, y, h)
                for c in range(3):
                    half_out[c, out_first + k, at, lanes] = half[c, x, at, lanes] + scale * total[c]
        return carry

    lax.fori_loop(0, count, layer, 0)


def turned_layers(u, left, right):
    def shifted(x, carry):
        for y in range(LO, LO + CY, 8):
            turn(u, left, right, x, y)
        return carry

    lax.fori_loop(2, CX + 2, shifted, 0)


def turn_kernel(u, left, right, token):
    turned_layers(u, left, right)
    token[...] = left[0, 0, 1, LO : LO + 8, :]


def late_inner_kernel(scale, u, left, right, half, w, after, half_out, token):
    advance(scale, u, left, right, w, half, half_out, 2, 0, CX - 4)
    token[...] = half_out[0, 0, 0:8, 0:128]


def inner_kernel(scale, u, half, w, half_out, left, right, token):
    turned_layers(u, left, right)
    advance(scale, u, left, right, w, half, half_out, 2, 0, CX - 4)
    token[...] = half_out[0, 0, 0:8, 0:128]


def edge_kernel(scale, xa, xb, u_own, left_own, right_own, half, w, after, half_out, token, u, left, right):
    slab, split = position()
    even_x = lax.rem(slab, 2) == 0
    to_a = jnp.where(even_x, CX + 2, 0)
    to_b = jnp.where(even_x, 0, CX + 2)
    rows = slice(LO, LO + CY)
    for c in range(3):
        for layer in range(2):
            part = slice((2 * c + layer) * CY, (2 * c + layer + 1) * CY)
            for h in range(2):
                lanes = slice(128 * h, 128 * h + 128)
                u[c, h, to_a + layer, rows, :] = xa[part, lanes]
                u[c, h, to_b + layer, rows, :] = xb[part, lanes]

    def own(x, carry):
        for c in range(3):
            for h in range(2):
                u[c, h, x + 2, rows, :] = u_own[c, h, x + 2, rows, :]
        return carry

    def sides(k, carry):
        x = jnp.where(k < 3, k, k + CX - 6)
        for c in range(3):
            for h in range(2):
                left[c, h, x + 1, rows, :] = left_own[c, h, x + 1, rows, :]
                right[c, h, x + 1, rows, :] = right_own[c, h, x + 1, rows, :]
        return carry

    lax.fori_loop(0, CX, own, 0)
    lax.fori_loop(0, 6, sides, 0)
    for x in (1, CX + 2):
        for y in range(LO, LO + CY, 8):
            turn(u, left, right, x, y)
    advance(scale, u, left, right, w, half, half_out, 0, 0, 2)
    advance(scale, u, left, right, w, half, half_out, CX - 2, 2, 2)
    token[...] = half_out[0, 0, 0:8, 0:128]


def rim_forces(own, halo, rim, side, even_y, crossing):
    sub = lax.broadcasted_iota(jnp.int32, (8, 128), 0)
    lane = lax.broadcasted_iota(jnp.int32, (8, 128), 1)
    sign = -1 if side == 0 else 1
    for h in range(2):
        lanes = slice(128 * h, 128 * h + 128)
        total = [[None] * 3, [None] * 3]
        variants = {}

        def near(c, r, ex, ez):
            key = (c, r, ex, ez)
            if key not in variants:
                if ez:
                    both = [near_at(c, r, ex, k) for k in range(2)]
                    turned = [pltpu.roll(value, -ez % 128, 1) for value in both]
                    wraps = lane < -ez if ez < 0 else lane >= 128 - ez
                    variants[key] = jnp.where(wraps, turned[1 - h], turned[h])
                else:
                    variants[key] = near_at(c, r, ex, h)
            return variants[key]

        def near_at(c, r, ex, k):
            here = halo(c, r, slice(0, 8), k)
            if ex == 0:
                return here
            ends = halo(c, r, slice(8, 16), k)
            if ex > 0:
                return jnp.where(sub == 7, ends[1:2], pltpu.roll(here, 7, 0))
            return jnp.where(sub == 0, ends[0:1], pltpu.roll(here, 1, 0))

        for number, e in enumerate(OFFSETS):
            if e[1] * sign <= 0:
                continue
            squared_length = sum(k * k for k in e)
            for r in range(2):
                if abs(e[1]) <= r:
                    continue
                beyond = abs(e[1]) - r - 1
                mine = 1 - r if side else r
                theirs = beyond if side else 1 - beyond
                d = [near(c, theirs, e[0], e[2]) - (own(c, mine, h) - float(e[c])) for c in range(3)]
                q = jnp.maximum(d[0] * d[0] + d[1] * d[1] + d[2] * d[2], 1e-30)
                pull = (q * lax.rsqrt(q) - math.sqrt(squared_length)) * (STIFF / squared_length)
                word = rim[2 * side + mine, :, lanes]
                pull = jnp.where((word & as_int32(1 << number)) != 0, pull, 0.0)
                for c in range(3):
                    if e[c]:
                        term = float(e[c]) * pull
                        total[mine][c] = term if total[mine][c] is None else total[mine][c] + term
        for mine in range(2):
            for c in range(3):
                value = total[mine][c]
                crossing[2 * side + mine, c, h] = jnp.zeros((8, 128), F32) if value is None else value


def close(scale, inner, edge, surface, ya_own, yb_own, ya, yb, rim, even_y, crossing, store):
    for side in range(2):
        first = even_y == (side == 1)

        def own(c, r, h):
            lanes = slice(128 * h, 128 * h + 128)
            return jnp.where(first, ya_own[c, r, :, lanes], yb_own[c, r, :, lanes])

        def halo(c, r, rows, h):
            lanes = slice(128 * h, 128 * h + 128)
            return jnp.where(first, ya[c, r, rows, lanes], yb[c, r, rows, lanes])

        rim_forces(own, halo, rim, side, even_y, crossing)
    sub = lax.broadcasted_iota(jnp.int32, (8, 128), 0)
    for x in range(CX):
        source, at = (inner, x - 2) if 2 <= x < CX - 2 else (edge, x if x < 2 else x - CX + 4)
        for c in range(3):
            for h in range(2):
                for y in range(0, CY, 8):
                    value = source[c, at, y : y + 8, 128 * h : 128 * h + 128]
                    if h == 1:
                        value = value + surface[c, x, y : y + 8, :]
                    for r in (0, 1) if y == 0 else (2, 3) if y == CY - 8 else ():
                        more = crossing[r, c, h, x : x + 1, :]
                        value = value + scale * jnp.where(sub == (r if r < 2 else r + 4), more, 0.0)
                    store(c, x, y, h, value)


def particle_force(xa, ya, own_force, c):
    theirs = jnp.concatenate([ya[c, 0, CX + 2 : CX + 2 + GROUP, 0:128], jnp.zeros((4, 128), F32)], axis=0)
    return own_force[c] + chip_force(xa, c) + theirs


def close_kernel(
    u, inner, edge, surface, ya_own, yb_own, xa, ya, yb, rim, pst, own_force,
    u_out, half_out, pst_out, xb_out, ya_out, yb_out, crossing,
):
    slab, split = position()
    even_x, even_y = lax.rem(slab, 2) == 0, lax.rem(split, 2) == 0

    def store(c, x, y, h, value):
        half_out[c, x, y : y + 8, 128 * h : 128 * h + 128] = value
        pad = slice(LO + y, LO + y + 8)
        u_out[c, h, x + 2, pad, :] = u[c, h, x + 2, pad, :] + DT * value

    close(DT, inner, edge, surface, ya_own, yb_own, ya, yb, rim, even_y, crossing, store)

    pst_out[6] = pst[6]
    for c in range(3):
        moved = pst[3 + c] + DT * INV_MASS * particle_force(xa, ya, own_force, c)
        pst_out[3 + c] = moved
        pst_out[c] = pst[c] + DT * moved
    send_edges(u_out, xb_out, ya_out, yb_out, even_x, even_y)


def pair_kernel(xa, own_force, out):
    for c in range(3):
        out[c] = own_force[c] + chip_force(xa, c)


def state_kernel(ours, theirs, pst, token, out):
    for c in range(3):
        out[c] = pst[c, 0:GROUP]
        acc = INV_MASS * (ours[c] + theirs[c])
        out[3 + c] = (pst[3 + c] + 0.5 * DT * acc)[0:GROUP]


def merge_kernel(*refs):
    *parts, token, out = refs
    count = parts[0].shape[1]
    for k, part in enumerate(parts):
        out[:, k * count : (k + 1) * count] = part[...]


def last_kernel(u, inner, edge, surface, ya_own, yb_own, ya, yb, rim, after, u_out, v_out, token, crossing):
    slab, split = position()

    def store(c, x, y, h, value):
        lanes = slice(128 * h, 128 * h + 128)
        v_out[c, x, y : y + 8, lanes] = value
        u_out[c, x, y : y + 8, lanes] = u[c, h, x + 2, LO + y : LO + y + 8, :]

    even_y = lax.rem(split, 2) == 0
    close(0.5 * DT, inner, edge, surface, ya_own, yb_own, ya, yb, rim, even_y, crossing, store)
    token[...] = crossing[0, 0, 0]


def final_kernel(perm, *refs):
    *parts, token, pos_out, vel_out = refs
    for c in range(3):
        for at, out in ((c, pos_out), (3 + c, vel_out)):
            out[c] = jnp.dot(
                perm[...],
                jnp.concatenate([part[at] for part in parts], axis=0),
                precision=lax.Precision.HIGHEST,
                preferred_element_type=F32,
            )


VMEM = pl.BlockSpec(memory_space=pltpu.VMEM)
SMEM = pl.BlockSpec(memory_space=pltpu.SMEM)
HBM = pl.BlockSpec(memory_space=pltpu.HBM)
STATE = jax.ShapeDtypeStruct((3, CX, CY, CZ), F32)
PADDED = jax.ShapeDtypeStruct((3, 2, CX + 4, CY + 16, 128), F32)
SIDE = jax.ShapeDtypeStruct((3, 2, CX + 2, CY + 16, 128), F32)
WORDS = jax.ShapeDtypeStruct((CX, CY, CZ), jnp.int32)
PST = jax.ShapeDtypeStruct((7, 8, 128), F32)
SURFACE = jax.ShapeDtypeStruct((3, CX, CY, 128), F32)
XA = jax.ShapeDtypeStruct((6 * CY + 8, CZ), F32)
XB = jax.ShapeDtypeStruct((6 * CY + 16, CZ), F32)
YE = jax.ShapeDtypeStruct((3, 2, CX, CZ), F32)
YA = jax.ShapeDtypeStruct((3, 2, 16, CZ), F32)
PAIR = jax.ShapeDtypeStruct((3, 8, 128), F32)
TOKEN = jax.ShapeDtypeStruct((8, 128), F32)
HALVES = jax.ShapeDtypeStruct((3, 4, CY, CZ), F32)
RIM = jax.ShapeDtypeStruct((4, CX, CZ), jnp.int32)
CROSSING = pltpu.VMEM((4, 3, 2, CX, 128), F32)
PLACES = pltpu.VMEM((3, CX, SL * CY, 128), F32)


def call(kernel, inputs, outputs, scalars=0, scratch=(), ins=None, limit=40, us=1.0):
    return pl.pallas_call(
        kernel,
        out_shape=outputs,
        in_specs=ins or [SMEM] * scalars + [VMEM] * (len(inputs) - scalars),
        out_specs=[VMEM] * len(outputs),
        scratch_shapes=list(scratch),
        compiler_params=pltpu.CompilerParams(vmem_limit_bytes=limit << 20),
        cost_estimate=pl.CostEstimate(flops=0, transcendentals=0, bytes_accessed=int(us * 3.0e6)),
    )(*inputs)


def swap(value, axis, offset):
    count = lax.axis_size(axis)
    pairs = []
    for i in range(offset, count, 2):
        pairs += [(i, (i + 1) % count), ((i + 1) % count, i)]
    return lax.ppermute(value, axis, pairs)


def rows_of(count):
    return jax.ShapeDtypeStruct((6, count, 128), F32)


def swapped(gathered, rounds):
    slabs, splits = lax.axis_size("slab"), lax.axis_size("split")
    pairs = []
    for i in range(slabs):
        for j in range(splits):
            place = {"slab": i, "split": j}
            for number in rounds:
                axis, bit = ROUNDS[i % 2][number]
                place[axis] ^= bit
            pairs.append((i * splits + j, place["slab"] * splits + place["split"]))
    return lax.ppermute(gathered, ("slab", "split"), pairs)


def shared(gathered, first, count):
    subsets = [[first + k for k in range(count) if number >> k & 1] for number in range(1, 1 << count)]
    return [gathered] + [swapped(gathered, rounds) for rounds in subsets]


def merge(parts, token):
    rows = sum(part.shape[1] for part in parts)
    (merged,) = call(merge_kernel, (*parts, token), [rows_of(rows)], us=0.1)
    return merged


def per_device(u, v, a, masks, proj_pos, proj_vel, proj_acc, pairs):
    pp, pv, pa = [jnp.transpose(p, (1, 0, 2)) for p in (proj_pos, proj_vel, proj_acc)]
    blocks = pp.shape[1]
    u, v, a, pp, pv, pa = [pltpu.with_memory_space_constraint(x, pltpu.HBM) for x in (u, v, a, pp, pv, pa)]
    u, half, pst, perm, *edges = call(
        begin_kernel,
        (u, v, a, pp, pv, pa),
        [PADDED, STATE, PST, jax.ShapeDtypeStruct((blocks, blocks), F32), XB, YE, YE],
        ins=[HBM] * 6,
        scratch=(
            pltpu.VMEM((3, *STATE.shape), F32),
            pltpu.VMEM((3, *pp.shape), F32),
            pltpu.SemaphoreType.DMA((3, CX // STEP)),
            pltpu.SemaphoreType.DMA((3,)),
        ),
    )
    words, rim = call(words_kernel, (masks,), [WORDS, RIM])
    for substep in range(SUB):
        last = substep == SUB - 1
        scale = 0.5 * DT if last else DT
        xb, ya_own, yb_own = edges
        xb = swap(xb, "slab", 1)
        surface, own_force, xa = call(
            functools.partial(contact_kernel, substep),
            (pairs, u, pst),
            [SURFACE, PAIR, XA],
            scalars=1,
            scratch=(PLACES,),
            us=1.5,
        )
        xa = swap(xa, "slab", 0)
        if last:
            (ours,) = call(pair_kernel, (xa, own_force), [PAIR], us=0.1)
            theirs = swap(ours, "split", 0)
            left, right, token = call(turn_kernel, (u,), [SIDE, SIDE, TOKEN])
            (gathered,) = call(state_kernel, (ours, theirs, pst, token), [rows_of(GROUP)], us=0.1)
            inner, token = call(
                functools.partial(late_inner_kernel, scale),
                (u, left, right, half, words, gathered),
                [HALVES, TOKEN],
                us=2.6,
            )
        else:
            inner, left, right, token = call(
                functools.partial(inner_kernel, scale), (u, half, words), [HALVES, SIDE, SIDE, TOKEN], us=3.6
            )
        after = gathered if last else token
        ya, yb = call(corner_kernel, (ya_own, yb_own, xa, xb, own_force, after), [YA, YA], us=0.1)
        ya, yb = swap(ya, "split", 0), swap(yb, "split", 1)
        if last:
            gathered = after = merge(shared(gathered, 0, 1), token)
        edge, token = call(
            functools.partial(edge_kernel, scale),
            (xa, xb, u, left, right, half, words, after),
            [HALVES, TOKEN],
            scratch=[pltpu.VMEM(shape.shape, F32) for shape in (PADDED, SIDE, SIDE)],
            us=3.6,
        )
        if last:
            break
        u, half, pst, *edges = call(
            close_kernel,
            (u, inner, edge, surface, ya_own, yb_own, xa, ya, yb, rim, pst, own_force),
            [PADDED, STATE, PST, XB, YE, YE],
            scratch=(CROSSING,),
            us=1.3,
        )

    gathered = merge(shared(gathered, 1, 2), token)
    final_u, final_v, token = call(
        last_kernel,
        (u, inner, edge, surface, ya_own, yb_own, ya, yb, rim, gathered),
        [STATE, STATE, TOKEN],
        scratch=(CROSSING,),
        us=1.4,
    )
    final_pos, final_vel = call(
        final_kernel,
        (perm, *shared(gathered, 3, 2), token),
        [jax.ShapeDtypeStruct(pp.shape, F32)] * 2,
    )
    return (
        final_u,
        final_v,
        jnp.transpose(final_pos, (1, 0, 2)),
        jnp.transpose(final_vel, (1, 0, 2)),
    )


def solution(mesh):
    cells = P(None, "slab", "split", None)
    return jax.shard_map(
        per_device,
        mesh=mesh,
        in_specs=(cells, cells, cells, cells, P(), P(), P(), P(None, None, ("slab", "split"))),
        out_specs=(cells, cells, P(), P()),
        check_vma=False,
    )
```

```python
import functools
import math

import jax
import jax.numpy as jnp
from jax import lax
from jax.experimental import pallas as pl
from jax.experimental.pallas import tpu as pltpu
from jax.sharding import PartitionSpec as P

SUB = 3
SL = 4
SLOTS = 16
CHUNK = 8
STEP = 2
GROUP = 4
ROUNDS = (
    (("slab", 8), ("slab", 4), ("split", 2), ("split", 4), ("slab", 2)),
    (("slab", 8), ("split", 2), ("slab", 4), ("slab", 2), ("split", 4)),
)

DT = 0.25
STIFF = 0.5
CONTACT = 0.05
WIDTH = 8.0
INV_MASS = 0.5

CX, CY, CZ = 8, 32, 256
LO = 8
F32 = jnp.float32


def bond_offsets():
    listed = []
    for sx in (-2, -1, 0, 1, 2):
        for sy in (-2, -1, 0, 1, 2):
            for sz in (-2, -1, 0, 1, 2):
                if 0 < sx * sx + sy * sy + sz * sz <= 4:
                    listed.append((sx, sy, sz))
    return listed


OFFSETS = bond_offsets()


def as_int32(bits):
    return bits - (1 << 32) if bits >= 1 << 31 else bits


def keep_bits(dim, allowed):
    return as_int32(sum(1 << n for n, e in enumerate(OFFSETS) if allowed(e[dim])))


def keep_word(index, last, dim):
    word = jnp.where(index == 0, keep_bits(dim, lambda e: e >= 0), -1)
    word = jnp.where(index == 1, keep_bits(dim, lambda e: e >= -1), word)
    word = jnp.where(index == last - 1, keep_bits(dim, lambda e: e <= 1), word)
    return jnp.where(index == last, keep_bits(dim, lambda e: e <= 0), word)


def position():
    return lax.axis_index("slab"), lax.axis_index("split")


def lane_sums(parts):
    whole = jnp.concatenate(parts, axis=0)
    high = whole.astype(jnp.bfloat16)
    low = (whole - high.astype(F32)).astype(jnp.bfloat16)
    ones = jnp.ones((256, 128), jnp.bfloat16)
    return jnp.dot(jnp.concatenate([high, low], axis=1), ones, preferred_element_type=F32)


def contact_kernel(substep, pairs, u_ref, pst, surface_out, force_out, xa, places):
    slab, split = position()
    corner = (slab * CX, split * CY)
    share = 0.5 * DT if substep == SUB - 1 else DT
    at_a = jnp.where(lax.rem(slab, 2) == 0, CX, 2)
    pos, ids = [pst[c] for c in range(3)], pst[6].astype(jnp.int32)
    surface_out[...] = jnp.zeros_like(surface_out)
    row = lax.broadcasted_iota(jnp.int32, (CY, 128), 0)
    lane = lax.broadcasted_iota(jnp.int32, (CY, 128), 1)
    place_y = (row + corner[1]).astype(F32)
    live = jnp.int32(0)
    for k in range(SLOTS):
        live += (pairs[substep, 1, k] >= 0).astype(jnp.int32)

    @pl.when(live > 0)
    def _():
        def place(x, carry):
            for c in range(3):
                top = u_ref[c, 1, x + 2, LO : LO + CY, :]
                for z in range(SL):
                    lattice = ((corner[0] + x).astype(F32), place_y, float(CZ - SL + z))[c]
                    at = 128 - SL + z
                    column = jnp.broadcast_to(top[:, at : at + 1], (CY, 128))
                    places[c, x, z * CY : (z + 1) * CY, :] = column + lattice
            return carry

        lax.fori_loop(0, CX, place, 0)

    def slot(k, totals):
        target = jnp.clip(pairs[substep, 0, k], 0, CX - 1)
        chosen = pairs[substep, 1, k]
        hit = ids == chosen
        stiff = jnp.where(chosen >= 0, CONTACT, 0.0)
        q = [jnp.sum(jnp.where(hit, pos[c], 0.0), axis=0, keepdims=True) for c in range(3)]
        r = [places[c, target] - q[c] for c in range(3)]
        squared = r[0] * r[0] + r[1] * r[1] + r[2] * r[2]
        weight = stiff * jnp.exp(squared * (-1.0 / WIDTH))
        pulled = [weight * r[c] for c in range(3)]
        sums = lane_sums(pulled)
        for c in range(3):
            surface = jnp.zeros((CY, 128), F32)
            for z in range(SL):
                at = c * SL * CY + z * CY
                surface = jnp.where(lane == 128 - SL + z, sums[at : at + CY], surface)
            surface_out[c, target] += share * surface
        return tuple(
            totals[c] - jnp.where(hit, jnp.sum(pulled[c], axis=0, keepdims=True), 0.0)
            for c in range(3)
        )

    def some(k, totals):
        for j in range(CHUNK):
            totals = slot(CHUNK * k + j, totals)
        return totals

    none = tuple(jnp.zeros((8, 128), F32) for _ in range(3))
    force = lax.fori_loop(0, (live + CHUNK - 1) // CHUNK, some, none)
    for c in range(3):
        force_out[c] = force[c]
        for h in range(2):
            lanes = slice(128 * h, 128 * h + 128)
            for layer in range(2):
                rows = slice((2 * c + layer) * CY, (2 * c + layer + 1) * CY)
                xa[rows, lanes] = u_ref[c, h, at_a + layer, LO : LO + CY, :]


    xa[6 * CY :, 0:128] = jnp.concatenate([force[0][0:GROUP], force[2][0:GROUP]], axis=0)
    xa[6 * CY :, 128:256] = force[1]


def chip_force(xa, c):
    at, lane = 6 * CY + GROUP * (c // 2), 128 * (c % 2)
    return jnp.concatenate(
        [xa[at : at + GROUP, lane : lane + 128], jnp.zeros((8 - GROUP, 128), F32)], axis=0
    )


def send_edges(u_ref, xb, ya, yb, even_x, even_y):
    at_b = jnp.where(even_x, 2, CX)
    xb[6 * CY :, :] = jnp.zeros((XB.shape[0] - 6 * CY, CZ), F32)
    for c in range(3):
        for h in range(2):
            lanes = slice(128 * h, 128 * h + 128)
            for layer in range(2):
                rows = slice((2 * c + layer) * CY, (2 * c + layer + 1) * CY)
                xb[rows, lanes] = u_ref[c, h, at_b + layer, LO : LO + CY, :]
    for want_even, low, high in ((True, yb, ya), (False, ya, yb)):

        @pl.when(even_y == want_even)
        def _(low=low, high=high):
            for c in range(3):
                for h in range(2):
                    lanes = slice(128 * h, 128 * h + 128)
                    for x in range(CX):
                        for r in range(2):
                            low[c, r, x : x + 1, lanes] = u_ref[c, h, x + 2, LO + r : LO + r + 1, :]
                            high[c, r, x : x + 1, lanes] = u_ref[
                                c, h, x + 2, LO + CY - 2 + r : LO + CY - 1 + r, :
                            ]


def begin_kernel(
    u, v, a, pp, pv, pa, u_out, half_out, pst, perm, xb, ya, yb, cells, blocks_in, sems, block_sems
):
    slab, split = position()
    splits = lax.axis_size("split")
    even_x, even_y = lax.rem(slab, 2) == 0, lax.rem(split, 2) == 0

    copies = []
    for x in range(0, CX, STEP):
        copies.append(
            [
                pltpu.make_async_copy(
                    source.at[:, x : x + STEP], cells.at[k, :, x : x + STEP], sems.at[k, x // STEP]
                )
                for k, source in enumerate((u, v, a))
            ]
        )
    block_copies = [
        pltpu.make_async_copy(source, blocks_in.at[k], block_sems.at[k])
        for k, source in enumerate((pp, pv, pa))
    ]
    for copy in block_copies:
        copy.start()
    for group in copies:
        for copy in group:
            copy.start()

    for copy in block_copies:
        copy.wait()
    pp, pv, pa = blocks_in.at[0], blocks_in.at[1], blocks_in.at[2]
    blocks = pp.shape[1]
    mean_x = jnp.sum(pp[0], axis=1, keepdims=True) * (1.0 / pp.shape[2])
    mean_y = jnp.sum(pp[1], axis=1, keepdims=True) * (1.0 / pp.shape[2])
    group_x = jnp.floor((mean_x + 0.5) * (1.0 / (2 * CX)))
    group_y = jnp.floor((mean_y + 0.5) * (1.0 / (2 * CY)))
    group = jnp.broadcast_to(group_x * (splits // 2) + group_y, (blocks, blocks))
    row = lax.broadcasted_iota(jnp.int32, (blocks, blocks), 0)
    lane = lax.broadcasted_iota(jnp.int32, (blocks, blocks), 1)
    earlier = jnp.where((group == group.T) & (lane < row), 1.0, 0.0)
    rank = jnp.sum(earlier, axis=1, keepdims=True).astype(jnp.int32)
    group = group.astype(jnp.int32)
    mine = (slab // 2) * (splits // 2) + split // 2
    other = group ^ mine
    slot = rank
    for order, ways in enumerate(zip(*ROUNDS)):
        even, odd = [bit // 2 * (splits // 2 if axis == "slab" else 1) for axis, bit in ways]
        slot = slot + jnp.where((other & jnp.where(even_x, even, odd)) != 0, GROUP << order, 0)
    perm[...] = jnp.where(slot == lane, 1.0, 0.0)

    pst[...] = jnp.zeros_like(pst)
    pst[6] = jnp.full((8, 128), -5.0, F32)
    for k in range(GROUP):
        chosen = slot == k
        pst[6, k : k + 1, :] = jnp.sum(jnp.where(chosen, row.astype(F32), 0.0), axis=0, keepdims=True)
        for c in range(3):
            pos, vel, acc = [
                jnp.sum(jnp.where(chosen, p[c], 0.0), axis=0, keepdims=True) for p in (pp, pv, pa)
            ]
            half = vel + 0.5 * DT * acc
            pst[3 + c, k : k + 1, :] = half
            pst[c, k : k + 1, :] = pos + DT * half

    for at, waits in zip(range(0, CX, STEP), copies):
        for copy in waits:
            copy.wait()
        for x in range(at, at + STEP):
            for c in range(3):
                half = cells[1, c, x] + 0.5 * DT * cells[2, c, x]
                half_out[c, x] = half
                moved = cells[0, c, x] + DT * half
                for h in range(2):
                    u_out[c, h, x + 2, LO : LO + CY, :] = moved[:, 128 * h : 128 * h + 128]
    send_edges(u_out, xb, ya, yb, even_x, even_y)


def words_kernel(masks, w_out, rim_out):
    slab, split = position()
    slabs, splits = lax.axis_size("slab"), lax.axis_size("split")

    for x in range(CX):
        kx = keep_word(slab * CX + x, slabs * CX - 1, 0)
        y = lax.broadcasted_iota(jnp.int32, (CY, CZ), 0)
        ky = keep_word(split * CY + y, splits * CY - 1, 1)
        kz = keep_word(lax.broadcasted_iota(jnp.int32, (CY, CZ), 1), CZ - 1, 2)
        word = masks[0, x] | (masks[1, x] << 8) | (masks[2, x] << 16) | (masks[3, x] << 24)
        word = word & ky & kz & kx
        w_out[x] = word & keep_word(y, CY - 1, 1)
        for r in range(4):
            y = r if r < 2 else CY - 4 + r
            rim_out[r, x : x + 1, :] = word[y : y + 1, :]


def corner_kernel(ya_own, yb_own, xa, xb, own_force, token, ya, yb):
    slab, split = position()
    even_x, even_y = lax.rem(slab, 2) == 0, lax.rem(split, 2) == 0
    for c in range(3):
        for r in range(2):
            ya[c, r, 0:CX, :] = ya_own[c, r]
            yb[c, r, 0:CX, :] = yb_own[c, r]
        force = own_force[c] + chip_force(xa, c)
        for h in range(2):
            ya[c, 0, CX + 2 : CX + 2 + GROUP, 128 * h : 128 * h + 128] = force[0:GROUP]
    for is_x in (True, False):
        for is_y in (True, False):

            @pl.when((even_x == is_x) & (even_y == is_y))
            def _(is_x=is_x, is_y=is_y):
                for c in range(3):
                    for message, high in ((ya, is_y), (yb, not is_y)):
                        for got, top in ((xa, is_x), (xb, not is_x)):
                            entry, layer = (CX + 1, 0) if top else (CX, 1)
                            for r in range(2):
                                at = (2 * c + layer) * CY + (CY - 2 if high else 0) + r
                                message[c, r, entry : entry + 1, :] = got[at : at + 1, :]


def rolled(u, c, x, at, by):
    lane = lax.broadcasted_iota(jnp.int32, (8, 128), 1)
    turned = [pltpu.roll(u[c, h, x, at, :], by % 128, 1) for h in range(2)]
    wraps = lane < by if by > 0 else lane >= 128 + by
    return [jnp.where(wraps, turned[1 - h], turned[h]) for h in range(2)]


def turn(u, left, right, x, y):
    at = slice(y, y + 8)
    for c in range(3):
        for side, by in ((left, -1), (right, 1)):
            for h, value in enumerate(rolled(u, c, x, at, by)):
                side[c, h, x - 1, at, :] = value


def forces(u, left, right, w, x, y, h):
    own = [u[c, h, x + 2, LO + y : LO + y + 8, :] for c in range(3)]
    less = {(c, e): own[c] - float(e) if e else own[c] for c in range(3) for e in (-2, -1, 0, 1, 2)}
    word = w[x, y : y + 8, 128 * h : 128 * h + 128]
    total = [None] * 3
    for squared_length in (1, 2, 3, 4):
        sums = [None] * 3
        for number, e in enumerate(OFFSETS):
            if sum(k * k for k in e) != squared_length:
                continue
            at = slice(LO + y + e[1], LO + y + e[1] + 8)
            if e[2] == 0:
                near = [u[c, h, x + 2 + e[0], at, :] for c in range(3)]
            elif abs(e[2]) == 2:
                near = [rolled(u, c, x + 2, at, -e[2])[h] for c in range(3)]
            else:
                source = left if e[2] > 0 else right
                near = [source[c, h, x + 1 + e[0], at, :] for c in range(3)]
            d = [near[c] - less[c, e[c]] for c in range(3)]
            q = jnp.maximum(d[0] * d[0] + d[1] * d[1] + d[2] * d[2], 1e-30)
            pull = q * lax.rsqrt(q) - math.sqrt(squared_length)
            pull = jnp.where((word & as_int32(1 << number)) != 0, pull, 0.0)
            for c in range(3):
                if e[c] > 0:
                    sums[c] = pull if sums[c] is None else sums[c] + pull
                elif e[c] < 0:
                    sums[c] = -pull if sums[c] is None else sums[c] - pull
        factor = STIFF / squared_length * (2.0 if squared_length == 4 else 1.0)
        for c in range(3):
            term = factor * sums[c]
            total[c] = term if total[c] is None else total[c] + term
    return total


def advance(scale, u, left, right, w, half, half_out, first, out_first, count):
    def layer(k, carry):
        x = first + k
        for y in range(0, CY, 8):
            for h in range(2):
                at, lanes = slice(y, y + 8), slice(128 * h, 128 * h + 128)
                total = forces(u, left, right, w, x, y, h)
                for c in range(3):
                    half_out[c, out_first + k, at, lanes] = half[c, x, at, lanes] + scale * total[c]
        return carry

    lax.fori_loop(0, count, layer, 0)


def turned_layers(u, left, right):
    def shifted(x, carry):
        for y in range(LO, LO + CY, 8):
            turn(u, left, right, x, y)
        return carry

    lax.fori_loop(2, CX + 2, shifted, 0)


def turn_kernel(u, left, right, token):
    turned_layers(u, left, right)
    token[...] = left[0, 0, 1, LO : LO + 8, :]


def late_inner_kernel(scale, u, left, right, half, w, after, half_out, token):
    advance(scale, u, left, right, w, half, half_out, 2, 0, CX - 4)
    token[...] = half_out[0, 0, 0:8, 0:128]


def inner_kernel(scale, u, half, w, half_out, left, right, token):
    turned_layers(u, left, right)
    advance(scale, u, left, right, w, half, half_out, 2, 0, CX - 4)
    token[...] = half_out[0, 0, 0:8, 0:128]


def edge_kernel(scale, xa, xb, u_own, left_own, right_own, half, w, after, half_out, token, u, left, right):
    slab, split = position()
    even_x = lax.rem(slab, 2) == 0
    to_a = jnp.where(even_x, CX + 2, 0)
    to_b = jnp.where(even_x, 0, CX + 2)
    rows = slice(LO, LO + CY)
    for c in range(3):
        for layer in range(2):
            part = slice((2 * c + layer) * CY, (2 * c + layer + 1) * CY)
            for h in range(2):
                lanes = slice(128 * h, 128 * h + 128)
                u[c, h, to_a + layer, rows, :] = xa[part, lanes]
                u[c, h, to_b + layer, rows, :] = xb[part, lanes]

    def own(x, carry):
        for c in range(3):
            for h in range(2):
                u[c, h, x + 2, rows, :] = u_own[c, h, x + 2, rows, :]
        return carry

    def sides(k, carry):
        x = jnp.where(k < 3, k, k + CX - 6)
        for c in range(3):
            for h in range(2):
                left[c, h, x + 1, rows, :] = left_own[c, h, x + 1, rows, :]
                right[c, h, x + 1, rows, :] = right_own[c, h, x + 1, rows, :]
        return carry

    lax.fori_loop(0, CX, own, 0)
    lax.fori_loop(0, 6, sides, 0)
    for x in (1, CX + 2):
        for y in range(LO, LO + CY, 8):
            turn(u, left, right, x, y)
    advance(scale, u, left, right, w, half, half_out, 0, 0, 2)
    advance(scale, u, left, right, w, half, half_out, CX - 2, 2, 2)
    token[...] = half_out[0, 0, 0:8, 0:128]


def rim_forces(own, halo, rim, side, even_y, crossing):
    sub = lax.broadcasted_iota(jnp.int32, (8, 128), 0)
    lane = lax.broadcasted_iota(jnp.int32, (8, 128), 1)
    sign = -1 if side == 0 else 1
    for h in range(2):
        lanes = slice(128 * h, 128 * h + 128)
        total = [[None] * 3, [None] * 3]
        variants = {}

        def near(c, r, ex, ez):
            key = (c, r, ex, ez)
            if key not in variants:
                if ez:
                    both = [near_at(c, r, ex, k) for k in range(2)]
                    turned = [pltpu.roll(value, -ez % 128, 1) for value in both]
                    wraps = lane < -ez if ez < 0 else lane >= 128 - ez
                    variants[key] = jnp.where(wraps, turned[1 - h], turned[h])
                else:
                    variants[key] = near_at(c, r, ex, h)
            return variants[key]

        def near_at(c, r, ex, k):
            here = halo(c, r, slice(0, 8), k)
            if ex == 0:
                return here
            ends = halo(c, r, slice(8, 16), k)
            if ex > 0:
                return jnp.where(sub == 7, ends[1:2], pltpu.roll(here, 7, 0))
            return jnp.where(sub == 0, ends[0:1], pltpu.roll(here, 1, 0))

        for number, e in enumerate(OFFSETS):
            if e[1] * sign <= 0:
                continue
            squared_length = sum(k * k for k in e)
            for r in range(2):
                if abs(e[1]) <= r:
                    continue
                beyond = abs(e[1]) - r - 1
                mine = 1 - r if side else r
                theirs = beyond if side else 1 - beyond
                d = [near(c, theirs, e[0], e[2]) - (own(c, mine, h) - float(e[c])) for c in range(3)]
                q = jnp.maximum(d[0] * d[0] + d[1] * d[1] + d[2] * d[2], 1e-30)
                pull = (q * lax.rsqrt(q) - math.sqrt(squared_length)) * (STIFF / squared_length)
                word = rim[2 * side + mine, :, lanes]
                pull = jnp.where((word & as_int32(1 << number)) != 0, pull, 0.0)
                for c in range(3):
                    if e[c]:
                        term = float(e[c]) * pull
                        total[mine][c] = term if total[mine][c] is None else total[mine][c] + term
        for mine in range(2):
            for c in range(3):
                value = total[mine][c]
                crossing[2 * side + mine, c, h] = jnp.zeros((8, 128), F32) if value is None else value


def close(scale, inner, edge, surface, ya_own, yb_own, ya, yb, rim, even_y, crossing, store):
    for side in range(2):
        first = even_y == (side == 1)

        def own(c, r, h):
            lanes = slice(128 * h, 128 * h + 128)
            return jnp.where(first, ya_own[c, r, :, lanes], yb_own[c, r, :, lanes])

        def halo(c, r, rows, h):
            lanes = slice(128 * h, 128 * h + 128)
            return jnp.where(first, ya[c, r, rows, lanes], yb[c, r, rows, lanes])

        rim_forces(own, halo, rim, side, even_y, crossing)
    sub = lax.broadcasted_iota(jnp.int32, (8, 128), 0)
    for x in range(CX):
        source, at = (inner, x - 2) if 2 <= x < CX - 2 else (edge, x if x < 2 else x - CX + 4)
        for c in range(3):
            for h in range(2):
                for y in range(0, CY, 8):
                    value = source[c, at, y : y + 8, 128 * h : 128 * h + 128]
                    if h == 1:
                        value = value + surface[c, x, y : y + 8, :]
                    for r in (0, 1) if y == 0 else (2, 3) if y == CY - 8 else ():
                        more = crossing[r, c, h, x : x + 1, :]
                        value = value + scale * jnp.where(sub == (r if r < 2 else r + 4), more, 0.0)
                    store(c, x, y, h, value)


def particle_force(xa, ya, own_force, c):
    theirs = jnp.concatenate([ya[c, 0, CX + 2 : CX + 2 + GROUP, 0:128], jnp.zeros((4, 128), F32)], axis=0)
    return own_force[c] + chip_force(xa, c) + theirs


def close_kernel(
    u, inner, edge, surface, ya_own, yb_own, xa, ya, yb, rim, pst, own_force,
    u_out, half_out, pst_out, xb_out, ya_out, yb_out, crossing,
):
    slab, split = position()
    even_x, even_y = lax.rem(slab, 2) == 0, lax.rem(split, 2) == 0

    def store(c, x, y, h, value):
        half_out[c, x, y : y + 8, 128 * h : 128 * h + 128] = value
        pad = slice(LO + y, LO + y + 8)
        u_out[c, h, x + 2, pad, :] = u[c, h, x + 2, pad, :] + DT * value

    close(DT, inner, edge, surface, ya_own, yb_own, ya, yb, rim, even_y, crossing, store)

    pst_out[6] = pst[6]
    for c in range(3):
        moved = pst[3 + c] + DT * INV_MASS * particle_force(xa, ya, own_force, c)
        pst_out[3 + c] = moved
        pst_out[c] = pst[c] + DT * moved
    send_edges(u_out, xb_out, ya_out, yb_out, even_x, even_y)


def pair_kernel(xa, own_force, out):
    for c in range(3):
        out[c] = own_force[c] + chip_force(xa, c)


def state_kernel(ours, theirs, pst, token, out):
    for c in range(3):
        out[c] = pst[c, 0:GROUP]
        acc = INV_MASS * (ours[c] + theirs[c])
        out[3 + c] = (pst[3 + c] + 0.5 * DT * acc)[0:GROUP]


def merge_kernel(*refs):
    *parts, token, out = refs
    count = parts[0].shape[1]
    for k, part in enumerate(parts):
        out[:, k * count : (k + 1) * count] = part[...]


def last_kernel(u, inner, edge, surface, ya_own, yb_own, ya, yb, rim, after, u_out, v_out, token, crossing):
    slab, split = position()

    def store(c, x, y, h, value):
        lanes = slice(128 * h, 128 * h + 128)
        v_out[c, x, y : y + 8, lanes] = value
        u_out[c, x, y : y + 8, lanes] = u[c, h, x + 2, LO + y : LO + y + 8, :]

    even_y = lax.rem(split, 2) == 0
    close(0.5 * DT, inner, edge, surface, ya_own, yb_own, ya, yb, rim, even_y, crossing, store)
    token[...] = crossing[0, 0, 0]


def final_kernel(perm, *refs):
    *parts, token, pos_out, vel_out = refs
    once = perm[...].astype(jnp.bfloat16)
    order = jnp.concatenate([once] * 3, axis=1)
    for c in range(3):
        for at, out in ((c, pos_out), (3 + c, vel_out)):
            left = jnp.concatenate([part[at] for part in parts], axis=0)
            pieces = []
            for _ in range(3):
                pieces.append(left.astype(jnp.bfloat16))
                left = left - pieces[-1].astype(F32)
            out[c] = jnp.dot(order, jnp.concatenate(pieces, axis=0), preferred_element_type=F32)


VMEM = pl.BlockSpec(memory_space=pltpu.VMEM)
SMEM = pl.BlockSpec(memory_space=pltpu.SMEM)
HBM = pl.BlockSpec(memory_space=pltpu.HBM)
STATE = jax.ShapeDtypeStruct((3, CX, CY, CZ), F32)
PADDED = jax.ShapeDtypeStruct((3, 2, CX + 4, CY + 16, 128), F32)
SIDE = jax.ShapeDtypeStruct((3, 2, CX + 2, CY + 16, 128), F32)
WORDS = jax.ShapeDtypeStruct((CX, CY, CZ), jnp.int32)
PST = jax.ShapeDtypeStruct((7, 8, 128), F32)
SURFACE = jax.ShapeDtypeStruct((3, CX, CY, 128), F32)
XA = jax.ShapeDtypeStruct((6 * CY + 8, CZ), F32)
XB = jax.ShapeDtypeStruct((6 * CY + 16, CZ), F32)
YE = jax.ShapeDtypeStruct((3, 2, CX, CZ), F32)
YA = jax.ShapeDtypeStruct((3, 2, 16, CZ), F32)
PAIR = jax.ShapeDtypeStruct((3, 8, 128), F32)
TOKEN = jax.ShapeDtypeStruct((8, 128), F32)
HALVES = jax.ShapeDtypeStruct((3, 4, CY, CZ), F32)
RIM = jax.ShapeDtypeStruct((4, CX, CZ), jnp.int32)
CROSSING = pltpu.VMEM((4, 3, 2, CX, 128), F32)
PLACES = pltpu.VMEM((3, CX, SL * CY, 128), F32)


def call(kernel, inputs, outputs, scalars=0, scratch=(), ins=None, limit=40, us=1.0):
    return pl.pallas_call(
        kernel,
        out_shape=outputs,
        in_specs=ins or [SMEM] * scalars + [VMEM] * (len(inputs) - scalars),
        out_specs=[VMEM] * len(outputs),
        scratch_shapes=list(scratch),
        compiler_params=pltpu.CompilerParams(vmem_limit_bytes=limit << 20),
        cost_estimate=pl.CostEstimate(flops=0, transcendentals=0, bytes_accessed=int(us * 3.0e6)),
    )(*inputs)


def swap(value, axis, offset):
    count = lax.axis_size(axis)
    pairs = []
    for i in range(offset, count, 2):
        pairs += [(i, (i + 1) % count), ((i + 1) % count, i)]
    return lax.ppermute(value, axis, pairs)


def rows_of(count):
    return jax.ShapeDtypeStruct((6, count, 128), F32)


def swapped(gathered, rounds):
    slabs, splits = lax.axis_size("slab"), lax.axis_size("split")
    pairs = []
    for i in range(slabs):
        for j in range(splits):
            place = {"slab": i, "split": j}
            for number in rounds:
                axis, bit = ROUNDS[i % 2][number]
                place[axis] ^= bit
            pairs.append((i * splits + j, place["slab"] * splits + place["split"]))
    return lax.ppermute(gathered, ("slab", "split"), pairs)


def shared(gathered, first, count):
    subsets = [[first + k for k in range(count) if number >> k & 1] for number in range(1, 1 << count)]
    return [gathered] + [swapped(gathered, rounds) for rounds in subsets]


def merge(parts, token):
    rows = sum(part.shape[1] for part in parts)
    (merged,) = call(merge_kernel, (*parts, token), [rows_of(rows)], us=0.1)
    return merged


def per_device(u, v, a, masks, proj_pos, proj_vel, proj_acc, pairs):
    pp, pv, pa = [jnp.transpose(p, (1, 0, 2)) for p in (proj_pos, proj_vel, proj_acc)]
    blocks = pp.shape[1]
    u, v, a, pp, pv, pa = [pltpu.with_memory_space_constraint(x, pltpu.HBM) for x in (u, v, a, pp, pv, pa)]
    u, half, pst, perm, *edges = call(
        begin_kernel,
        (u, v, a, pp, pv, pa),
        [PADDED, STATE, PST, jax.ShapeDtypeStruct((blocks, blocks), F32), XB, YE, YE],
        ins=[HBM] * 6,
        scratch=(
            pltpu.VMEM((3, *STATE.shape), F32),
            pltpu.VMEM((3, *pp.shape), F32),
            pltpu.SemaphoreType.DMA((3, CX // STEP)),
            pltpu.SemaphoreType.DMA((3,)),
        ),
    )
    words, rim = call(words_kernel, (masks,), [WORDS, RIM])
    for substep in range(SUB):
        last = substep == SUB - 1
        scale = 0.5 * DT if last else DT
        xb, ya_own, yb_own = edges
        xb = swap(xb, "slab", 1)
        surface, own_force, xa = call(
            functools.partial(contact_kernel, substep),
            (pairs, u, pst),
            [SURFACE, PAIR, XA],
            scalars=1,
            scratch=(PLACES,),
            us=1.5,
        )
        xa = swap(xa, "slab", 0)
        if last:
            (ours,) = call(pair_kernel, (xa, own_force), [PAIR], us=0.1)
            theirs = swap(ours, "split", 0)
            left, right, token = call(turn_kernel, (u,), [SIDE, SIDE, TOKEN])
            (gathered,) = call(state_kernel, (ours, theirs, pst, token), [rows_of(GROUP)], us=0.1)
            inner, token = call(
                functools.partial(late_inner_kernel, scale),
                (u, left, right, half, words, gathered),
                [HALVES, TOKEN],
                us=2.6,
            )
        else:
            inner, left, right, token = call(
                functools.partial(inner_kernel, scale), (u, half, words), [HALVES, SIDE, SIDE, TOKEN], us=3.6
            )
        after = gathered if last else token
        ya, yb = call(corner_kernel, (ya_own, yb_own, xa, xb, own_force, after), [YA, YA], us=0.1)
        ya, yb = swap(ya, "split", 0), swap(yb, "split", 1)
        if last:
            gathered = after = merge(shared(gathered, 0, 1), token)
        edge, token = call(
            functools.partial(edge_kernel, scale),
            (xa, xb, u, left, right, half, words, after),
            [HALVES, TOKEN],
            scratch=[pltpu.VMEM(shape.shape, F32) for shape in (PADDED, SIDE, SIDE)],
            us=3.6,
        )
        if last:
            break
        u, half, pst, *edges = call(
            close_kernel,
            (u, inner, edge, surface, ya_own, yb_own, xa, ya, yb, rim, pst, own_force),
            [PADDED, STATE, PST, XB, YE, YE],
            scratch=(CROSSING,),
            us=1.3,
        )

    gathered = merge(shared(gathered, 1, 2), token)
    final_u, final_v, token = call(
        last_kernel,
        (u, inner, edge, surface, ya_own, yb_own, ya, yb, rim, gathered),
        [STATE, STATE, TOKEN],
        scratch=(CROSSING,),
        us=1.4,
    )
    final_pos, final_vel = call(
        final_kernel,
        (perm, *shared(gathered, 3, 2), token),
        [jax.ShapeDtypeStruct(pp.shape, F32)] * 2,
    )
    return (
        final_u,
        final_v,
        jnp.transpose(final_pos, (1, 0, 2)),
        jnp.transpose(final_vel, (1, 0, 2)),
    )


def solution(mesh):
    cells = P(None, "slab", "split", None)
    return jax.shard_map(
        per_device,
        mesh=mesh,
        in_specs=(cells, cells, cells, cells, P(), P(), P(), P(None, None, ("slab", "split"))),
        out_specs=(cells, cells, P(), P()),
        check_vma=False,
    )
```
